32 devices in a mesh: wide: 8 (over z, x), narrow: 4 (over y, core).
Axes of the slice: x: 2, y: 2, z: 4, core: 2. Of those that a mesh axis runs over, the one named last changes fastest.
Arguments:
- tokens: bfloat16 [32, 512, 768], P(('wide', 'narrow')), may hold values from -6 to 6
- query_weight: bfloat16 [768, 768], P('wide'), may hold values from -0.0546875 to 0.0546875
- key_weight: bfloat16 [768, 768], P('wide'), may hold values from -0.21875 to 0.21875
- value_weight: bfloat16 [768, 768], P('wide'), may hold values from -0.21875 to 0.21875
- output_weight: bfloat16 [768, 768], P('wide'), may hold values from -1.25 to 1.25
- expand_weight: bfloat16 [768, 3072], P('wide'), may hold values from -0.21875 to 0.21875
- contract_weight: bfloat16 [3072, 768], P('wide'), may hold values from -0.109375 to 0.109375
- attention_gain: float32 [768], replicated, may hold values from 0.5 to 1.5
- feedforward_gain: float32 [768], replicated, may hold values from 0.5 to 1.5
- bias_table: float32 [32, 12], replicated, may hold values from -4 to 4
- query_length: int32 [32], P(('wide', 'narrow')), may hold values from 4 to 64, as said below
- passage_length: int32 [32], P(('wide', 'narrow')), may hold values from 252 to 508, as said below
- pair_order: int32 [32], replicated, may hold values from 0 to 31, as said below
- regrouped_grad: bfloat16 [32, 512, 768], P('narrow', 'wide'), may hold values from -6 to 6
Outputs:
- regrouped: bfloat16 [32, 512, 768], P('narrow', 'wide')
- tokens_grad: float32 [32, 512, 768], P(('wide', 'narrow'))
- query_weight_grad: float32 [768, 768], P('wide')
- key_weight_grad: float32 [768, 768], P('wide')
- value_weight_grad: float32 [768, 768], P('wide')
- output_weight_grad: float32 [768, 768], P('wide')
- expand_weight_grad: float32 [768, 3072], P('wide')
- contract_weight_grad: float32 [3072, 768], P('wide')
- attention_gain_grad: float32 [768], replicated
- feedforward_gain_grad: float32 [768], replicated
- bias_table_grad: float32 [32, 12], replicated
The draws below stay inside these ranges and needn't reach their ends.
Inputs may be any that keep to these rules, and one draw needn't show every extreme that they name: query_length + passage_length lies between half of 512 and 512; in every draw some pair has exactly 512 and some pair exactly half of 512. `passage_length`: see query_length. `pair_order`: a permutation of the 32 pairs; the pair at place k has an index r with (r) % 4 equal to k // 8.
All inputs are finite; a program needn't handle non-finite values.
Results may differ from the reference program's by a relative error of at most 0.015.
Values may be sent and summed in bfloat16 or wider, within the bound.
No kernel may reach another device: no remote copies, remote signals or barrier semaphores. Data moves between devices by JAX's collectives and lax.ppermute only.
A program may use at most 192 MiB of HBM per device.

```python
import math
import jax
import jax.numpy as jnp
import numpy as np
from jax import lax

D = 768
HEADS = 12
HEAD_DIM = 64
FF = 3072
BUCKETS = 32
MAX_DIST = 128
SEQ = 512
ROWS_DEV = 1
ROWS = 32
N_NARROW = 4


def pair_lengths(key):
    key_one, key_two, key_three, key_four, key_five = jax.random.split(key, 5)
    longest_query = min(64, SEQ // 4)
    shortness = jax.random.randint(key_one, (ROWS,), 0, longest_query - 3)
    shortness = jnp.minimum(shortness, jax.random.randint(key_two, (ROWS,), 0, longest_query - 3))
    shortness = jnp.minimum(shortness, jax.random.randint(key_three, (ROWS,), 0, longest_query - 3))
    query_part = 4 + shortness
    picked = jax.random.permutation(key_five, ROWS)
    query_part = query_part.at[picked[0]].set(4)
    query_part = query_part.at[picked[1]].set(4)
    query_part = query_part.at[picked[2]].set(longest_query)
    passage_part = jnp.minimum(SEQ - query_part, jax.random.randint(key_four, (ROWS,), SEQ // 2, SEQ + SEQ // 4))
    passage_part = passage_part.at[picked[0]].set(SEQ - query_part[picked[0]])
    passage_part = passage_part.at[picked[1]].set(SEQ // 2 - query_part[picked[1]])
    return (query_part.astype(jnp.int32), passage_part.astype(jnp.int32))


def draw_query_length(key, part):
    lengths = pair_lengths(key)
    return lengths[0]


def draw_passage_length(key, part):
    lengths = pair_lengths(key)
    return lengths[1]


def draw_pair_order(key, part):
    key = jax.random.fold_in(key, 7)
    block_rows = ROWS // N_NARROW
    groups = jax.random.randint(key, (N_NARROW, block_rows), 0, max(block_rows // 4, 2))
    within = jnp.argsort(groups, axis=1, stable=True).astype(jnp.int32)
    narrow_ids = jnp.arange(N_NARROW, dtype=jnp.int32)[:, None]
    global_rows = within // ROWS_DEV * (ROWS_DEV * N_NARROW) + narrow_ids * ROWS_DEV + within % ROWS_DEV
    return global_rows.reshape(ROWS).astype(jnp.int32)


def shard_levels(key, extent, cuts, low, high):
    factor_of = 1.0
    for axis_at, parts in cuts:
        draws = jax.random.uniform(jax.random.fold_in(jax.random.fold_in(key, 6), axis_at), (parts,), jnp.float32, low / len(cuts), high / len(cuts))
        factor_of = factor_of * jnp.repeat(jnp.exp(draws), extent[axis_at] // parts).reshape((-1,) + (1,) * (len(extent) - 1 - axis_at))
    return factor_of


def normal_values(stream_key, dims, width, limit, pieces=(), kind=jnp.bfloat16):
    array = width * jax.random.normal(stream_key, dims, jnp.float32)
    if pieces:
        array = array * shard_levels(stream_key, dims, pieces, -0.22, 0.18)
    return jnp.clip(array, -limit, limit).astype(kind)


def setup_inputs(seed: int = 0) -> dict:
    seeds = jax.random.split(jax.random.key(seed), 15)
    return {
        "tokens": normal_values(seeds[0], (ROWS, SEQ, D), 1.0, 6.0, ((0, 32),)),
        "query_weight": normal_values(seeds[1], (D, D), (D * HEAD_DIM // 4) ** -0.5, 0.0546875, ((0, 8),)),
        "key_weight": normal_values(seeds[2], (D, D), D ** -0.5, 0.21875, ((0, 8),)),
        "value_weight": normal_values(seeds[3], (D, D), D ** -0.5, 0.21875, ((0, 8),)),
        "output_weight": normal_values(seeds[4], (D, D), (D // 32) ** -0.5, 1.25, ((0, 8),)),
        "expand_weight": normal_values(seeds[5], (D, FF), D ** -0.5, 0.21875, ((0, 8),)),
        "contract_weight": normal_values(seeds[6], (FF, D), FF ** -0.5, 0.109375, ((0, 8),)),
        "attention_gain": jnp.clip(1.0 + 0.1 * jax.random.normal(seeds[7], (D,), jnp.float32), 0.5, 1.5),
        "feedforward_gain": jnp.clip(1.0 + 0.1 * jax.random.normal(seeds[8], (D,), jnp.float32), 0.5, 1.5),
        "bias_table": normal_values(seeds[9], (BUCKETS, HEADS), 1.0, 4.0, (), jnp.float32),
        "query_length": draw_query_length(jax.random.fold_in(seeds[14], 71), 0),
        "passage_length": draw_passage_length(jax.random.fold_in(seeds[14], 71), 0),
        "pair_order": draw_pair_order(jax.random.fold_in(seeds[14], 71), 0),
        "regrouped_grad": normal_values(seeds[13], (ROWS, SEQ, D), 1.0, 6.0, ((0, 4), (1, 8))),
    }


epsilon = 1e-06
negative = -1000000000.0

@jax.custom_vjp
def low(v):
    return lax.optimization_barrier(v.astype(jnp.bfloat16)).astype(jnp.float32)

@jax.custom_vjp
def low_back(v):
    return v

def low_keep(v):
    return (low(v), None)

def low_pass(kept, grad):
    return (grad,)

def back_keep(v):
    return (v, None)

def back_low(kept, grad):
    return (low(grad),)
low.defvjp(low_keep, low_pass)
low_back.defvjp(back_keep, back_low)

def bucket_index(offset_values, bucket_total, max_reach):
    exact_part = bucket_total // 4
    bounds_table = np.ceil(exact_part * (max_reach / exact_part) ** (np.arange(1, exact_part) / exact_part) - 1e-06).astype(np.int32)
    distance = jnp.abs(offset_values)
    passed = jnp.zeros_like(distance)
    for limit_value in bounds_table:
        passed = passed + (distance >= int(limit_value)).astype(jnp.int32)
    coarse = jnp.where(distance < exact_part, distance, exact_part + passed)
    return coarse + (offset_values > 0).astype(jnp.int32) * (bucket_total // 2)

def rms_norm(values, gain_values):
    return values * lax.rsqrt(lax.optimization_barrier(jnp.mean(values * values, axis=-1, keepdims=True)) + epsilon) * gain_values

def product(left, right):
    return jnp.einsum('bld,de->ble', left, right, precision=lax.Precision.HIGHEST)

def layer_rows(weight_list, block, pair_total):
    query_weight, key_weight, value_weight, output_weight, expand_weight, contract_weight, attention_gain, feedforward_gain, bias_table = weight_list
    row_count = block.shape[0]
    attention_input = low(rms_norm(block, attention_gain))
    queries = low_back(low(product(attention_input, query_weight))).reshape(row_count, SEQ, HEADS, HEAD_DIM)
    key_vectors = low_back(low(product(attention_input, key_weight))).reshape(row_count, SEQ, HEADS, HEAD_DIM)
    value_vectors = low_back(low(product(attention_input, value_weight))).reshape(row_count, SEQ, HEADS, HEAD_DIM)
    positions = jnp.arange(SEQ, dtype=jnp.int32)
    bucket_ids = bucket_index(positions[None, :] - positions[:, None], BUCKETS, MAX_DIST)
    bias_square = jnp.transpose(bias_table[bucket_ids], (2, 0, 1))
    key_fill = jnp.where(positions[None, :] < pair_total[:, None], jnp.float32(0.0), jnp.float32(negative))
    scores = jnp.einsum('bqhd,bkhd->bhqk', queries, key_vectors, precision=lax.Precision.HIGHEST)
    scores = low_back(scores + bias_square[None] + key_fill[:, None, None, :])
    probs_low = low(jax.nn.softmax(scores, axis=-1))
    mixed = jnp.einsum('bhqk,bkhd->bqhd', probs_low, value_vectors, precision=lax.Precision.HIGHEST)
    mixed = low_back(low(mixed.reshape(row_count, SEQ, D)))
    residual = block + low_back(product(mixed, output_weight))
    expand_input = low(rms_norm(residual, feedforward_gain))
    pre_activation = low_back(product(expand_input, expand_weight))
    hidden = low(jax.nn.gelu(pre_activation))
    return low(residual + low_back(product(hidden, contract_weight)))

def forward(floats, query_length, passage_length, pair_order):
    tokens = floats[0]
    weight_list = floats[1:]
    pair_total = query_length + passage_length
    per_block = math.gcd(ROWS, max(1, 4096 // SEQ))
    blocks = tokens.reshape(ROWS // per_block, per_block, SEQ, D)
    totals = pair_total.reshape(ROWS // per_block, per_block)
    checked_layer = jax.checkpoint(layer_rows)

    def block_step(block_items):
        return checked_layer(weight_list, block_items[0], block_items[1])
    outputs = lax.map(block_step, (blocks, totals))
    return outputs.reshape(ROWS, SEQ, D)[pair_order]

def reference(tokens, query_weight, key_weight, value_weight, output_weight, expand_weight, contract_weight, attention_gain, feedforward_gain, bias_table, query_length, passage_length, pair_order, regrouped_grad):
    floats = (tokens.astype(jnp.float32), query_weight.astype(jnp.float32), key_weight.astype(jnp.float32), value_weight.astype(jnp.float32), output_weight.astype(jnp.float32), expand_weight.astype(jnp.float32), contract_weight.astype(jnp.float32), attention_gain.astype(jnp.float32), feedforward_gain.astype(jnp.float32), bias_table.astype(jnp.float32))
    regrouped, pull_back = jax.vjp(lambda *inputs_list: forward(inputs_list, query_length, passage_length, pair_order), *floats)
    grads = pull_back(regrouped_grad.astype(jnp.float32))
    return (regrouped.astype(jnp.bfloat16), grads[0], grads[1], grads[2], grads[3], grads[4], grads[5], grads[6], grads[7], grads[8], grads[9])
```

```python
import functools

import jax
import jax.numpy as jnp
import numpy as np
from jax import lax
from jax.experimental import pallas as pl
from jax.experimental.pallas import tpu as pltpu
from jax.sharding import PartitionSpec as P

MAX_DIST = 128
epsilon = 1e-06
negative = -1000000000.0
F32 = jnp.float32
BF16 = jnp.bfloat16
MIB = 1024 * 1024


def bucket_index(offset_values, bucket_total, max_reach):
    exact_part = bucket_total // 4
    bounds_table = np.ceil(
        exact_part * (max_reach / exact_part) ** (np.arange(1, exact_part) / exact_part) - 1e-06
    ).astype(np.int32)
    distance = np.abs(offset_values)
    passed = np.zeros_like(distance)
    for limit_value in bounds_table:
        passed = passed + (distance >= int(limit_value)).astype(np.int32)
    coarse = np.where(distance < exact_part, distance, exact_part + passed)
    return coarse + (offset_values > 0).astype(np.int32) * (bucket_total // 2)


def one_hot_rows(offset_values, bucket_total):
    ids = bucket_index(np.asarray(offset_values, np.int32), bucket_total, MAX_DIST)
    return (ids[:, None] == np.arange(bucket_total)[None, :]).astype(np.float32)


def nn(left, right):
    return lax.dot_general(left, right, (((1,), (0,)), ((), ())), preferred_element_type=F32)


def nt(left, right):
    return lax.dot_general(left, right, (((1,), (1,)), ((), ())), preferred_element_type=F32)


def tn(left, right):
    return lax.dot_general(left, right, (((0,), (0,)), ((), ())), preferred_element_type=F32)


def norm_scale(values):
    return lax.rsqrt(jnp.mean(values * values, axis=-1, keepdims=True) + epsilon)


def norm_backward(values, gain, grad):
    scale = norm_scale(values)
    scaled = grad * gain
    dots = jnp.mean(scaled * values, axis=-1, keepdims=True)
    grad_values = scale * scaled - values * (scale * scale * scale * dots)
    grad_gain = jnp.sum(grad * (values * scale), axis=0, keepdims=True)
    return grad_values, grad_gain


def whole(shape):
    return pl.BlockSpec(shape, lambda *_: (0,) * len(shape))


def call(kernel, grid, in_specs, out_specs, out_shape, scratch=(), flops=0, vmem=56):
    return pl.pallas_call(
        kernel,
        grid=grid,
        in_specs=in_specs,
        out_specs=out_specs,
        out_shape=out_shape,
        scratch_shapes=list(scratch),
        compiler_params=pltpu.CompilerParams(vmem_limit_bytes=vmem * MIB),
        cost_estimate=pl.CostEstimate(flops=flops, bytes_accessed=8 * MIB, transcendentals=0),
    )


def shaped(shape, kind):
    return jax.ShapeDtypeStruct(shape, kind)


def project_kernel(tokens_ref, gain_ref, weight_ref, normed_ref, qkv_ref):
    @pl.when(pl.program_id(0) == 0)
    def _():
        values = tokens_ref[...].astype(F32)
        normed_ref[...] = (values * norm_scale(values) * gain_ref[...]).astype(BF16)

    qkv_ref[...] = nn(normed_ref[...], weight_ref[...]).astype(BF16)


def project(tokens, gain, weight):
    length, width = tokens.shape
    total = weight.shape[1]
    block = width
    return call(
        project_kernel,
        (total // block,),
        [whole((length, width)), whole((1, width)), pl.BlockSpec((width, block), lambda j: (0, j))],
        [whole((length, width)), pl.BlockSpec((length, block), lambda j: (0, j))],
        [shaped((length, width), BF16), shaped((length, total), BF16)],
        flops=2 * length * width * total,
    )(tokens, gain, weight)


QB = 256
KB = 128


def head_lanes(shape, which, size):
    lanes = lax.broadcasted_iota(jnp.int32, shape, 1)
    return (lanes < size) == (which == 0)


def attend_kernel(q_ref, k_ref, v_ref, line_ref, fill_ref, mixed_ref, probs_ref):
    length, pair = q_ref.shape
    size = pair // 2
    queries = q_ref[...]
    keys = k_ref[...]
    values_t = v_ref[...].T
    fill = fill_ref[...]
    heads = []
    for a in range(2):
        own = jnp.where(head_lanes(queries.shape, a, size), queries, jnp.zeros_like(queries))
        line = jnp.broadcast_to(line_ref[0, a : a + 1, :], (KB, 2 * length))
        band = pltpu.roll(line, 0, 1, stride=1, stride_axis=0)
        parts = []
        for qb in range(0, length, QB):
            raw = nt(keys, own[qb : qb + QB])
            rows = []
            for kb in range(0, length, KB):
                start = length - KB - kb + qb
                rows.append(
                    raw[kb : kb + KB] + (band[:, start : start + QB] + fill[kb : kb + KB])
                )
            scores = jnp.concatenate(rows, axis=0)
            peak = jnp.max(scores, axis=0, keepdims=True)
            weights = jnp.exp(scores - peak)
            total = jnp.sum(weights, axis=0, keepdims=True)
            probs = (weights * (1.0 / total)).astype(BF16)
            probs_ref[a, :, qb : qb + QB] = probs
            parts.append(nn(values_t[a * size : (a + 1) * size], probs))
        heads.append(jnp.concatenate(parts, axis=1))
    mixed_ref[...] = jnp.concatenate(heads, axis=0).T.astype(BF16)


def attend(qkv, lines, fill, head_count):
    length = qkv.shape[0]
    width = qkv.shape[1] // 3
    pairs = head_count // 2
    size = width // pairs

    def column(base):
        return pl.BlockSpec((length, size), lambda p: (0, base + p))

    return call(
        attend_kernel,
        (pairs,),
        [
            column(0),
            column(pairs),
            column(2 * pairs),
            pl.BlockSpec((1, 2, 2 * length), lambda p: (p, 0, 0)),
            whole((length, 1)),
        ],
        [column(0), pl.BlockSpec((2, length, length), lambda p: (p, 0, 0))],
        [shaped((length, width), BF16), shaped((head_count, length, length), BF16)],
        flops=8 * head_count * length * length * size,
    )(qkv, qkv, qkv, lines, fill)


def attend_back_kernel(
    q_ref, k_ref, v_ref, grad_ref, probs_ref, dq_ref, dk_ref, dv_ref, line_ref
):
    length, pair = q_ref.shape
    size = pair // 2
    queries = q_ref[...]
    keys_t = k_ref[...].T
    values = v_ref[...]
    grads = grad_ref[...]
    blocks = length // KB
    dq_heads, dk_heads, dv_heads = [], [], []
    for a in range(2):
        own = jnp.where(head_lanes(grads.shape, a, size), grads, jnp.zeros_like(grads))
        dq_parts = []
        dk = dv = None
        near = {}
        for qb in range(0, length, QB):
            probs = probs_ref[a, :, qb : qb + QB]
            probs_wide = probs.astype(F32)
            pulled = nt(values, own[qb : qb + QB])
            dots = jnp.sum(probs_wide * pulled, axis=0, keepdims=True)
            grad_scores = (probs_wide * (pulled - dots)).astype(BF16)
            dq_parts.append(nn(keys_t[a * size : (a + 1) * size], grad_scores))
            dk_part = nn(grad_scores, queries[qb : qb + QB])
            dv_part = nn(probs, grads[qb : qb + QB])
            dk = dk_part if dk is None else dk + dk_part
            dv = dv_part if dv is None else dv + dv_part
            wide = grad_scores.astype(F32)
            for i in range(blocks):
                for j in range(QB // KB):
                    gap = i - (qb // KB + j)
                    gap = max(-2, min(2, gap))
                    piece = wide[i * KB : (i + 1) * KB, j * KB : (j + 1) * KB]
                    near[gap] = piece if gap not in near else near[gap] + piece
        dq_heads.append(jnp.concatenate(dq_parts, axis=1))
        dk_heads.append(dk)
        dv_heads.append(dv)
        fold = jnp.concatenate([near[1], near[0], near[-1], jnp.zeros_like(near[0])], axis=1)
        rows = KB
        while rows > 8:
            rows //= 2
            fold = fold[:rows] + pltpu.roll(fold[rows : 2 * rows], 4 * KB - rows, 1)
        line_ref[0, a, :, 0 : 4 * KB] = fold
        far = jnp.concatenate([near[2], near[-2]], axis=1)
        line_ref[0, a, :, 4 * KB : 6 * KB] = jnp.sum(far.reshape(KB // 8, 8, 2 * KB), axis=0)
    first = head_lanes(queries.shape, 0, size)
    dq_ref[...] = jnp.concatenate(dq_heads, axis=0).T.astype(BF16)
    dk_ref[...] = jnp.where(first, dk_heads[0], dk_heads[1]).astype(BF16)
    dv_ref[...] = jnp.where(first, dv_heads[0], dv_heads[1]).astype(BF16)


def attend_back(qkv, grad_mixed, probs):
    head_count, length, _ = probs.shape
    width = grad_mixed.shape[1]
    pairs = head_count // 2
    size = width // pairs

    def column(base):
        return pl.BlockSpec((length, size), lambda p: (0, base + p))

    grad_shape = shaped((length, width), BF16)
    return call(
        attend_back_kernel,
        (pairs,),
        [
            column(0),
            column(pairs),
            column(2 * pairs),
            column(0),
            pl.BlockSpec((2, length, length), lambda p: (p, 0, 0)),
        ],
        [
            column(0),
            column(0),
            column(0),
            pl.BlockSpec((1, 2, 8, 6 * KB), lambda p: (p, 0, 0, 0)),
        ],
        [grad_shape, grad_shape, grad_shape, shaped((pairs, 2, 8, 6 * KB), F32)],
        flops=12 * head_count * length * length * size,
    )(qkv, qkv, qkv, grad_mixed, probs)


def line_one_hot(bucket_total):
    column = np.arange(4 * KB)
    rows = []
    for s in range(8):
        place = (column - s) % (4 * KB)
        offset = np.where(place <= 3 * KB, KB - place, 5 * KB - place)
        rows.append(np.concatenate([offset, np.full(KB, 3 * KB), np.full(KB, -3 * KB)]))
    return one_hot_rows(np.concatenate(rows), bucket_total)


def residual_kernel(tokens_ref, mixed_ref, weight_ref, gain_ref, residual_ref, normed_ref):
    residual = tokens_ref[...].astype(F32) + nn(mixed_ref[...], weight_ref[...])
    residual_ref[...] = residual
    normed_ref[...] = (residual * norm_scale(residual) * gain_ref[...]).astype(BF16)


def residual_step(tokens, mixed, weight, gain):
    length, width = tokens.shape
    return call(
        residual_kernel,
        (1,),
        [
            whole((length, width)),
            whole((length, width)),
            whole((width, width)),
            whole((1, width)),
        ],
        [whole((length, width)), whole((length, width))],
        [shaped((length, width), F32), shaped((length, width), BF16)],
        flops=2 * length * width * width,
    )(tokens, mixed, weight, gain)


def feed_kernel(
    normed_ref,
    grad_ref,
    residual_ref,
    gain_ref,
    expand_ref,
    contract_ref,
    out_ref,
    grad_residual_ref,
    grad_low_ref,
    gain_grad_ref,
    expand_grad_ref,
    contract_grad_ref,
    total_ref,
    pulled_ref,
    turned_ref,
):
    step = pl.program_id(0)

    @pl.when(step == 0)
    def _():
        total_ref[...] = residual_ref[...]
        pulled_ref[...] = jnp.zeros_like(pulled_ref)
        turned_ref[...] = normed_ref[...].T

    expand = expand_ref[...]
    contract = contract_ref[...]
    grad_block = grad_ref[...]
    pre = nn(normed_ref[...], expand)
    grad_hidden = nt(grad_block, contract)
    scale = np.float32(np.sqrt(2.0 / np.pi))
    square = pre * pre
    bent = jnp.tanh(pre * (scale + (scale * np.float32(0.044715)) * square))
    half = 0.5 + 0.5 * bent
    hidden = (pre * half).astype(BF16)
    slope = half + (0.5 * pre) * (1.0 - bent * bent) * (
        scale + (scale * np.float32(3 * 0.044715)) * square
    )
    grad_pre = (grad_hidden * slope).astype(BF16)
    total_ref[...] += nn(hidden, contract)
    pulled_ref[...] += nt(grad_pre, expand)
    contract_grad_ref[...] = tn(hidden, grad_block).astype(BF16)
    expand_grad_ref[...] = nn(turned_ref[...], grad_pre).astype(BF16)

    @pl.when(step == pl.num_programs(0) - 1)
    def _():
        out_ref[...] = total_ref[...].astype(BF16)
        grad_values, grad_gain = norm_backward(residual_ref[...], gain_ref[...], pulled_ref[...])
        grad_residual = grad_block.astype(F32) + grad_values
        grad_residual_ref[...] = grad_residual
        grad_low_ref[...] = grad_residual.astype(BF16)
        gain_grad_ref[...] = grad_gain


def feed(normed, grad_block, residual, gain, expand, contract):
    length, width = normed.shape
    hidden = expand.shape[1]
    block = 512
    full = whole((length, width))
    columns = pl.BlockSpec((width, block), lambda j: (0, j))
    rows = pl.BlockSpec((block, width), lambda j: (j, 0))
    return call(
        feed_kernel,
        (hidden // block,),
        [full, full, full, whole((1, width)), columns, rows],
        [full, full, full, whole((1, width)), columns, rows],
        [
            shaped((length, width), BF16),
            shaped((length, width), F32),
            shaped((length, width), BF16),
            shaped((1, width), F32),
            shaped((width, hidden), BF16),
            shaped((hidden, width), BF16),
        ],
        scratch=[
            pltpu.VMEM((length, width), F32),
            pltpu.VMEM((length, width), F32),
            pltpu.VMEM((width, length), BF16),
        ],
        flops=12 * length * width * hidden,
    )(normed, grad_block, residual, gain, expand, contract)


def output_back_kernel(mixed_ref, grad_ref, weight_ref, weight_grad_ref, grad_mixed_ref):
    grad = grad_ref[...]
    grad_mixed_ref[...] = nt(grad, weight_ref[...]).astype(BF16)
    weight_grad_ref[...] = tn(mixed_ref[...], grad).astype(BF16)


def output_back(mixed, grad, weight):
    length, width = mixed.shape
    full = whole((length, width))
    square = whole((width, width))
    return call(
        output_back_kernel,
        (1,),
        [full, full, square],
        [square, full],
        [shaped((width, width), BF16), shaped((length, width), BF16)],
        flops=4 * length * width * width,
    )(mixed, grad, weight)


def project_grad_kernel(normed_ref, dq_ref, dk_ref, dv_ref, out_ref):
    turned = normed_ref[...].T
    width = dq_ref.shape[1]
    for i, ref in enumerate((dq_ref, dk_ref, dv_ref)):
        out_ref[:, i * width : (i + 1) * width] = nn(turned, ref[...]).astype(BF16)


def project_grad(normed, dq, dk, dv):
    length, width = normed.shape
    full = whole((length, width))
    return call(
        project_grad_kernel,
        (1,),
        [full] * 4,
        whole((width, 3 * width)),
        shaped((width, 3 * width), BF16),
        flops=6 * length * width * width,
    )(normed, dq, dk, dv)


def tokens_back_kernel(
    dq_ref, dk_ref, dv_ref, weight_ref, tokens_ref, gain_ref, residual_ref, out_ref, gain_grad_ref
):
    width = dq_ref.shape[1]
    pulled = nt(dq_ref[...], weight_ref[:, 0:width])
    pulled += nt(dk_ref[...], weight_ref[:, width : 2 * width])
    pulled += nt(dv_ref[...], weight_ref[:, 2 * width : 3 * width])
    grad_values, grad_gain = norm_backward(tokens_ref[...].astype(F32), gain_ref[...], pulled)
    out_ref[...] = residual_ref[...] + grad_values
    gain_grad_ref[...] = grad_gain


def tokens_back(dq, dk, dv, weight, tokens, gain, grad_residual):
    length, width = tokens.shape
    full = whole((length, width))
    return call(
        tokens_back_kernel,
        (1,),
        [full, full, full, whole((width, 3 * width)), full, whole((1, width)), full],
        [full, whole((1, width))],
        [shaped((length, width), F32), shaped((1, width), F32)],
        flops=6 * length * width * width,
    )(dq, dk, dv, weight, tokens, gain, grad_residual)


def on_device(
    tokens,
    query_weight,
    key_weight,
    value_weight,
    output_weight,
    expand_weight,
    contract_weight,
    attention_gain,
    feedforward_gain,
    bias_table,
    query_length,
    passage_length,
    pair_order,
    regrouped_grad,
):
    row_count, length, width = tokens.shape
    bucket_count, head_count = bias_table.shape
    narrow_index = lax.axis_index("narrow")
    narrow_count = lax.axis_size("narrow")

    def gathered(weight):
        return lax.all_gather(weight, "wide", axis=0, tiled=True)

    full_qkv = gathered(jnp.concatenate([query_weight, key_weight, value_weight], axis=1))
    full_output = gathered(output_weight)
    full_expand = gathered(expand_weight)
    full_contract = gathered(contract_weight)

    group_rows = regrouped_grad.shape[0]
    chosen = lax.dynamic_slice_in_dim(pair_order, narrow_index * group_rows, group_rows)
    local_rows = chosen // (row_count * narrow_count) * row_count + chosen % row_count
    arranged = jnp.zeros_like(regrouped_grad).at[local_rows].set(regrouped_grad)
    grad_block = lax.all_to_all(arranged, "wide", split_axis=0, concat_axis=1, tiled=True).reshape(
        length, width
    )

    place = np.arange(2 * length)
    offsets = np.where(place <= 2 * length - KB, length - KB - place, 3 * length - KB - place)
    band_hot = jnp.asarray(one_hot_rows(np.clip(offsets, 1 - length, length - 1), bucket_count))
    lines = jnp.dot(bias_table.T, band_hot.T, precision=lax.Precision.HIGHEST)
    lines = lines.reshape(head_count // 2, 2, 2 * length)
    positions = jnp.arange(length, dtype=jnp.int32)
    fill = jnp.where(positions < query_length[0] + passage_length[0], 0.0, negative)
    fill = fill.astype(F32)[:, None]

    inputs = tokens.reshape(length, width)
    gain_one = attention_gain[None]
    gain_two = feedforward_gain[None]
    attention_input, qkv = project(inputs, gain_one, full_qkv)
    mixed, probs = attend(qkv, lines, fill, head_count)
    residual, expand_input = residual_step(inputs, mixed, full_output, gain_two)
    block_output, grad_residual, grad_low, gain_two_grad, expand_grad, contract_grad = feed(
        expand_input, grad_block, residual, gain_two, full_expand, full_contract
    )
    received = lax.all_to_all(
        block_output.reshape(row_count, length, width),
        "wide",
        split_axis=1,
        concat_axis=0,
        tiled=True,
    )
    regrouped = jnp.take(received, local_rows, axis=0)
    output_grad, grad_mixed = output_back(mixed, grad_low, full_output)
    dq, dk, dv, line_grads = attend_back(qkv, grad_mixed, probs)
    qkv_grad = project_grad(attention_input, dq, dk, dv)
    tokens_grad, gain_one_grad = tokens_back(
        dq, dk, dv, full_qkv, inputs, gain_one, grad_residual
    )
    table_grad = jnp.dot(
        jnp.asarray(line_one_hot(bucket_count).T),
        line_grads.reshape(head_count, -1).T,
        precision=lax.Precision.HIGHEST,
    )

    def summed(grad):
        part = lax.psum_scatter(grad, "wide", scatter_dimension=0, tiled=True)
        return lax.psum(part, "narrow").astype(F32)

    final_qkv = summed(qkv_grad)
    final_output = summed(output_grad)
    final_expand = summed(expand_grad)
    final_contract = summed(contract_grad)
    final_attention_gain, final_feedforward_gain, final_table = lax.psum(
        (gain_one_grad[0], gain_two_grad[0], table_grad), ("wide", "narrow")
    )
    return (
        regrouped,
        tokens_grad.reshape(row_count, length, width),
        final_qkv[:, :width],
        final_qkv[:, width : 2 * width],
        final_qkv[:, 2 * width :],
        final_output,
        final_expand,
        final_contract,
        final_attention_gain,
        final_feedforward_gain,
        final_table,
    )


def solution(mesh):
    in_specs = (
        P(("wide", "narrow"), None, None),
        P("wide", None),
        P("wide", None),
        P("wide", None),
        P("wide", None),
        P("wide", None),
        P("wide", None),
        P(),
        P(),
        P(),
        P(("wide", "narrow")),
        P(("wide", "narrow")),
        P(),
        P("narrow", "wide", None),
    )
    out_specs = (
        P("narrow", "wide", None),
        P(("wide", "narrow"), None, None),
        P("wide", None),
        P("wide", None),
        P("wide", None),
        P("wide", None),
        P("wide", None),
        P("wide", None),
        P(),
        P(),
        P(),
    )
    return jax.shard_map(
        on_device, mesh=mesh, in_specs=in_specs, out_specs=out_specs, check_vma=False
    )
```

```python
import functools

import jax
import jax.numpy as jnp
import numpy as np
from jax import lax
from jax.experimental import pallas as pl
from jax.experimental.pallas import tpu as pltpu
from jax.sharding import PartitionSpec as P

MAX_DIST = 128
epsilon = 1e-06
negative = -1000000000.0
F32 = jnp.float32
BF16 = jnp.bfloat16
MIB = 1024 * 1024


def bucket_index(offset_values, bucket_total, max_reach):
    exact_part = bucket_total // 4
    bounds_table = np.ceil(
        exact_part * (max_reach / exact_part) ** (np.arange(1, exact_part) / exact_part) - 1e-06
    ).astype(np.int32)
    distance = np.abs(offset_values)
    passed = np.zeros_like(distance)
    for limit_value in bounds_table:
        passed = passed + (distance >= int(limit_value)).astype(np.int32)
    coarse = np.where(distance < exact_part, distance, exact_part + passed)
    return coarse + (offset_values > 0).astype(np.int32) * (bucket_total // 2)


def one_hot_rows(offset_values, bucket_total):
    ids = bucket_index(np.asarray(offset_values, np.int32), bucket_total, MAX_DIST)
    return (ids[:, None] == np.arange(bucket_total)[None, :]).astype(np.float32)


def nn(left, right):
    return lax.dot_general(left, right, (((1,), (0,)), ((), ())), preferred_element_type=F32)


def nt(left, right):
    return lax.dot_general(left, right, (((1,), (1,)), ((), ())), preferred_element_type=F32)


def tn(left, right):
    return lax.dot_general(left, right, (((0,), (0,)), ((), ())), preferred_element_type=F32)


def norm_scale(values):
    return lax.rsqrt(jnp.mean(values * values, axis=-1, keepdims=True) + epsilon)


def norm_backward(values, gain, grad):
    scale = norm_scale(values)
    scaled = grad * gain
    dots = jnp.mean(scaled * values, axis=-1, keepdims=True)
    grad_values = scale * scaled - values * (scale * scale * scale * dots)
    grad_gain = jnp.sum(grad * (values * scale), axis=0, keepdims=True)
    return grad_values, grad_gain


def whole(shape):
    return pl.BlockSpec(shape, lambda *_: (0,) * len(shape))


def cost_of(flops, bytes_accessed, transcendentals):
    return pl.CostEstimate(flops=10 * int(flops), bytes_accessed=bytes_accessed, transcendentals=0)


def call(kernel, grid, in_specs, out_specs, out_shape, scratch=(), flops=0, vmem=56):
    return pl.pallas_call(
        kernel,
        grid=grid,
        in_specs=in_specs,
        out_specs=out_specs,
        out_shape=out_shape,
        scratch_shapes=list(scratch),
        compiler_params=pltpu.CompilerParams(vmem_limit_bytes=vmem * MIB),
        cost_estimate=cost_of(flops=flops, bytes_accessed=8 * MIB, transcendentals=0),
    )


def shaped(shape, kind):
    return jax.ShapeDtypeStruct(shape, kind)


def project_kernel(place_ref, tokens_ref, gain_ref, own_ref, other_ref, normed_ref, qkv_ref):
    step = pl.program_id(0)
    own_half = 1 - place_ref[2]

    @pl.when(step == 0)
    def _():
        values = tokens_ref[...].astype(F32)
        normed_ref[...] = (values * norm_scale(values) * gain_ref[...]).astype(BF16)

    @pl.when((step < 2) & (own_half * 2 + step < 3))
    def _():
        qkv_ref[...] = nn(normed_ref[...], own_ref[...]).astype(BF16)

    @pl.when((step >= 2) & (step - own_half * 2 < 3))
    def _():
        qkv_ref[...] = nn(normed_ref[...], other_ref[...]).astype(BF16)


def project(place, tokens, gain, own, other):
    length, width = tokens.shape

    def column(j, place_ref):
        own_half = 1 - place_ref[2]
        return (0, jnp.where(j < 2, own_half * 2 + j, j - own_half * 2))

    def full(*shape):
        return pl.BlockSpec(shape, lambda j, place_ref: (0,) * len(shape))

    return pl.pallas_call(
        project_kernel,
        grid_spec=pltpu.PrefetchScalarGridSpec(
            num_scalar_prefetch=1,
            grid=(4,),
            in_specs=[
                full(length, width),
                full(1, width),
                pl.BlockSpec((width, width), lambda j, place_ref: (0, jnp.minimum(j, 1))),
                pl.BlockSpec((width, width), lambda j, place_ref: (0, jnp.maximum(j - 2, 0))),
            ],
            out_specs=[full(length, width), pl.BlockSpec((length, width), column)],
        ),
        out_shape=[shaped((length, width), BF16), shaped((length, 4 * width), BF16)],
        compiler_params=pltpu.CompilerParams(vmem_limit_bytes=56 * MIB),
        cost_estimate=cost_of(
            flops=6 * length * width * width, bytes_accessed=8 * MIB, transcendentals=0
        ),
    )(place, tokens, gain, own, other)


QB = 256
KB = 128


def head_lanes(shape, which, size):
    lanes = lax.broadcasted_iota(jnp.int32, shape, 1)
    return (lanes < size) == (which == 0)


def attend_kernel(q_ref, k_ref, v_ref, line_ref, fill_ref, mixed_ref, probs_ref):
    length, pair = q_ref.shape
    size = pair // 2
    queries = q_ref[...]
    keys = k_ref[...]
    values_t = v_ref[...].T
    fill = fill_ref[...]
    heads = []
    for a in range(2):
        own = jnp.where(head_lanes(queries.shape, a, size), queries, jnp.zeros_like(queries))
        line = jnp.broadcast_to(line_ref[0, a : a + 1, :], (KB, 2 * length))
        band = pltpu.roll(line, 0, 1, stride=1, stride_axis=0)
        parts = []
        for qb in range(0, length, QB):
            raw = nt(keys, own[qb : qb + QB])
            rows = []
            for kb in range(0, length, KB):
                start = length - KB - kb + qb
                rows.append(
                    raw[kb : kb + KB] + (band[:, start : start + QB] + fill[kb : kb + KB])
                )
            scores = jnp.concatenate(rows, axis=0)
            peak = jnp.max(scores, axis=0, keepdims=True)
            weights = jnp.exp(scores - peak)
            total = jnp.sum(weights, axis=0, keepdims=True)
            probs = (weights * (1.0 / total)).astype(BF16)
            probs_ref[a, :, qb : qb + QB] = probs
            parts.append(nn(values_t[a * size : (a + 1) * size], probs))
        heads.append(jnp.concatenate(parts, axis=1))
    mixed_ref[...] = jnp.concatenate(heads, axis=0).T.astype(BF16)


def attend(qkv, lines, fill, head_count):
    length = qkv.shape[0]
    width = qkv.shape[1] // 4
    pairs = head_count // 2
    size = width // pairs

    def column(base):
        return pl.BlockSpec((length, size), lambda p: (0, base + p))

    return call(
        attend_kernel,
        (pairs,),
        [
            column(0),
            column(pairs),
            column(2 * pairs),
            pl.BlockSpec((1, 2, 2 * length), lambda p: (p, 0, 0)),
            whole((length, 1)),
        ],
        [column(0), pl.BlockSpec((2, length, length), lambda p: (p, 0, 0))],
        [shaped((length, width), BF16), shaped((head_count, length, length), BF16)],
        flops=8 * head_count * length * length * size,
    )(qkv, qkv, qkv, lines, fill)


def attend_back_kernel(
    q_ref, k_ref, v_ref, grad_ref, probs_ref, dq_ref, dk_ref, dv_ref, line_ref
):
    length, pair = q_ref.shape
    size = pair // 2
    queries = q_ref[...]
    keys_t = k_ref[...].T
    values = v_ref[...]
    grads = grad_ref[...]
    blocks = length // KB
    dq_heads, dk_heads, dv_heads = [], [], []
    for a in range(2):
        own = jnp.where(head_lanes(grads.shape, a, size), grads, jnp.zeros_like(grads))
        dq_parts = []
        dk = dv = None
        near = {}
        for qb in range(0, length, QB):
            probs = probs_ref[a, :, qb : qb + QB]
            probs_wide = probs.astype(F32)
            pulled = nt(values, own[qb : qb + QB])
            dots = jnp.sum(probs_wide * pulled, axis=0, keepdims=True)
            grad_scores = (probs_wide * (pulled - dots)).astype(BF16)
            dq_parts.append(nn(keys_t[a * size : (a + 1) * size], grad_scores))
            dk_part = nn(grad_scores, queries[qb : qb + QB])
            dv_part = nn(probs, grads[qb : qb + QB])
            dk = dk_part if dk is None else dk + dk_part
            dv = dv_part if dv is None else dv + dv_part
            wide = grad_scores.astype(F32)
            for i in range(blocks):
                for j in range(QB // KB):
                    gap = i - (qb // KB + j)
                    gap = max(-2, min(2, gap))
                    piece = wide[i * KB : (i + 1) * KB, j * KB : (j + 1) * KB]
                    near[gap] = piece if gap not in near else near[gap] + piece
        dq_heads.append(jnp.concatenate(dq_parts, axis=1))
        dk_heads.append(dk)
        dv_heads.append(dv)
        fold = jnp.concatenate([near[1], near[0], near[-1], jnp.zeros_like(near[0])], axis=1)
        rows = KB
        while rows > 8:
            rows //= 2
            fold = fold[:rows] + pltpu.roll(fold[rows : 2 * rows], 4 * KB - rows, 1)
        line_ref[0, a, :, 0 : 4 * KB] = fold
        far = jnp.concatenate([near[2], near[-2]], axis=1)
        line_ref[0, a, :, 4 * KB : 6 * KB] = jnp.sum(far.reshape(KB // 8, 8, 2 * KB), axis=0)
    first = head_lanes(queries.shape, 0, size)
    dq_ref[...] = jnp.concatenate(dq_heads, axis=0).T.astype(BF16)
    dk_ref[...] = jnp.where(first, dk_heads[0], dk_heads[1]).astype(BF16)
    dv_ref[...] = jnp.where(first, dv_heads[0], dv_heads[1]).astype(BF16)


def attend_back(qkv, grad_mixed, probs):
    head_count, length, _ = probs.shape
    width = grad_mixed.shape[1]
    pairs = head_count // 2
    size = width // pairs

    def column(base):
        return pl.BlockSpec((length, size), lambda p: (0, base + p))

    grad_shape = shaped((length, width), BF16)
    return call(
        attend_back_kernel,
        (pairs,),
        [
            column(0),
            column(pairs),
            column(2 * pairs),
            column(0),
            pl.BlockSpec((2, length, length), lambda p: (p, 0, 0)),
        ],
        [
            column(0),
            column(0),
            column(0),
            pl.BlockSpec((1, 2, 8, 6 * KB), lambda p: (p, 0, 0, 0)),
        ],
        [grad_shape, grad_shape, grad_shape, shaped((pairs, 2, 8, 6 * KB), F32)],
        flops=12 * head_count * length * length * size,
    )(qkv, qkv, qkv, grad_mixed, probs)


def line_one_hot(bucket_total):
    column = np.arange(4 * KB)
    rows = []
    for s in range(8):
        place = (column - s) % (4 * KB)
        offset = np.where(place <= 3 * KB, KB - place, 5 * KB - place)
        rows.append(np.concatenate([offset, np.full(KB, 3 * KB), np.full(KB, -3 * KB)]))
    return one_hot_rows(np.concatenate(rows), bucket_total)


def output_weight_of(place_ref, own_ref, other_ref, use):
    @pl.when(place_ref[2] == 0)
    def _():
        use(own_ref)

    @pl.when(place_ref[2] == 1)
    def _():
        use(other_ref)


def residual_kernel(
    place_ref, tokens_ref, mixed_ref, own_ref, other_ref, gain_ref, residual_ref, normed_ref
):
    def use(weight_ref):
        residual_ref[...] = tokens_ref[...].astype(F32) + nn(mixed_ref[...], weight_ref[...])

    output_weight_of(place_ref, own_ref, other_ref, use)
    residual = residual_ref[...]
    normed_ref[...] = (residual * norm_scale(residual) * gain_ref[...]).astype(BF16)


def residual_step(place, tokens, mixed, own, other, gain):
    length, width = tokens.shape

    def full(*shape):
        return pl.BlockSpec(shape, lambda j, place_ref: (0,) * len(shape))

    table = full(length, width)
    weight = pl.BlockSpec((width, width), lambda j, place_ref: (0, 1))
    return pl.pallas_call(
        residual_kernel,
        grid_spec=pltpu.PrefetchScalarGridSpec(
            num_scalar_prefetch=1,
            grid=(1,),
            in_specs=[table, table, weight, weight, full(1, width)],
            out_specs=[table, table],
        ),
        out_shape=[shaped((length, width), F32), shaped((length, width), BF16)],
        compiler_params=pltpu.CompilerParams(vmem_limit_bytes=56 * MIB),
        cost_estimate=cost_of(
            flops=2 * length * width * width, bytes_accessed=8 * MIB, transcendentals=0
        ),
    )(place, tokens, mixed, own, other, gain)


DEEP = 4


def blocks_of(place_ref, read_a, read_b, write):
    wide = place_ref[0]
    for dx in range(2):
        for dy in range(2):
            for k in range(DEEP):
                to_wide, to_narrow = wide ^ (2 * k + dx), place_ref[1] ^ dy
                write(0, dx, dy, k, read_a(to_wide, to_narrow))
                write(1, dy, dx, k, read_b(to_wide, to_narrow))


def write_mine(refs):
    def write(which, part, row, k, value):
        refs[2 * which + part][row, k] = value

    return write


def write_other(ref):
    def write(which, part, row, k, value):
        ref[which, part, row, k] = value

    return write


FEED_STEPS = 2


def feed_kernel(last, *refs):
    place_ref, normed_ref, grad_ref, base_ref, expand_ref, contract_ref = refs[:6]
    refs = refs[6:]
    if last:
        pulled_in_ref, residual_ref, gain_ref, own_ref, other_ref = refs[:5]
        out_ref, grad_residual_ref, grad_low_ref, grad_mixed_ref, gain_grad_ref = refs[5:10]
        refs = refs[10:]
        mine = refs[:4]
        refs = refs[4:]
    else:
        out_ref, pulled_out_ref, both_ref = refs[:3]
        refs = refs[3:]
    total_ref, pulled_ref, turned_ref, expand_grad_ref, contract_grad_ref = refs
    step = pl.program_id(0)

    @pl.when(step == 0)
    def _():
        total_ref[...] = base_ref[...]
        pulled_ref[...] = pulled_in_ref[...] if last else jnp.zeros_like(pulled_ref)
        turned_ref[...] = normed_ref[...].T

    expand = expand_ref[0]
    contract = contract_ref[0]
    grad_block = grad_ref[...]
    pre = nn(normed_ref[...], expand)
    grad_hidden = nt(grad_block, contract)
    scale = np.float32(np.sqrt(2.0 / np.pi))
    square = pre * pre
    bent = jnp.tanh(pre * (scale + (scale * np.float32(0.044715)) * square))
    half = 0.5 + 0.5 * bent
    hidden = (pre * half).astype(BF16)
    slope = half + (0.5 * pre) * (1.0 - bent * bent) * (
        scale + (scale * np.float32(3 * 0.044715)) * square
    )
    grad_pre = (grad_hidden * slope).astype(BF16)
    total_ref[...] += nn(hidden, contract)
    pulled_ref[...] += nt(grad_pre, expand)
    block = expand.shape[1]
    contract_grad_ref[pl.ds(pl.multiple_of(step * block, block), block), :] = tn(
        hidden, grad_block
    ).astype(BF16)
    expand_grad_ref[step] = nn(turned_ref[...], grad_pre).astype(BF16)

    @pl.when(step == pl.num_programs(0) - 1)
    def _():
        rows = expand_grad_ref.shape[1] // (2 * DEEP)

        def read_expand(wide, narrow):
            return expand_grad_ref[narrow, pl.ds(pl.multiple_of(wide * rows, 16), rows), :]

        def read_contract(wide, narrow):
            start = pl.multiple_of((wide * 2 + narrow) * rows, 16)
            return contract_grad_ref[pl.ds(start, rows), :]

        if last:
            blocks_of(place_ref, read_expand, read_contract, write_mine(mine))
            out_ref[...] = total_ref[...].astype(BF16)
            grad_values, grad_gain = norm_backward(
                residual_ref[...], gain_ref[...], pulled_ref[...]
            )
            grad_residual = grad_block.astype(F32) + grad_values
            grad_residual_ref[...] = grad_residual
            grad_low_ref[...] = grad_residual.astype(BF16)
            gain_grad_ref[...] = grad_gain

            def use(weight_ref):
                grad_mixed_ref[...] = nt(grad_low_ref[...], weight_ref[...]).astype(BF16)

            output_weight_of(place_ref, own_ref, other_ref, use)
        else:
            blocks_of(place_ref, read_expand, read_contract, write_other(both_ref))
            out_ref[...] = total_ref[...]
            pulled_out_ref[...] = pulled_ref[...]


def feed_half(last, place, normed, grad_block, base, weights, more=()):
    length, width = normed.shape
    half = weights.shape[1]
    block = half // FEED_STEPS
    rows = width // (2 * DEEP)

    def full(*shape):
        return pl.BlockSpec(shape, lambda j, place_ref: (0,) * len(shape))

    table = full(length, width)
    in_specs = [
        table,
        table,
        table,
        pl.BlockSpec((1, width, block), lambda j, place_ref: (0, j, 0)),
        pl.BlockSpec((1, block, width), lambda j, place_ref: (1, j, 0)),
    ]
    grad_dims = (2, DEEP, rows, block)
    if last:
        weight = pl.BlockSpec((width, width), lambda j, place_ref: (0, 1))
        in_specs += [table, table, full(1, width), weight, weight]
        out_specs = [table, table, table, table, full(1, width)] + [full(*grad_dims)] * 4
        out_shape = [
            shaped((length, width), BF16),
            shaped((length, width), F32),
            shaped((length, width), BF16),
            shaped((length, width), BF16),
            shaped((1, width), F32),
        ] + [shaped(grad_dims, BF16)] * 4
    else:
        out_specs = [table, table, full(2, 2, *grad_dims)]
        out_shape = [
            shaped((length, width), F32),
            shaped((length, width), F32),
            shaped((2, 2) + grad_dims, BF16),
        ]
    return pl.pallas_call(
        functools.partial(feed_kernel, last),
        grid_spec=pltpu.PrefetchScalarGridSpec(
            num_scalar_prefetch=1,
            grid=(FEED_STEPS,),
            in_specs=in_specs,
            out_specs=out_specs,
            scratch_shapes=[
                pltpu.VMEM((length, width), F32),
                pltpu.VMEM((length, width), F32),
                pltpu.VMEM((width, length), BF16),
                pltpu.VMEM((FEED_STEPS, width, block), BF16),
                pltpu.VMEM((half, width), BF16),
            ],
        ),
        out_shape=out_shape,
        compiler_params=pltpu.CompilerParams(vmem_limit_bytes=56 * MIB),
        cost_estimate=cost_of(
            flops=6 * length * width * half * 2, bytes_accessed=8 * MIB, transcendentals=0
        ),
    )(place, normed, grad_block, base, weights, weights, *more)


def project_grad_kernel(place_ref, *refs):
    normed_ref, dq_ref, dk_ref, dv_ref, mixed_ref, grad_ref = refs[:6]
    mine = refs[6:10]
    other_ref, turned_ref, grads_ref = refs[10:]
    step = pl.program_id(0)
    width = dq_ref.shape[1]
    rows = width // (4 * DEEP)

    @pl.when(step == 0)
    def _():
        turned_ref[...] = normed_ref[...].T
        grads_ref[0] = nn(turned_ref[...], dq_ref[...]).astype(BF16)

    @pl.when(step == 1)
    def _():
        grads_ref[1] = nn(turned_ref[...], dk_ref[...]).astype(BF16)

    @pl.when(step == 2)
    def _():
        grads_ref[2] = nn(turned_ref[...], dv_ref[...]).astype(BF16)

    @pl.when(step == 3)
    def _():
        grads_ref[3] = tn(mixed_ref[...], grad_ref[...]).astype(BF16)

        def reader(which, core):
            def read(wide, narrow):
                start = pl.multiple_of((wide * 2 + core) * rows, 16)
                return grads_ref[2 * narrow + which, pl.ds(start, rows), :]

            return read

        core = place_ref[2]
        blocks_of(place_ref, reader(0, 1 - core), reader(1, 1 - core), write_other(other_ref))
        blocks_of(place_ref, reader(0, core), reader(1, core), write_mine(mine))


def project_grad(place, normed, dq, dk, dv, mixed, grad):
    length, width = normed.shape
    rows = width // (4 * DEEP)

    def full(*shape):
        return pl.BlockSpec(shape, lambda j, place_ref: (0,) * len(shape))

    dims = (2, DEEP, rows, width)
    return pl.pallas_call(
        project_grad_kernel,
        grid_spec=pltpu.PrefetchScalarGridSpec(
            num_scalar_prefetch=1,
            grid=(4,),
            in_specs=[full(length, width)] * 6,
            out_specs=[full(*dims)] * 4 + [full(2, 2, *dims)],
            scratch_shapes=[
                pltpu.VMEM((width, length), BF16),
                pltpu.VMEM((4, width, width), BF16),
            ],
        ),
        out_shape=[shaped(dims, BF16)] * 4 + [shaped((2, 2) + dims, BF16)],
        compiler_params=pltpu.CompilerParams(vmem_limit_bytes=56 * MIB),
        cost_estimate=cost_of(
            flops=8 * length * width * width, bytes_accessed=8 * MIB, transcendentals=0
        ),
    )(place, normed, dq, dk, dv, mixed, grad)


HALF = DEEP // 2
SOURCES = [
    (range(DEEP), 0, 0),
    (range(DEEP), 1, 0),
    (range(DEEP), 0, 1),
    (range(HALF), 1, 1),
    (range(HALF, DEEP), 1, 1),
]
EARLY, LATE = (0, 2), (1, 3)
FEED_SOURCES = [
    source
    for some in (EARLY, LATE)
    for source in [(some, 0, 0), (some, 1, 0), (some, 0, 1), (some[:1], 1, 1), (some[1:], 1, 1)]
]


def assemble_kernel(place_ref, *refs):
    out_ref = refs[-1]
    for ref, (deep, dx, dy) in zip(refs, SOURCES):
        rows = ref.shape[1]
        for i in range(ref.shape[0]):
            start = (place_ref[0] ^ (2 * deep[i] + dx)) * 2 + (place_ref[1] ^ dy)
            out_ref[pl.ds(pl.multiple_of(start * rows, 16), rows), :] = ref[i]


def assemble(place, pieces):
    rows, columns = pieces[0].shape[1:]
    dims = (4 * DEEP * rows, columns)
    return pl.pallas_call(
        assemble_kernel,
        grid_spec=pltpu.PrefetchScalarGridSpec(
            num_scalar_prefetch=1,
            grid=(1,),
            in_specs=[
                pl.BlockSpec(piece.shape, lambda j, place_ref: (0, 0, 0)) for piece in pieces
            ],
            out_specs=pl.BlockSpec(dims, lambda j, place_ref: (0, 0)),
        ),
        out_shape=shaped(dims, BF16),
        compiler_params=pltpu.CompilerParams(vmem_limit_bytes=56 * MIB),
        cost_estimate=cost_of(flops=0, bytes_accessed=8 * MIB, transcendentals=0),
    )(place, *pieces)


def assemble_feed_kernel(place_ref, *refs):
    out_ref = refs[-1]
    for ref, (deep, dx, dy) in zip(refs, FEED_SOURCES):
        rows, columns = ref.shape[2:]
        half = rows // FEED_STEPS
        for i in range(ref.shape[0]):
            start = (place_ref[0] ^ (2 * deep[i] + dx)) * 2 + (place_ref[1] ^ dy)
            for j in range(FEED_STEPS):
                base = pl.multiple_of(j * columns + start * half, 16)
                out_ref[0, pl.ds(base, half), :] = ref[i, 0, j * half : (j + 1) * half]
            out_ref[1, pl.ds(pl.multiple_of(start * rows, 16), rows), :] = ref[i, 1]


def assemble_feed(place, pieces):
    rows, columns = pieces[0].shape[2:]
    dims = (2, 4 * DEEP * rows, columns)
    return pl.pallas_call(
        assemble_feed_kernel,
        grid_spec=pltpu.PrefetchScalarGridSpec(
            num_scalar_prefetch=1,
            grid=(1,),
            in_specs=[
                pl.BlockSpec(piece.shape, lambda j, place_ref: (0, 0, 0, 0)) for piece in pieces
            ],
            out_specs=pl.BlockSpec(dims, lambda j, place_ref: (0, 0, 0)),
        ),
        out_shape=shaped(dims, BF16),
        compiler_params=pltpu.CompilerParams(vmem_limit_bytes=56 * MIB),
        cost_estimate=cost_of(flops=0, bytes_accessed=8 * MIB, transcendentals=0),
    )(place, *pieces)


def finish_feed_kernel(place_ref, *refs):
    parts, (expand_ref, contract_ref) = refs[:-2], refs[-2:]
    rows, columns = parts[0].shape[1:]
    unit = columns // DEEP
    for ref, (dy, dc) in zip(parts, ((0, 0), (0, 1), (1, 0), (1, 1))):
        y, c = place_ref[1] ^ dy, place_ref[2] ^ dc
        contract_ref[pl.ds(pl.multiple_of((c * 2 + y) * rows, 8), rows), :] = ref[1].astype(F32)
        for to_y in range(2):
            for to_c in range(2):

                @pl.when((y == to_y) & (c == to_c))
                def _(ref=ref, to_y=to_y, to_c=to_c):
                    value = ref[0].astype(F32)
                    for i in range(DEEP):
                        base = ((to_y * DEEP + i) * 2 + to_c) * unit
                        expand_ref[:, base : base + unit] = value[:, i * unit : (i + 1) * unit]


def finish_feed(place, parts):
    rows, columns = parts[0].shape[1:]
    dims = [(rows, 4 * columns), (4 * rows, columns)]
    return pl.pallas_call(
        finish_feed_kernel,
        grid_spec=pltpu.PrefetchScalarGridSpec(
            num_scalar_prefetch=1,
            grid=(1,),
            in_specs=[pl.BlockSpec(part.shape, lambda j, place_ref: (0, 0, 0)) for part in parts],
            out_specs=[pl.BlockSpec(d, lambda j, place_ref: (0, 0)) for d in dims],
        ),
        out_shape=[shaped(d, F32) for d in dims],
        compiler_params=pltpu.CompilerParams(vmem_limit_bytes=56 * MIB),
        cost_estimate=cost_of(flops=0, bytes_accessed=4 * MIB, transcendentals=0),
    )(place, *parts)


def finish_square_kernel(place_ref, *refs):
    parts, outs = refs[:-4], refs[-4:]
    rows = parts[0].shape[1]
    for ref, (dy, dc) in zip(parts, ((0, 0), (0, 1), (1, 0), (1, 1))):
        y, c = place_ref[1] ^ dy, place_ref[2] ^ dc
        for to_y in range(2):

            @pl.when(y == to_y)
            def _(ref=ref, to_y=to_y, c=c):
                for i in range(2):
                    start = pl.multiple_of(c * rows, 8)
                    outs[2 * to_y + i][pl.ds(start, rows), :] = ref[i].astype(F32)


def finish_square(place, parts):
    rows, columns = parts[0].shape[1:]
    dims = (2 * rows, columns)
    return pl.pallas_call(
        finish_square_kernel,
        grid_spec=pltpu.PrefetchScalarGridSpec(
            num_scalar_prefetch=1,
            grid=(1,),
            in_specs=[pl.BlockSpec(part.shape, lambda j, place_ref: (0, 0, 0)) for part in parts],
            out_specs=[pl.BlockSpec(dims, lambda j, place_ref: (0, 0))] * 4,
        ),
        out_shape=[shaped(dims, F32)] * 4,
        compiler_params=pltpu.CompilerParams(vmem_limit_bytes=56 * MIB),
        cost_estimate=cost_of(flops=0, bytes_accessed=4 * MIB, transcendentals=0),
    )(place, *parts)


def tokens_back_kernel(
    place_ref,
    dq_ref,
    dk_ref,
    dv_ref,
    own_ref,
    other_ref,
    tokens_ref,
    gain_ref,
    residual_ref,
    out_ref,
    gain_grad_ref,
    pulled_ref,
):
    width = dq_ref.shape[1]

    def pull(first_ref, second_ref):
        pulled = nt(dq_ref[...], first_ref[:, 0:width])
        pulled += nt(dk_ref[...], first_ref[:, width : 2 * width])
        pulled += nt(dv_ref[...], second_ref[:, 0:width])
        pulled_ref[...] = pulled

    @pl.when(place_ref[2] == 1)
    def _():
        pull(own_ref, other_ref)

    @pl.when(place_ref[2] == 0)
    def _():
        pull(other_ref, own_ref)

    grad_values, grad_gain = norm_backward(
        tokens_ref[...].astype(F32), gain_ref[...], pulled_ref[...]
    )
    out_ref[...] = residual_ref[...] + grad_values
    gain_grad_ref[...] = grad_gain


def tokens_back(place, dq, dk, dv, own, other, tokens, gain, grad_residual):
    length, width = tokens.shape

    def full(*shape):
        return pl.BlockSpec(shape, lambda j, place_ref: (0,) * len(shape))

    table = full(length, width)
    return pl.pallas_call(
        tokens_back_kernel,
        grid_spec=pltpu.PrefetchScalarGridSpec(
            num_scalar_prefetch=1,
            grid=(1,),
            in_specs=[table, table, table]
            + [full(width, 2 * width)] * 2
            + [table, full(1, width), table],
            out_specs=[table, full(1, width)],
            scratch_shapes=[pltpu.VMEM((length, width), F32)],
        ),
        out_shape=[shaped((length, width), F32), shaped((1, width), F32)],
        compiler_params=pltpu.CompilerParams(vmem_limit_bytes=56 * MIB),
        cost_estimate=cost_of(
            flops=6 * length * width * width, bytes_accessed=8 * MIB, transcendentals=0
        ),
    )(place, dq, dk, dv, own, other, tokens, gain, grad_residual)


def exchange(value, dz=0, dx=0, dy=0, dc=0):
    flip = ((2 * dz + dx) * 2 + dy) * 2 + dc
    total = 8 * DEEP
    return lax.ppermute(value, ("wide", "narrow"), [(i, i ^ flip) for i in range(total)])


def after(value, *done):
    return lax.optimization_barrier((value,) + done)[0]


def together(*values):
    return lax.optimization_barrier(values)


def gather_stage_z(piece):
    return jnp.stack([piece] + [exchange(piece, dz=k) for k in range(1, DEEP)])


def gather_stage_xy(near):
    return exchange(near, dx=1), exchange(near, dy=1)


def gather_stage_far(over_x, over_y):
    half = over_x.shape[0] // 2
    return exchange(over_y[:half], dx=1), exchange(over_x[half:], dy=1)


def low(value):
    return value.astype(BF16)


def add(*values):
    return sum(value.astype(F32) for value in values)


def reduce_first_out(mine, other):
    return low(add(mine[1], other[0, 1])), low(add(mine[3], other[1, 1]))


def reduce_first(outs):
    return exchange(outs[0], dx=1), exchange(outs[1], dy=1)


def reduce_second_out(mine, other, first):
    return tuple(low(add(mine[2 * i][1], other[i, 0, 1], first[i][1])) for i in range(2))


def reduce_second(outs):
    return exchange(outs[0], dy=1), exchange(outs[1], dx=1)


def reduce_level(mine, other, first, second, k):
    return jnp.stack(
        [add(mine[2 * i][0, k], other[i, 0, 0, k], first[i][0, k], second[i][k]) for i in range(2)]
    )


def reduce_deep_out(*parts):
    return tuple(low(reduce_level(*parts, k)) for k in range(1, DEEP))


def reduce_deep(outs):
    return tuple(exchange(out, dz=k + 1) for k, out in enumerate(outs))


def reduce_last(parts, deep):
    return low(reduce_level(*parts, 0) + add(*deep))


def spread_out(part):
    return exchange(part, dc=1), exchange(part, dy=1), exchange(part, dy=1, dc=1)


def on_device(
    tokens,
    query_weight,
    key_weight,
    value_weight,
    output_weight,
    expand_weight,
    contract_weight,
    attention_gain,
    feedforward_gain,
    bias_table,
    query_length,
    passage_length,
    pair_order,
    regrouped_grad,
):
    row_count, length, width = tokens.shape
    bucket_count, head_count = bias_table.shape
    wide_index = lax.axis_index("wide")
    wide_count = lax.axis_size("wide")
    narrow_index = lax.axis_index("narrow")
    narrow_count = lax.axis_size("narrow")
    by_hand = wide_count == 2 * DEEP and narrow_count == 4
    hidden_count = expand_weight.shape[1]
    part_rows = hidden_count // (4 * DEEP)

    square_weights = (query_weight, key_weight, value_weight, output_weight)
    if by_hand:
        narrow_y, core = narrow_index // 2, narrow_index % 2
    else:
        wide_index = narrow_y = core = jnp.int32(0)
    place = jnp.stack([wide_index, narrow_y, core]).astype(jnp.int32)

    group_rows = regrouped_grad.shape[0]
    chosen = lax.dynamic_slice_in_dim(pair_order, narrow_index * group_rows, group_rows)
    local_rows = chosen // (row_count * narrow_count) * row_count + chosen % row_count
    arranged = jnp.zeros_like(regrouped_grad).at[local_rows].set(regrouped_grad)

    spot = np.arange(2 * length)
    offsets = np.where(spot <= 2 * length - KB, length - KB - spot, 3 * length - KB - spot)
    band_hot = jnp.asarray(one_hot_rows(np.clip(offsets, 1 - length, length - 1), bucket_count))
    lines = jnp.dot(bias_table.T, band_hot.T, precision=lax.Precision.HIGHEST)
    lines = lines.reshape(head_count // 2, 2, 2 * length)
    positions = jnp.arange(length, dtype=jnp.int32)
    fill = jnp.where(positions < query_length[0] + passage_length[0], 0.0, negative)
    fill = fill.astype(F32)[:, None]

    if by_hand:
        half_rows = query_weight.shape[0] // 2
        own_half = 1 - core
        first = jnp.concatenate(square_weights[:2], axis=1)
        second = jnp.concatenate(square_weights[2:], axis=1)
        square_piece = lax.dynamic_slice_in_dim(
            jnp.where(core == 1, first, second), narrow_y * half_rows, half_rows
        )
        expand_piece = lax.dynamic_slice_in_dim(
            lax.dynamic_index_in_dim(
                expand_weight.reshape(-1, 2 * DEEP, 2, part_rows), own_half, 2, False
            ).reshape(-1, hidden_count // 2),
            narrow_y * half_rows,
            half_rows,
        )
        contract_rows = contract_weight.shape[0] // 4
        contract_piece = lax.dynamic_slice_in_dim(
            contract_weight, (own_half * 2 + narrow_y) * contract_rows, contract_rows
        )
        feed_piece = jnp.stack(
            [
                jnp.concatenate(
                    [expand_piece[:, j * width : (j + 1) * width] for j in range(FEED_STEPS)]
                ),
                contract_piece,
            ]
        )
        square_near = gather_stage_z(square_piece)
        square_near, arranged, lines, fill, feed_piece = together(
            square_near, arranged, lines, fill, feed_piece
        )
        square_xy = gather_stage_xy(square_near)
        feed_two = exchange(feed_piece, dz=2)
        feed_early = jnp.stack([feed_piece, feed_two])
        square_xy, feed_early, feed_piece = together(square_xy, feed_early, feed_piece)
        square_far = gather_stage_far(*square_xy)
        feed_one = exchange(feed_piece, dz=1)
        square_far, feed_one = together(square_far, feed_one)
        square_own = assemble(place, [square_near, *square_xy, *square_far])
        square_own, feed_early, feed_piece = together(square_own, feed_early, feed_piece)
        square_other = exchange(square_own, dc=1)
        feed_early_xy = gather_stage_xy(feed_early)
        feed_three = exchange(feed_piece, dz=3)
    else:

        def gathered(weight):
            return lax.all_gather(weight, "wide", axis=0, tiled=True)

        square_other = gathered(jnp.concatenate(square_weights[:2], axis=1))
        square_own = gathered(jnp.concatenate(square_weights[2:], axis=1))
        full_expand = gathered(expand_weight).reshape(width, 2 * DEEP, 2, part_rows)
        full_contract = gathered(contract_weight).reshape(2 * DEEP, 2, part_rows, width)
        feed_other, feed_own = (
            jnp.stack(
                [
                    full_expand[:, :, i]
                    .reshape(width, FEED_STEPS, -1)
                    .transpose(1, 0, 2)
                    .reshape(-1, width),
                    full_contract[:, i].reshape(-1, width),
                ]
            )
            for i in range(2)
        )

    inputs = tokens.reshape(length, width)
    gain_one = attention_gain[None]
    gain_two = feedforward_gain[None]
    attention_input, qkv = project(place, inputs, gain_one, square_own, square_other)
    if by_hand:
        arranged = after(arranged, qkv)
    grad_block = lax.all_to_all(arranged, "wide", split_axis=0, concat_axis=0, tiled=True).reshape(
        length, width
    )
    if by_hand:
        qkv, feed_early_xy, feed_three = together(qkv, feed_early_xy, feed_three)
        feed_late = jnp.stack([feed_one, feed_three])
        qkv, feed_late = together(qkv, feed_late)
        feed_late_xy = gather_stage_xy(feed_late)
        feed_early_far = gather_stage_far(*feed_early_xy)
    mixed, probs = attend(qkv, lines, fill, head_count)
    if by_hand:
        mixed, grad_block, feed_late_xy, feed_early_far = together(
            mixed, grad_block, feed_late_xy, feed_early_far
        )
        feed_late_far = gather_stage_far(*feed_late_xy)
    residual, expand_input = residual_step(
        place, inputs, mixed, square_own, square_other, gain_two
    )
    if by_hand:
        feed_own = assemble_feed(
            place,
            [feed_early, *feed_early_xy, *feed_early_far]
            + [feed_late, *feed_late_xy, *feed_late_far],
        )
        feed_other = exchange(feed_own, dc=1)
    partial_out, partial_pulled, feed_sent = feed_half(
        False, place, expand_input, grad_block, residual, feed_own
    )
    if by_hand:
        feed_got = exchange(feed_sent, dc=1)
    results = feed_half(
        True,
        place,
        expand_input,
        grad_block,
        partial_out,
        feed_other,
        (partial_pulled, residual, gain_two, square_own, square_other),
    )
    block_output, grad_residual, grad_low, grad_mixed, gain_two_grad = results[:5]
    feed_mine = results[5:9]
    if by_hand:
        feed_got, grad_mixed, block_output = together(feed_got, grad_mixed, block_output)
        outs = reduce_first_out(feed_mine, feed_got)
        grad_mixed, *outs = together(grad_mixed, *outs)
        feed_first = reduce_first(outs)
    dq, dk, dv, line_grads = attend_back(qkv, grad_mixed, probs)
    results = project_grad(place, attention_input, dq, dk, dv, mixed, grad_low)
    square_mine, square_sent = results[:4], results[4]
    table_grad = jnp.dot(
        jnp.asarray(line_one_hot(bucket_count).T),
        line_grads.reshape(head_count, -1).T,
        precision=lax.Precision.HIGHEST,
    )
    if by_hand:
        block_output = after(block_output, square_sent)
    received = lax.all_to_all(
        block_output.reshape(-1, regrouped_grad.shape[1], width),
        "wide",
        split_axis=0,
        concat_axis=0,
        tiled=True,
    )
    if by_hand:
        square_sent, *feed_first = together(square_sent, *feed_first)
        square_got = exchange(square_sent, dc=1)
        outs = reduce_second_out(feed_mine, feed_got, feed_first)
        dq, *outs = together(dq, *outs)
        feed_second = reduce_second(outs)
    tokens_grad, gain_one_grad = tokens_back(
        place, dq, dk, dv, square_own, square_other, inputs, gain_one, grad_residual
    )
    small = jnp.concatenate([gain_one_grad[0], gain_two_grad[0], table_grad.reshape(-1)])
    small_count = small.shape[0]

    regrouped = jnp.take(received, local_rows, axis=0)
    if by_hand:
        small = jnp.pad(small, (0, -small_count % 1024)).reshape(-1, 128)
        square_got, small, table_grad = together(square_got, small, table_grad)
        outs = reduce_first_out(square_mine, square_got)
        square_first = reduce_first(outs)
        feed_second = after(feed_second, *outs)
        feed_parts = (feed_mine, feed_got, feed_first, feed_second)
        outs = reduce_deep_out(*feed_parts)
        feed_deep = reduce_deep(outs)
        square_first = after(square_first, *outs)
        small = small + exchange(small, dc=1)
        outs = reduce_second_out(square_mine, square_got, square_first)
        square_second = reduce_second(outs)
        feed_deep = after(feed_deep, *outs)
        small = small + exchange(after(small, *outs), dy=1)
        feed_deep, regrouped = together(feed_deep, regrouped)
        feed_part = reduce_last(feed_parts, feed_deep)
        feed_spread = spread_out(feed_part)
        square_second = after(square_second, feed_part)
        square_parts = (square_mine, square_got, square_first, square_second)
        outs = reduce_deep_out(*square_parts)
        square_deep = reduce_deep(outs)
        small = small + exchange(after(small, *outs), dx=1)
        feed_spread = after(feed_spread, *outs)
        final_expand, final_contract = finish_feed(place, (feed_part, *feed_spread))
        small = small + exchange(after(small, final_expand), dz=1)
        square_deep = after(square_deep, final_expand)
        square_part = reduce_last(square_parts, square_deep)
        square_spread = spread_out(square_part)
        small = small + exchange(after(small, square_part), dz=2)
        finals = finish_square(place, (square_part, *square_spread))
        small = small.reshape(-1)
    else:

        def summed(grad):
            part = lax.psum_scatter(grad, "wide", scatter_dimension=0, tiled=True)
            return lax.psum(part, "narrow").astype(F32)

        def stacked(which, mine, other):
            kept = jnp.stack(mine[2 * which : 2 * which + 2])
            return jnp.stack([kept, other[which]])

        expand_all = stacked(0, feed_mine, feed_sent)
        expand_all = expand_all.reshape(expand_all.shape[:5] + (DEEP, part_rows))
        expand_all = expand_all.transpose(3, 1, 4, 2, 5, 0, 6)
        contract_all = stacked(1, feed_mine, feed_sent).transpose(3, 2, 0, 1, 4, 5)
        first = stacked(0, square_mine, square_sent)
        second = stacked(1, square_mine, square_sent).transpose(0, 2, 1, 3, 4, 5)
        square_all = jnp.stack([first, second]).transpose(4, 2, 1, 5, 3, 0, 6)
        final_contract = summed(contract_all.reshape(hidden_count, width))
        final_expand = summed(expand_all.reshape(width, hidden_count))
        final_square = summed(square_all.reshape(width, 4 * width))
        finals = [final_square[:, i * width : (i + 1) * width] for i in range(4)]
        small = lax.psum(small, ("wide", "narrow"))

    return (
        regrouped,
        tokens_grad.reshape(row_count, length, width),
        *finals,
        final_expand,
        final_contract,
        small[:width],
        small[width : 2 * width],
        small[2 * width : small_count].reshape(bucket_count, head_count),
    )


def solution(mesh):
    in_specs = (
        P(("wide", "narrow"), None, None),
        P("wide", None),
        P("wide", None),
        P("wide", None),
        P("wide", None),
        P("wide", None),
        P("wide", None),
        P(),
        P(),
        P(),
        P(("wide", "narrow")),
        P(("wide", "narrow")),
        P(),
        P("narrow", "wide", None),
    )
    out_specs = (
        P("narrow", "wide", None),
        P(("wide", "narrow"), None, None),
        P("wide", None),
        P("wide", None),
        P("wide", None),
        P("wide", None),
        P("wide", None),
        P("wide", None),
        P(),
        P(),
        P(),
    )
    return jax.shard_map(
        on_device, mesh=mesh, in_specs=in_specs, out_specs=out_specs, check_vma=False
    )
```

```python
import functools

import jax
import jax.numpy as jnp
import numpy as np
from jax import lax
from jax.experimental import pallas as pl
from jax.experimental.pallas import tpu as pltpu
from jax.sharding import PartitionSpec as P

MAX_DIST = 128
epsilon = 1e-06
negative = -1000000000.0
F32 = jnp.float32
BF16 = jnp.bfloat16
MIB = 1024 * 1024


def bucket_index(offset_values, bucket_total, max_reach):
    exact_part = bucket_total // 4
    bounds_table = np.ceil(
        exact_part * (max_reach / exact_part) ** (np.arange(1, exact_part) / exact_part) - 1e-06
    ).astype(np.int32)
    distance = np.abs(offset_values)
    passed = np.zeros_like(distance)
    for limit_value in bounds_table:
        passed = passed + (distance >= int(limit_value)).astype(np.int32)
    coarse = np.where(distance < exact_part, distance, exact_part + passed)
    return coarse + (offset_values > 0).astype(np.int32) * (bucket_total // 2)


def one_hot_rows(offset_values, bucket_total):
    ids = bucket_index(np.asarray(offset_values, np.int32), bucket_total, MAX_DIST)
    return (ids[:, None] == np.arange(bucket_total)[None, :]).astype(np.float32)


def nn(left, right):
    return lax.dot_general(left, right, (((1,), (0,)), ((), ())), preferred_element_type=F32)


def nt(left, right):
    return lax.dot_general(left, right, (((1,), (1,)), ((), ())), preferred_element_type=F32)


def tn(left, right):
    return lax.dot_general(left, right, (((0,), (0,)), ((), ())), preferred_element_type=F32)


def norm_scale(values):
    return lax.rsqrt(jnp.mean(values * values, axis=-1, keepdims=True) + epsilon)


def norm_backward(values, gain, grad):
    scale = norm_scale(values)
    scaled = grad * gain
    dots = jnp.mean(scaled * values, axis=-1, keepdims=True)
    grad_values = scale * scaled - values * (scale * scale * scale * dots)
    grad_gain = jnp.sum(grad * (values * scale), axis=0, keepdims=True)
    return grad_values, grad_gain


def whole(shape):
    return pl.BlockSpec(shape, lambda *_: (0,) * len(shape))


def cost_of(flops, bytes_accessed, transcendentals):
    return pl.CostEstimate(flops=10 * int(flops), bytes_accessed=bytes_accessed, transcendentals=0)


def call(kernel, grid, in_specs, out_specs, out_shape, scratch=(), flops=0, vmem=56):
    return pl.pallas_call(
        kernel,
        grid=grid,
        in_specs=in_specs,
        out_specs=out_specs,
        out_shape=out_shape,
        scratch_shapes=list(scratch),
        compiler_params=pltpu.CompilerParams(vmem_limit_bytes=vmem * MIB),
        cost_estimate=cost_of(flops=flops, bytes_accessed=8 * MIB, transcendentals=0),
    )


def shaped(shape, kind):
    return jax.ShapeDtypeStruct(shape, kind)


def project_kernel(place_ref, tokens_ref, gain_ref, own_ref, other_ref, normed_ref, qkv_ref):
    step = pl.program_id(0)
    own_half = 1 - place_ref[2]

    @pl.when(step == 0)
    def _():
        values = tokens_ref[...].astype(F32)
        normed_ref[...] = (values * norm_scale(values) * gain_ref[...]).astype(BF16)

    @pl.when((step < 2) & (own_half * 2 + step < 3))
    def _():
        qkv_ref[...] = nn(normed_ref[...], own_ref[...]).astype(BF16)

    @pl.when((step >= 2) & (step - own_half * 2 < 3))
    def _():
        qkv_ref[...] = nn(normed_ref[...], other_ref[...]).astype(BF16)


def project(place, tokens, gain, own, other):
    length, width = tokens.shape

    def column(j, place_ref):
        own_half = 1 - place_ref[2]
        return (0, jnp.where(j < 2, own_half * 2 + j, j - own_half * 2))

    def full(*shape):
        return pl.BlockSpec(shape, lambda j, place_ref: (0,) * len(shape))

    return pl.pallas_call(
        project_kernel,
        grid_spec=pltpu.PrefetchScalarGridSpec(
            num_scalar_prefetch=1,
            grid=(4,),
            in_specs=[
                full(length, width),
                full(1, width),
                pl.BlockSpec((width, width), lambda j, place_ref: (0, jnp.minimum(j, 1))),
                pl.BlockSpec((width, width), lambda j, place_ref: (0, jnp.maximum(j - 2, 0))),
            ],
            out_specs=[full(length, width), pl.BlockSpec((length, width), column)],
        ),
        out_shape=[shaped((length, width), BF16), shaped((length, 4 * width), BF16)],
        compiler_params=pltpu.CompilerParams(vmem_limit_bytes=56 * MIB),
        cost_estimate=cost_of(
            flops=6 * length * width * width, bytes_accessed=8 * MIB, transcendentals=0
        ),
    )(place, tokens, gain, own, other)


QB = 512
KB = 128


def head_lanes(shape, which, size):
    lanes = lax.broadcasted_iota(jnp.int32, shape, 1)
    return (lanes < size) == (which == 0)


def attend_kernel(q_ref, k_ref, v_ref, line_ref, fill_ref, mixed_ref, probs_ref):
    length, pair = q_ref.shape
    size = pair // 2
    queries = q_ref[...]
    keys = k_ref[...]
    values_t = v_ref[...].T
    fill = fill_ref[...]
    heads = []
    for a in range(2):
        own = jnp.where(head_lanes(queries.shape, a, size), queries, jnp.zeros_like(queries))
        line = jnp.broadcast_to(line_ref[0, a : a + 1, :], (KB, 2 * length))
        band = pltpu.roll(line, 0, 1, stride=1, stride_axis=0)
        parts = []
        for qb in range(0, length, QB):
            raw = nt(keys, own[qb : qb + QB])
            rows = []
            for kb in range(0, length, KB):
                start = length - KB - kb + qb
                rows.append(
                    raw[kb : kb + KB] + (band[:, start : start + QB] + fill[kb : kb + KB])
                )
            scores = jnp.concatenate(rows, axis=0)
            peak = jnp.max(scores, axis=0, keepdims=True)
            weights = jnp.exp(scores - peak)
            total = jnp.sum(weights, axis=0, keepdims=True)
            probs = (weights * (1.0 / total)).astype(BF16)
            probs_ref[a, :, qb : qb + QB] = probs
            parts.append(nn(values_t[a * size : (a + 1) * size], probs))
        heads.append(jnp.concatenate(parts, axis=1))
    mixed_ref[...] = jnp.concatenate(heads, axis=0).T.astype(BF16)


def attend(qkv, lines, fill, head_count):
    length = qkv.shape[0]
    width = qkv.shape[1] // 4
    pairs = head_count // 2
    size = width // pairs

    def column(base):
        return pl.BlockSpec((length, size), lambda p: (0, base + p))

    return call(
        attend_kernel,
        (pairs,),
        [
            column(0),
            column(pairs),
            column(2 * pairs),
            pl.BlockSpec((1, 2, 2 * length), lambda p: (p, 0, 0)),
            whole((length, 1)),
        ],
        [column(0), pl.BlockSpec((2, length, length), lambda p: (p, 0, 0))],
        [shaped((length, width), BF16), shaped((head_count, length, length), BF16)],
        flops=8 * head_count * length * length * size,
    )(qkv, qkv, qkv, lines, fill)


def attend_back_kernel(
    q_ref, k_ref, v_ref, grad_ref, probs_ref, dq_ref, dk_ref, dv_ref, line_ref
):
    length, pair = q_ref.shape
    size = pair // 2
    queries = q_ref[...]
    keys_t = k_ref[...].T
    values = v_ref[...]
    grads = grad_ref[...]
    blocks = length // KB
    dq_heads, dk_heads, dv_heads = [], [], []
    for a in range(2):
        own = jnp.where(head_lanes(grads.shape, a, size), grads, jnp.zeros_like(grads))
        dq_parts = []
        dk = dv = None
        near = {}
        for qb in range(0, length, QB):
            probs = probs_ref[a, :, qb : qb + QB]
            probs_wide = probs.astype(F32)
            pulled = nt(values, own[qb : qb + QB])
            dots = jnp.sum(probs_wide * pulled, axis=0, keepdims=True)
            grad_scores = (probs_wide * (pulled - dots)).astype(BF16)
            dq_parts.append(nn(keys_t[a * size : (a + 1) * size], grad_scores))
            dk_part = nn(grad_scores, queries[qb : qb + QB])
            dv_part = nn(probs, grads[qb : qb + QB])
            dk = dk_part if dk is None else dk + dk_part
            dv = dv_part if dv is None else dv + dv_part
            wide = grad_scores.astype(F32)
            for i in range(blocks):
                for j in range(QB // KB):
                    gap = i - (qb // KB + j)
                    gap = max(-2, min(2, gap))
                    piece = wide[i * KB : (i + 1) * KB, j * KB : (j + 1) * KB]
                    near[gap] = piece if gap not in near else near[gap] + piece
        dq_heads.append(jnp.concatenate(dq_parts, axis=1))
        dk_heads.append(dk)
        dv_heads.append(dv)
        fold = jnp.concatenate([near[1], near[0], near[-1], jnp.zeros_like(near[0])], axis=1)
        rows = KB
        while rows > 8:
            rows //= 2
            fold = fold[:rows] + pltpu.roll(fold[rows : 2 * rows], 4 * KB - rows, 1)
        line_ref[0, a, :, 0 : 4 * KB] = fold
        far = jnp.concatenate([near[2], near[-2]], axis=1)
        line_ref[0, a, :, 4 * KB : 6 * KB] = jnp.sum(far.reshape(KB // 8, 8, 2 * KB), axis=0)
    first = head_lanes(queries.shape, 0, size)
    dq_ref[...] = jnp.concatenate(dq_heads, axis=0).T.astype(BF16)
    dk_ref[...] = jnp.where(first, dk_heads[0], dk_heads[1]).astype(BF16)
    dv_ref[...] = jnp.where(first, dv_heads[0], dv_heads[1]).astype(BF16)


def attend_back(qkv, grad_mixed, probs):
    head_count, length, _ = probs.shape
    width = grad_mixed.shape[1]
    pairs = head_count // 2
    size = width // pairs

    def column(base):
        return pl.BlockSpec((length, size), lambda p: (0, base + p))

    grad_shape = shaped((length, width), BF16)
    return call(
        attend_back_kernel,
        (pairs,),
        [
            column(0),
            column(pairs),
            column(2 * pairs),
            column(0),
            pl.BlockSpec((2, length, length), lambda p: (p, 0, 0)),
        ],
        [
            column(0),
            column(0),
            column(0),
            pl.BlockSpec((1, 2, 8, 6 * KB), lambda p: (p, 0, 0, 0)),
        ],
        [grad_shape, grad_shape, grad_shape, shaped((pairs, 2, 8, 6 * KB), F32)],
        flops=12 * head_count * length * length * size,
    )(qkv, qkv, qkv, grad_mixed, probs)


def line_one_hot(bucket_total):
    column = np.arange(4 * KB)
    rows = []
    for s in range(8):
        place = (column - s) % (4 * KB)
        offset = np.where(place <= 3 * KB, KB - place, 5 * KB - place)
        rows.append(np.concatenate([offset, np.full(KB, 3 * KB), np.full(KB, -3 * KB)]))
    return one_hot_rows(np.concatenate(rows), bucket_total)


def output_weight_of(place_ref, own_ref, other_ref, use):
    @pl.when(place_ref[2] == 0)
    def _():
        use(own_ref)

    @pl.when(place_ref[2] == 1)
    def _():
        use(other_ref)


def residual_kernel(
    place_ref, tokens_ref, mixed_ref, own_ref, other_ref, gain_ref, residual_ref, normed_ref
):
    def use(weight_ref):
        residual_ref[...] = tokens_ref[...].astype(F32) + nn(mixed_ref[...], weight_ref[...])

    output_weight_of(place_ref, own_ref, other_ref, use)
    residual = residual_ref[...]
    normed_ref[...] = (residual * norm_scale(residual) * gain_ref[...]).astype(BF16)


def residual_step(place, tokens, mixed, own, other, gain):
    length, width = tokens.shape

    def full(*shape):
        return pl.BlockSpec(shape, lambda j, place_ref: (0,) * len(shape))

    table = full(length, width)
    weight = pl.BlockSpec((width, width), lambda j, place_ref: (0, 1))
    return pl.pallas_call(
        residual_kernel,
        grid_spec=pltpu.PrefetchScalarGridSpec(
            num_scalar_prefetch=1,
            grid=(1,),
            in_specs=[table, table, weight, weight, full(1, width)],
            out_specs=[table, table],
        ),
        out_shape=[shaped((length, width), F32), shaped((length, width), BF16)],
        compiler_params=pltpu.CompilerParams(vmem_limit_bytes=56 * MIB),
        cost_estimate=cost_of(
            flops=2 * length * width * width, bytes_accessed=8 * MIB, transcendentals=0
        ),
    )(place, tokens, mixed, own, other, gain)


DEEP = 4


def blocks_of(place_ref, read_a, read_b, write):
    wide = place_ref[0]
    for dx in range(2):
        for dy in range(2):
            for k in range(DEEP):
                to_wide, to_narrow = wide ^ (2 * k + dx), place_ref[1] ^ dy
                write(0, dx, dy, k, read_a(to_wide, to_narrow))
                write(1, dy, dx, k, read_b(to_wide, to_narrow))


def write_mine(refs):
    def write(which, part, row, k, value):
        refs[2 * which + part][row, k] = value

    return write


def write_other(ref):
    def write(which, part, row, k, value):
        ref[which, part, row, k] = value

    return write


FEED_STEPS = 2


def feed_kernel(last, *refs):
    place_ref, normed_ref, grad_ref, base_ref, expand_ref, contract_ref = refs[:6]
    refs = refs[6:]
    if last:
        pulled_in_ref, residual_hbm, gain_ref, own_hbm, other_hbm = refs[:5]
        out_ref, grad_residual_ref, grad_low_ref, grad_mixed_ref, gain_grad_ref = refs[5:10]
        mine = refs[10:14]
        refs = refs[14:]
        residual_ref, weight_ref = refs[-2:]
        refs = refs[:-2]
    else:
        out_ref, pulled_out_ref, both_ref = refs[:3]
        refs = refs[3:]
    total_ref, pulled_ref, turned_ref, expand_grad_ref, contract_grad_ref, in_sems, out_sems = refs
    step = pl.program_id(0)
    wide, narrow, core = place_ref[0], place_ref[1], place_ref[2]
    width = normed_ref.shape[1]

    def base_copy():
        return pltpu.make_async_copy(base_ref, total_ref, in_sems.at[0])

    def pulled_copy():
        return pltpu.make_async_copy(pulled_in_ref, pulled_ref, in_sems.at[1])

    def residual_copy():
        return pltpu.make_async_copy(residual_hbm, residual_ref, in_sems.at[2])

    def weight_copy(hbm):
        source = hbm.at[:, pl.ds(width, width)]
        return pltpu.make_async_copy(source, weight_ref, in_sems.at[3])

    def grad_copies(j):
        rows = expand_grad_ref.shape[1] // (2 * DEEP)

        def target(which, part, row, k):
            if last:
                return mine[2 * which + part].at[row, k]
            return both_ref.at[which, part, row, k]

        copies = []

        def copy(source, place):
            sem = out_sems.at[j * 4 * DEEP + len(copies)]
            copies.append(pltpu.make_async_copy(source, place, sem))

        for dx in range(2):
            for k in range(DEEP):
                start = pl.multiple_of((wide ^ (2 * k + dx)) * rows, 16)
                copy(expand_grad_ref.at[j, pl.ds(start, rows), :], target(0, dx, narrow ^ j, k))
        for dy in range(2):
            for i in range(DEEP):
                to_wide = DEEP * j + i
                start = pl.multiple_of((to_wide * 2 + (narrow ^ dy)) * rows, 16)
                apart = wide ^ to_wide
                copy(
                    contract_grad_ref.at[pl.ds(start, rows), :],
                    target(1, dy, apart & 1, apart >> 1),
                )
        return copies

    @pl.when(step == 0)
    def _():
        base_copy().start()
        if last:
            pulled_copy().start()
            residual_copy().start()

            @pl.when(core == 0)
            def _():
                weight_copy(own_hbm).start()

            @pl.when(core == 1)
            def _():
                weight_copy(other_hbm).start()

        turned_ref[...] = normed_ref[...].T

    expand = expand_ref[0]
    contract = contract_ref[0]
    grad_block = grad_ref[...]
    pre = nn(normed_ref[...], expand)
    grad_hidden = nt(grad_block, contract)
    scale = np.float32(np.sqrt(2.0 / np.pi))
    square = pre * pre
    bent = jnp.tanh(pre * (scale + (scale * np.float32(0.044715)) * square))
    half = 0.5 + 0.5 * bent
    hidden = (pre * half).astype(BF16)
    slope = half + (0.5 * pre) * (1.0 - bent * bent) * (
        scale + (scale * np.float32(3 * 0.044715)) * square
    )
    grad_pre = (grad_hidden * slope).astype(BF16)
    made = nn(hidden, contract)
    pulled = nt(grad_pre, expand)
    block = expand.shape[1]
    contract_grad_ref[pl.ds(pl.multiple_of(step * block, block), block), :] = tn(
        hidden, grad_block
    ).astype(BF16)
    expand_grad_ref[step] = nn(turned_ref[...], grad_pre).astype(BF16)
    for j in range(FEED_STEPS):

        @pl.when(step == j)
        def _(j=j):
            for copy in grad_copies(j):
                copy.start()

    @pl.when(step == 0)
    def _():
        base_copy().wait()
        total_ref[...] += made
        if last:
            pulled_copy().wait()
            pulled_ref[...] += pulled
        else:
            pulled_ref[...] = pulled

    @pl.when(step > 0)
    def _():
        total_ref[...] += made
        pulled_ref[...] += pulled

    @pl.when(step == pl.num_programs(0) - 1)
    def _():
        if last:
            residual_copy().wait()

            @pl.when(core == 0)
            def _():
                weight_copy(own_hbm).wait()

            @pl.when(core == 1)
            def _():
                weight_copy(other_hbm).wait()

            out_ref[...] = total_ref[...].astype(BF16)
            grad_values, grad_gain = norm_backward(
                residual_ref[...], gain_ref[...], pulled_ref[...]
            )
            grad_residual = grad_block.astype(F32) + grad_values
            grad_residual_ref[...] = grad_residual
            grad_low_ref[...] = grad_residual.astype(BF16)
            gain_grad_ref[...] = grad_gain
            grad_mixed_ref[...] = nt(grad_low_ref[...], weight_ref[...]).astype(BF16)
        else:
            out_ref[...] = total_ref[...]
            pulled_out_ref[...] = pulled_ref[...]
        for j in range(FEED_STEPS):
            for copy in grad_copies(j):
                copy.wait()


def feed_half(last, place, normed, grad_block, base, weights, more=()):
    length, width = normed.shape
    half = weights.shape[1]
    block = half // FEED_STEPS
    rows = width // (2 * DEEP)

    def full(*shape):
        return pl.BlockSpec(shape, lambda j, place_ref: (0,) * len(shape))

    table = full(length, width)
    anywhere = pl.BlockSpec(memory_space=pl.ANY)
    in_specs = [
        table,
        table,
        anywhere,
        pl.BlockSpec((1, width, block), lambda j, place_ref: (0, j, 0)),
        pl.BlockSpec((1, block, width), lambda j, place_ref: (1, j, 0)),
    ]
    grad_dims = (2, DEEP, rows, block)
    if last:
        in_specs += [anywhere, anywhere, full(1, width), anywhere, anywhere]
        out_specs = [table, table, table, table, full(1, width)] + [anywhere] * 4
        out_shape = [
            shaped((length, width), BF16),
            shaped((length, width), F32),
            shaped((length, width), BF16),
            shaped((length, width), BF16),
            shaped((1, width), F32),
        ] + [shaped(grad_dims, BF16)] * 4
    else:
        out_specs = [table, table, anywhere]
        out_shape = [
            shaped((length, width), F32),
            shaped((length, width), F32),
            shaped((2, 2) + grad_dims, BF16),
        ]
    extra = []
    if last:
        extra = [pltpu.VMEM((length, width), F32), pltpu.VMEM((width, width), BF16)]
    return pl.pallas_call(
        functools.partial(feed_kernel, last),
        grid_spec=pltpu.PrefetchScalarGridSpec(
            num_scalar_prefetch=1,
            grid=(FEED_STEPS,),
            in_specs=in_specs,
            out_specs=out_specs,
            scratch_shapes=[
                pltpu.VMEM((length, width), F32),
                pltpu.VMEM((length, width), F32),
                pltpu.VMEM((width, length), BF16),
                pltpu.VMEM((FEED_STEPS, width, block), BF16),
                pltpu.VMEM((half, width), BF16),
                pltpu.SemaphoreType.DMA((4,)),
                pltpu.SemaphoreType.DMA((FEED_STEPS * 4 * DEEP,)),
            ]
            + extra,
        ),
        out_shape=out_shape,
        compiler_params=pltpu.CompilerParams(vmem_limit_bytes=56 * MIB),
        cost_estimate=cost_of(
            flops=6 * length * width * half * 2, bytes_accessed=8 * MIB, transcendentals=0
        ),
    )(place, normed, grad_block, base, weights, weights, *more)


def project_grad_kernel(place_ref, *refs):
    normed_ref, dq_ref, dk_ref, dv_ref, mixed_ref, grad_ref = refs[:6]
    mine = refs[6:10]
    other_ref, turned_ref, grads_ref = refs[10:]
    step = pl.program_id(0)
    width = dq_ref.shape[1]
    rows = width // (4 * DEEP)

    @pl.when(step == 0)
    def _():
        turned_ref[...] = normed_ref[...].T
        grads_ref[0] = nn(turned_ref[...], dq_ref[...]).astype(BF16)

    @pl.when(step == 1)
    def _():
        grads_ref[1] = nn(turned_ref[...], dk_ref[...]).astype(BF16)

    @pl.when(step == 2)
    def _():
        grads_ref[2] = nn(turned_ref[...], dv_ref[...]).astype(BF16)

    @pl.when(step == 3)
    def _():
        grads_ref[3] = tn(mixed_ref[...], grad_ref[...]).astype(BF16)

        def reader(which, core):
            def read(wide, narrow):
                start = pl.multiple_of((wide * 2 + core) * rows, 16)
                return grads_ref[2 * narrow + which, pl.ds(start, rows), :]

            return read

        core = place_ref[2]
        blocks_of(place_ref, reader(0, 1 - core), reader(1, 1 - core), write_other(other_ref))
        blocks_of(place_ref, reader(0, core), reader(1, core), write_mine(mine))


def project_grad(place, normed, dq, dk, dv, mixed, grad):
    length, width = normed.shape
    rows = width // (4 * DEEP)

    def full(*shape):
        return pl.BlockSpec(shape, lambda j, place_ref: (0,) * len(shape))

    dims = (2, DEEP, rows, width)
    return pl.pallas_call(
        project_grad_kernel,
        grid_spec=pltpu.PrefetchScalarGridSpec(
            num_scalar_prefetch=1,
            grid=(4,),
            in_specs=[full(length, width)] * 6,
            out_specs=[full(*dims)] * 4 + [full(2, 2, *dims)],
            scratch_shapes=[
                pltpu.VMEM((width, length), BF16),
                pltpu.VMEM((4, width, width), BF16),
            ],
        ),
        out_shape=[shaped(dims, BF16)] * 4 + [shaped((2, 2) + dims, BF16)],
        compiler_params=pltpu.CompilerParams(vmem_limit_bytes=56 * MIB),
        cost_estimate=cost_of(
            flops=8 * length * width * width, bytes_accessed=8 * MIB, transcendentals=0
        ),
    )(place, normed, dq, dk, dv, mixed, grad)


HALF = DEEP // 2
SOURCES = [
    (range(DEEP), 0, 0),
    (range(DEEP), 1, 0),
    (range(DEEP), 0, 1),
    (range(HALF), 1, 1),
    (range(HALF, DEEP), 1, 1),
]
EARLY, LATE = (0, 2), (1, 3)
FEED_SOURCES = [
    source
    for some, far in ((EARLY, [EARLY]), (LATE, [LATE[:1], LATE[1:]]))
    for source in [(some, 0, 0), (some, 1, 0), (some, 0, 1)] + [(part, 1, 1) for part in far]
]


def assemble_kernel(place_ref, *refs):
    out_ref = refs[-1]
    for ref, (deep, dx, dy) in zip(refs, SOURCES):
        rows = ref.shape[1]
        for i in range(ref.shape[0]):
            start = (place_ref[0] ^ (2 * deep[i] + dx)) * 2 + (place_ref[1] ^ dy)
            out_ref[pl.ds(pl.multiple_of(start * rows, 16), rows), :] = ref[i]


def assemble(place, pieces):
    rows, columns = pieces[0].shape[1:]
    dims = (4 * DEEP * rows, columns)
    return pl.pallas_call(
        assemble_kernel,
        grid_spec=pltpu.PrefetchScalarGridSpec(
            num_scalar_prefetch=1,
            grid=(1,),
            in_specs=[
                pl.BlockSpec(piece.shape, lambda j, place_ref: (0, 0, 0)) for piece in pieces
            ],
            out_specs=pl.BlockSpec(dims, lambda j, place_ref: (0, 0)),
        ),
        out_shape=shaped(dims, BF16),
        compiler_params=pltpu.CompilerParams(vmem_limit_bytes=56 * MIB),
        cost_estimate=cost_of(flops=0, bytes_accessed=8 * MIB, transcendentals=0),
    )(place, *pieces)


def assemble_feed_kernel(place_ref, *refs):
    out_ref = refs[-1]
    for ref, (deep, dx, dy) in zip(refs, FEED_SOURCES):
        rows, columns = ref.shape[2:]
        half = rows // FEED_STEPS
        for i in range(ref.shape[0]):
            start = (place_ref[0] ^ (2 * deep[i] + dx)) * 2 + (place_ref[1] ^ dy)
            for j in range(FEED_STEPS):
                base = pl.multiple_of(j * columns + start * half, 16)
                out_ref[0, pl.ds(base, half), :] = ref[i, 0, j * half : (j + 1) * half]
            out_ref[1, pl.ds(pl.multiple_of(start * rows, 16), rows), :] = ref[i, 1]


def assemble_feed(place, pieces):
    rows, columns = pieces[0].shape[2:]
    dims = (2, 4 * DEEP * rows, columns)
    return pl.pallas_call(
        assemble_feed_kernel,
        grid_spec=pltpu.PrefetchScalarGridSpec(
            num_scalar_prefetch=1,
            grid=(1,),
            in_specs=[
                pl.BlockSpec(piece.shape, lambda j, place_ref: (0, 0, 0, 0)) for piece in pieces
            ],
            out_specs=pl.BlockSpec(dims, lambda j, place_ref: (0, 0, 0)),
        ),
        out_shape=shaped(dims, BF16),
        compiler_params=pltpu.CompilerParams(vmem_limit_bytes=56 * MIB),
        cost_estimate=cost_of(flops=0, bytes_accessed=8 * MIB, transcendentals=0),
    )(place, *pieces)


def finish_feed_kernel(place_ref, *refs):
    parts, (expand_ref, contract_ref) = refs[:-2], refs[-2:]
    rows, columns = parts[0].shape[2:]
    unit = columns // DEEP
    for ref, dy, dc in [(parts[dc], dy, dc) for dc in range(2) for dy in range(2)]:
        y, c = place_ref[1] ^ dy, place_ref[2] ^ dc
        start = pl.multiple_of((c * 2 + y) * rows, 8)
        contract_ref[pl.ds(start, rows), :] = ref[dy, 1].astype(F32)
        for to_y in range(2):
            for to_c in range(2):

                @pl.when((y == to_y) & (c == to_c))
                def _(ref=ref, dy=dy, to_y=to_y, to_c=to_c):
                    value = ref[dy, 0].astype(F32)
                    for i in range(DEEP):
                        base = ((to_y * DEEP + i) * 2 + to_c) * unit
                        expand_ref[:, base : base + unit] = value[:, i * unit : (i + 1) * unit]


def finish_feed(place, parts):
    rows, columns = parts[0].shape[2:]
    dims = [(rows, 4 * columns), (4 * rows, columns)]
    return pl.pallas_call(
        finish_feed_kernel,
        grid_spec=pltpu.PrefetchScalarGridSpec(
            num_scalar_prefetch=1,
            grid=(1,),
            in_specs=[pl.BlockSpec(part.shape, lambda j, place_ref: (0, 0, 0, 0)) for part in parts],
            out_specs=[pl.BlockSpec(d, lambda j, place_ref: (0, 0)) for d in dims],
        ),
        out_shape=[shaped(d, F32) for d in dims],
        compiler_params=pltpu.CompilerParams(vmem_limit_bytes=56 * MIB),
        cost_estimate=cost_of(flops=0, bytes_accessed=4 * MIB, transcendentals=0),
    )(place, *parts)


def finish_square_kernel(place_ref, *refs):
    parts, outs = refs[:-4], refs[-4:]
    rows = parts[0].shape[2]
    for ref, dy, dc in [(parts[dc], dy, dc) for dc in range(2) for dy in range(2)]:
        y, c = place_ref[1] ^ dy, place_ref[2] ^ dc
        for to_y in range(2):

            @pl.when(y == to_y)
            def _(ref=ref, dy=dy, to_y=to_y, c=c):
                for i in range(2):
                    start = pl.multiple_of(c * rows, 8)
                    outs[2 * to_y + i][pl.ds(start, rows), :] = ref[dy, i].astype(F32)


def finish_square(place, parts):
    rows, columns = parts[0].shape[2:]
    dims = (2 * rows, columns)
    return pl.pallas_call(
        finish_square_kernel,
        grid_spec=pltpu.PrefetchScalarGridSpec(
            num_scalar_prefetch=1,
            grid=(1,),
            in_specs=[pl.BlockSpec(part.shape, lambda j, place_ref: (0, 0, 0, 0)) for part in parts],
            out_specs=[pl.BlockSpec(dims, lambda j, place_ref: (0, 0))] * 4,
        ),
        out_shape=[shaped(dims, F32)] * 4,
        compiler_params=pltpu.CompilerParams(vmem_limit_bytes=56 * MIB),
        cost_estimate=cost_of(flops=0, bytes_accessed=4 * MIB, transcendentals=0),
    )(place, *parts)


def tokens_back_kernel(
    place_ref,
    dq_ref,
    dk_ref,
    dv_ref,
    own_ref,
    other_ref,
    tokens_ref,
    gain_ref,
    residual_ref,
    out_ref,
    gain_grad_ref,
    pulled_ref,
):
    width = dq_ref.shape[1]

    def pull(first_ref, second_ref):
        pulled = nt(dq_ref[...], first_ref[:, 0:width])
        pulled += nt(dk_ref[...], first_ref[:, width : 2 * width])
        pulled += nt(dv_ref[...], second_ref[:, 0:width])
        pulled_ref[...] = pulled

    @pl.when(place_ref[2] == 1)
    def _():
        pull(own_ref, other_ref)

    @pl.when(place_ref[2] == 0)
    def _():
        pull(other_ref, own_ref)

    grad_values, grad_gain = norm_backward(
        tokens_ref[...].astype(F32), gain_ref[...], pulled_ref[...]
    )
    out_ref[...] = residual_ref[...] + grad_values
    gain_grad_ref[...] = grad_gain


def tokens_back(place, dq, dk, dv, own, other, tokens, gain, grad_residual):
    length, width = tokens.shape

    def full(*shape):
        return pl.BlockSpec(shape, lambda j, place_ref: (0,) * len(shape))

    table = full(length, width)
    return pl.pallas_call(
        tokens_back_kernel,
        grid_spec=pltpu.PrefetchScalarGridSpec(
            num_scalar_prefetch=1,
            grid=(1,),
            in_specs=[table, table, table]
            + [full(width, 2 * width)] * 2
            + [table, full(1, width), table],
            out_specs=[table, full(1, width)],
            scratch_shapes=[pltpu.VMEM((length, width), F32)],
        ),
        out_shape=[shaped((length, width), F32), shaped((1, width), F32)],
        compiler_params=pltpu.CompilerParams(vmem_limit_bytes=56 * MIB),
        cost_estimate=cost_of(
            flops=6 * length * width * width, bytes_accessed=8 * MIB, transcendentals=0
        ),
    )(place, dq, dk, dv, own, other, tokens, gain, grad_residual)


def exchange(value, dz=0, dx=0, dy=0, dc=0):
    flip = ((2 * dz + dx) * 2 + dy) * 2 + dc
    total = 8 * DEEP
    return lax.ppermute(value, ("wide", "narrow"), [(i, i ^ flip) for i in range(total)])


def after(value, *done):
    return lax.optimization_barrier((value,) + done)[0]


def together(*values):
    return lax.optimization_barrier(values)


def gather_stage_z(piece):
    return jnp.stack([piece] + [exchange(piece, dz=k) for k in range(1, DEEP)])


def gather_stage_xy(near):
    return exchange(near, dx=1), exchange(near, dy=1)


def gather_stage_far(over_x, over_y):
    half = over_x.shape[0] // 2
    return exchange(over_y[:half], dx=1), exchange(over_x[half:], dy=1)


def low(value):
    return value.astype(BF16)


def add(*values):
    return sum(value.astype(F32) for value in values)


def reduce_first_out(mine, other):
    return low(add(mine[1], other[0, 1])), low(add(mine[3], other[1, 1]))


def reduce_first(outs):
    return exchange(outs[0], dx=1), exchange(outs[1], dy=1)


def reduce_second_out(mine, other, first):
    return tuple(low(add(mine[2 * i][1], other[i, 0, 1], first[i][1])) for i in range(2))


def reduce_second(outs):
    return exchange(outs[0], dy=1), exchange(outs[1], dx=1)


def reduce_level(mine, other, first, second, k):
    return jnp.stack(
        [add(mine[2 * i][0, k], other[i, 0, 0, k], first[i][0, k], second[i][k]) for i in range(2)]
    )


def reduce_deep_out(*parts):
    return tuple(low(reduce_level(*parts, k)) for k in range(1, DEEP))


def reduce_deep(outs):
    return tuple(exchange(out, dz=k + 1) for k, out in enumerate(outs))


def reduce_last(parts, deep):
    return low(reduce_level(*parts, 0) + add(*deep))


def spread_y(part):
    return exchange(part, dy=1)


def spread_core(part, other_y):
    both = jnp.stack([part, other_y])
    return both, exchange(both, dc=1)


def on_device(
    tokens,
    query_weight,
    key_weight,
    value_weight,
    output_weight,
    expand_weight,
    contract_weight,
    attention_gain,
    feedforward_gain,
    bias_table,
    query_length,
    passage_length,
    pair_order,
    regrouped_grad,
):
    row_count, length, width = tokens.shape
    bucket_count, head_count = bias_table.shape
    wide_index = lax.axis_index("wide")
    wide_count = lax.axis_size("wide")
    narrow_index = lax.axis_index("narrow")
    narrow_count = lax.axis_size("narrow")
    by_hand = wide_count == 2 * DEEP and narrow_count == 4
    hidden_count = expand_weight.shape[1]
    part_rows = hidden_count // (4 * DEEP)

    square_weights = (query_weight, key_weight, value_weight, output_weight)
    if by_hand:
        narrow_y, core = narrow_index // 2, narrow_index % 2
    else:
        wide_index = narrow_y = core = jnp.int32(0)
    place = jnp.stack([wide_index, narrow_y, core]).astype(jnp.int32)

    group_rows = regrouped_grad.shape[0]
    chosen = lax.dynamic_slice_in_dim(pair_order, narrow_index * group_rows, group_rows)
    local_rows = chosen // (row_count * narrow_count) * row_count + chosen % row_count
    arranged = jnp.zeros_like(regrouped_grad).at[local_rows].set(regrouped_grad)

    spot = np.arange(2 * length)
    offsets = np.where(spot <= 2 * length - KB, length - KB - spot, 3 * length - KB - spot)
    band_hot = jnp.asarray(one_hot_rows(np.clip(offsets, 1 - length, length - 1), bucket_count))
    lines = jnp.dot(bias_table.T, band_hot.T, precision=lax.Precision.HIGHEST)
    lines = lines.reshape(head_count // 2, 2, 2 * length)
    positions = jnp.arange(length, dtype=jnp.int32)
    fill = jnp.where(positions < query_length[0] + passage_length[0], 0.0, negative)
    fill = fill.astype(F32)[:, None]

    if by_hand:
        half_rows = query_weight.shape[0] // 2
        own_half = 1 - core
        first = jnp.concatenate(square_weights[:2], axis=1)
        second = jnp.concatenate(square_weights[2:], axis=1)
        square_piece = lax.dynamic_slice_in_dim(
            jnp.where(core == 1, first, second), narrow_y * half_rows, half_rows
        )
        expand_piece = lax.dynamic_slice_in_dim(
            lax.dynamic_index_in_dim(
                expand_weight.reshape(-1, 2 * DEEP, 2, part_rows), own_half, 2, False
            ).reshape(-1, hidden_count // 2),
            narrow_y * half_rows,
            half_rows,
        )
        contract_rows = contract_weight.shape[0] // 4
        contract_piece = lax.dynamic_slice_in_dim(
            contract_weight, (own_half * 2 + narrow_y) * contract_rows, contract_rows
        )
        feed_piece = jnp.stack(
            [
                jnp.concatenate(
                    [expand_piece[:, j * width : (j + 1) * width] for j in range(FEED_STEPS)]
                ),
                contract_piece,
            ]
        )
        square_near = gather_stage_z(square_piece)
        square_near, arranged, lines, fill, feed_piece = together(
            square_near, arranged, lines, fill, feed_piece
        )
        square_xy = gather_stage_xy(square_near)
        feed_two = exchange(feed_piece, dz=2)
        feed_early = jnp.stack([feed_piece, feed_two])
        square_xy, feed_early, feed_piece = together(square_xy, feed_early, feed_piece)
        square_far = gather_stage_far(*square_xy)
        feed_one = exchange(feed_piece, dz=1)
        square_far, feed_one = together(square_far, feed_one)
        square_own = assemble(place, [square_near, *square_xy, *square_far])
        square_own, feed_early, feed_piece = together(square_own, feed_early, feed_piece)
        square_other = exchange(square_own, dc=1)
        feed_early_xy = gather_stage_xy(feed_early)
        feed_three = exchange(feed_piece, dz=3)
    else:

        def gathered(weight):
            return lax.all_gather(weight, "wide", axis=0, tiled=True)

        square_other = gathered(jnp.concatenate(square_weights[:2], axis=1))
        square_own = gathered(jnp.concatenate(square_weights[2:], axis=1))
        full_expand = gathered(expand_weight).reshape(width, 2 * DEEP, 2, part_rows)
        full_contract = gathered(contract_weight).reshape(2 * DEEP, 2, part_rows, width)
        feed_other, feed_own = (
            jnp.stack(
                [
                    full_expand[:, :, i]
                    .reshape(width, FEED_STEPS, -1)
                    .transpose(1, 0, 2)
                    .reshape(-1, width),
                    full_contract[:, i].reshape(-1, width),
                ]
            )
            for i in range(2)
        )

    inputs = tokens.reshape(length, width)
    gain_one = attention_gain[None]
    gain_two = feedforward_gain[None]
    attention_input, qkv = project(place, inputs, gain_one, square_own, square_other)
    if by_hand:
        arranged = after(arranged, qkv)
    grad_block = lax.all_to_all(arranged, "wide", split_axis=0, concat_axis=0, tiled=True).reshape(
        length, width
    )
    if by_hand:
        qkv, feed_early_xy, feed_three = together(qkv, feed_early_xy, feed_three)
        feed_late = jnp.stack([feed_one, feed_three])
        qkv, feed_late = together(qkv, feed_late)
        feed_late_xy = gather_stage_xy(feed_late)
        feed_early_far = [exchange(feed_early_xy[0], dy=1)]
    mixed, probs = attend(qkv, lines, fill, head_count)
    if by_hand:
        mixed, grad_block, feed_late_xy, feed_early_far = together(
            mixed, grad_block, feed_late_xy, feed_early_far
        )
        feed_late_far = gather_stage_far(*feed_late_xy)
    residual, expand_input = residual_step(
        place, inputs, mixed, square_own, square_other, gain_two
    )
    if by_hand:
        feed_own = assemble_feed(
            place,
            [feed_early, *feed_early_xy, *feed_early_far]
            + [feed_late, *feed_late_xy, *feed_late_far],
        )
        feed_other = exchange(feed_own, dc=1)
    partial_out, partial_pulled, feed_sent = feed_half(
        False, place, expand_input, grad_block, residual, feed_own
    )
    if by_hand:
        feed_got = exchange(feed_sent, dc=1)
    results = feed_half(
        True,
        place,
        expand_input,
        grad_block,
        partial_out,
        feed_other,
        (partial_pulled, residual, gain_two, square_own, square_other),
    )
    block_output, grad_residual, grad_low, grad_mixed, gain_two_grad = results[:5]
    feed_mine = results[5:9]
    if by_hand:
        feed_got, grad_mixed, block_output = together(feed_got, grad_mixed, block_output)
        outs = reduce_first_out(feed_mine, feed_got)
        grad_mixed, *outs = together(grad_mixed, *outs)
        feed_first = reduce_first(outs)
    dq, dk, dv, line_grads = attend_back(qkv, grad_mixed, probs)
    results = project_grad(place, attention_input, dq, dk, dv, mixed, grad_low)
    square_mine, square_sent = results[:4], results[4]
    if by_hand:
        square_sent, *feed_first = together(square_sent, *feed_first)
        square_got = exchange(square_sent, dc=1)
        outs = reduce_second_out(feed_mine, feed_got, feed_first)
        dq, *outs = together(dq, *outs)
        feed_second = reduce_second(outs)
    tokens_grad, gain_one_grad = tokens_back(
        place, dq, dk, dv, square_own, square_other, inputs, gain_one, grad_residual
    )
    if by_hand:
        block_output, line_grads, gain_one_grad = together(
            block_output, line_grads, gain_one_grad
        )
    received = lax.all_to_all(
        block_output.reshape(-1, regrouped_grad.shape[1], width),
        "wide",
        split_axis=0,
        concat_axis=0,
        tiled=True,
    )
    table_grad = jnp.dot(
        jnp.asarray(line_one_hot(bucket_count).T),
        line_grads.reshape(head_count, -1).T,
        precision=lax.Precision.HIGHEST,
    )
    small = jnp.concatenate([gain_one_grad[0], gain_two_grad[0], table_grad.reshape(-1)])
    small_count = small.shape[0]

    if not by_hand:
        regrouped = jnp.take(received, local_rows, axis=0)
    if by_hand:
        small = jnp.pad(small, (0, -small_count % 1024)).reshape(-1, 128)
        square_got, small, table_grad = together(square_got, small, table_grad)
        outs = reduce_first_out(square_mine, square_got)
        square_first = reduce_first(outs)
        feed_second = after(feed_second, *outs)
        feed_parts = (feed_mine, feed_got, feed_first, feed_second)
        outs = reduce_deep_out(*feed_parts)
        feed_deep = reduce_deep(outs)
        square_first, received = together(after(square_first, *outs), received)
        regrouped = jnp.take(received, local_rows, axis=0)
        small = jnp.broadcast_to(small[None], (8 * DEEP,) + small.shape)
        small = lax.all_to_all(small, ("wide", "narrow"), 0, 0, tiled=True)
        outs = reduce_second_out(square_mine, square_got, square_first)
        square_second = reduce_second(outs)
        feed_deep = after(feed_deep, *outs)
        square_parts = (square_mine, square_got, square_first, square_second)
        feed_deep, regrouped = together(feed_deep, regrouped)
        feed_part = reduce_last(feed_parts, feed_deep)
        feed_other_y = spread_y(feed_part)
        outs = reduce_deep_out(*square_parts)
        feed_other_y, outs, small = together(feed_other_y, outs, small)
        square_deep = reduce_deep(outs)
        feed_spread = spread_core(feed_part, feed_other_y)
        final_expand, final_contract = finish_feed(place, feed_spread)
        square_deep, small = together(after(square_deep, final_expand), small)
        square_part = reduce_last(square_parts, square_deep)
        finals = finish_square(place, spread_core(square_part, spread_y(square_part)))
        small = jnp.sum(small, axis=0).reshape(-1)
    else:

        def summed(grad):
            part = lax.psum_scatter(grad, "wide", scatter_dimension=0, tiled=True)
            return lax.psum(part, "narrow").astype(F32)

        def stacked(which, mine, other):
            kept = jnp.stack(mine[2 * which : 2 * which + 2])
            return jnp.stack([kept, other[which]])

        expand_all = stacked(0, feed_mine, feed_sent)
        expand_all = expand_all.reshape(expand_all.shape[:5] + (DEEP, part_rows))
        expand_all = expand_all.transpose(3, 1, 4, 2, 5, 0, 6)
        contract_all = stacked(1, feed_mine, feed_sent).transpose(3, 2, 0, 1, 4, 5)
        first = stacked(0, square_mine, square_sent)
        second = stacked(1, square_mine, square_sent).transpose(0, 2, 1, 3, 4, 5)
        square_all = jnp.stack([first, second]).transpose(4, 2, 1, 5, 3, 0, 6)
        final_contract = summed(contract_all.reshape(hidden_count, width))
        final_expand = summed(expand_all.reshape(width, hidden_count))
        final_square = summed(square_all.reshape(width, 4 * width))
        finals = [final_square[:, i * width : (i + 1) * width] for i in range(4)]
        small = lax.psum(small, ("wide", "narrow"))

    return (
        regrouped,
        tokens_grad.reshape(row_count, length, width),
        *finals,
        final_expand,
        final_contract,
        small[:width],
        small[width : 2 * width],
        small[2 * width : small_count].reshape(bucket_count, head_count),
    )


def solution(mesh):
    in_specs = (
        P(("wide", "narrow"), None, None),
        P("wide", None),
        P("wide", None),
        P("wide", None),
        P("wide", None),
        P("wide", None),
        P("wide", None),
        P(),
        P(),
        P(),
        P(("wide", "narrow")),
        P(("wide", "narrow")),
        P(),
        P("narrow", "wide", None),
    )
    out_specs = (
        P("narrow", "wide", None),
        P(("wide", "narrow"), None, None),
        P("wide", None),
        P("wide", None),
        P("wide", None),
        P("wide", None),
        P("wide", None),
        P("wide", None),
        P(),
        P(),
        P(),
    )
    return jax.shard_map(
        on_device, mesh=mesh, in_specs=in_specs, out_specs=out_specs, check_vma=False
    )
```

```python
import functools

import jax
import jax.numpy as jnp
import numpy as np
from jax import lax
from jax.experimental import pallas as pl
from jax.experimental.pallas import tpu as pltpu
from jax.sharding import PartitionSpec as P

MAX_DIST = 128
epsilon = 1e-06
negative = -1000000000.0
F32 = jnp.float32
BF16 = jnp.bfloat16
MIB = 1024 * 1024


def bucket_index(offset_values, bucket_total, max_reach):
    exact_part = bucket_total // 4
    bounds_table = np.ceil(
        exact_part * (max_reach / exact_part) ** (np.arange(1, exact_part) / exact_part) - 1e-06
    ).astype(np.int32)
    distance = np.abs(offset_values)
    passed = np.zeros_like(distance)
    for limit_value in bounds_table:
        passed = passed + (distance >= int(limit_value)).astype(np.int32)
    coarse = np.where(distance < exact_part, distance, exact_part + passed)
    return coarse + (offset_values > 0).astype(np.int32) * (bucket_total // 2)


def one_hot_rows(offset_values, bucket_total):
    ids = bucket_index(np.asarray(offset_values, np.int32), bucket_total, MAX_DIST)
    return (ids[:, None] == np.arange(bucket_total)[None, :]).astype(np.float32)


def nn(left, right):
    return lax.dot_general(left, right, (((1,), (0,)), ((), ())), preferred_element_type=F32)


def nt(left, right):
    return lax.dot_general(left, right, (((1,), (1,)), ((), ())), preferred_element_type=F32)


def tn(left, right):
    return lax.dot_general(left, right, (((0,), (0,)), ((), ())), preferred_element_type=F32)


def norm_scale(values):
    return lax.rsqrt(jnp.mean(values * values, axis=-1, keepdims=True) + epsilon)


def norm_backward(values, gain, grad):
    scale = norm_scale(values)
    scaled = grad * gain
    dots = jnp.mean(scaled * values, axis=-1, keepdims=True)
    grad_values = scale * scaled - values * (scale * scale * scale * dots)
    grad_gain = jnp.sum(grad * (values * scale), axis=0, keepdims=True)
    return grad_values, grad_gain


def whole(shape):
    return pl.BlockSpec(shape, lambda *_: (0,) * len(shape))


def cost_of(flops, bytes_accessed, transcendentals):
    return pl.CostEstimate(flops=10 * int(flops), bytes_accessed=bytes_accessed, transcendentals=0)


def call(kernel, grid, in_specs, out_specs, out_shape, scratch=(), flops=0, vmem=56):
    return pl.pallas_call(
        kernel,
        grid=grid,
        in_specs=in_specs,
        out_specs=out_specs,
        out_shape=out_shape,
        scratch_shapes=list(scratch),
        compiler_params=pltpu.CompilerParams(vmem_limit_bytes=vmem * MIB),
        cost_estimate=cost_of(flops=flops, bytes_accessed=8 * MIB, transcendentals=0),
    )


def shaped(shape, kind):
    return jax.ShapeDtypeStruct(shape, kind)


def project_kernel(place_ref, tokens_ref, gain_ref, own_ref, other_ref, normed_ref, qkv_ref):
    step = pl.program_id(0)
    own_half = 1 - place_ref[2]

    @pl.when(step == 0)
    def _():
        values = tokens_ref[...].astype(F32)
        normed_ref[...] = (values * norm_scale(values) * gain_ref[...]).astype(BF16)

    @pl.when((step < 2) & (own_half * 2 + step < 3))
    def _():
        qkv_ref[...] = nn(normed_ref[...], own_ref[...]).astype(BF16)

    @pl.when((step >= 2) & (step - own_half * 2 < 3))
    def _():
        qkv_ref[...] = nn(normed_ref[...], other_ref[...]).astype(BF16)


def project(place, tokens, gain, own, other):
    length, width = tokens.shape

    def column(j, place_ref):
        own_half = 1 - place_ref[2]
        return (0, jnp.where(j < 2, own_half * 2 + j, j - own_half * 2))

    def full(*shape):
        return pl.BlockSpec(shape, lambda j, place_ref: (0,) * len(shape))

    return pl.pallas_call(
        project_kernel,
        grid_spec=pltpu.PrefetchScalarGridSpec(
            num_scalar_prefetch=1,
            grid=(4,),
            in_specs=[
                full(length, width),
                full(1, width),
                pl.BlockSpec((width, width), lambda j, place_ref: (0, jnp.minimum(j, 1))),
                pl.BlockSpec((width, width), lambda j, place_ref: (0, jnp.maximum(j - 2, 0))),
            ],
            out_specs=[full(length, width), pl.BlockSpec((length, width), column)],
        ),
        out_shape=[shaped((length, width), BF16), shaped((length, 4 * width), BF16)],
        compiler_params=pltpu.CompilerParams(vmem_limit_bytes=56 * MIB),
        cost_estimate=cost_of(
            flops=6 * length * width * width, bytes_accessed=8 * MIB, transcendentals=0
        ),
    )(place, tokens, gain, own, other)


QB = 512
KB = 128


def head_lanes(shape, which, size):
    lanes = lax.broadcasted_iota(jnp.int32, shape, 1)
    return (lanes < size) == (which == 0)


def attend_kernel(q_ref, k_ref, v_ref, line_ref, fill_ref, mixed_ref, probs_ref):
    length, pair = q_ref.shape
    size = pair // 2
    queries = q_ref[...]
    keys = k_ref[...]
    values_t = v_ref[...].T
    fill = fill_ref[...]
    heads = []
    for a in range(2):
        own = jnp.where(head_lanes(queries.shape, a, size), queries, jnp.zeros_like(queries))
        line = jnp.broadcast_to(line_ref[0, a : a + 1, :], (KB, 2 * length))
        band = pltpu.roll(line, 0, 1, stride=1, stride_axis=0)
        parts = []
        for qb in range(0, length, QB):
            raw = nt(keys, own[qb : qb + QB])
            rows = []
            for kb in range(0, length, KB):
                start = length - KB - kb + qb
                rows.append(
                    raw[kb : kb + KB] + (band[:, start : start + QB] + fill[kb : kb + KB])
                )
            scores = jnp.concatenate(rows, axis=0)
            peak = jnp.max(scores, axis=0, keepdims=True)
            weights = jnp.exp(scores - peak)
            total = jnp.sum(weights, axis=0, keepdims=True)
            probs = (weights * (1.0 / total)).astype(BF16)
            probs_ref[a, :, qb : qb + QB] = probs
            parts.append(nn(values_t[a * size : (a + 1) * size], probs))
        heads.append(jnp.concatenate(parts, axis=1))
    mixed_ref[...] = jnp.concatenate(heads, axis=0).T.astype(BF16)


def attend(qkv, lines, fill, head_count):
    length = qkv.shape[0]
    width = qkv.shape[1] // 4
    pairs = head_count // 2
    size = width // pairs

    def column(base):
        return pl.BlockSpec((length, size), lambda p: (0, base + p))

    return call(
        attend_kernel,
        (pairs,),
        [
            column(0),
            column(pairs),
            column(2 * pairs),
            pl.BlockSpec((1, 2, 2 * length), lambda p: (p, 0, 0)),
            whole((length, 1)),
        ],
        [column(0), pl.BlockSpec((2, length, length), lambda p: (p, 0, 0))],
        [shaped((length, width), BF16), shaped((head_count, length, length), BF16)],
        flops=8 * head_count * length * length * size,
    )(qkv, qkv, qkv, lines, fill)


def attend_back_kernel(
    q_ref, k_ref, v_ref, grad_ref, probs_ref, dq_ref, dk_ref, dv_ref, line_ref
):
    length, pair = q_ref.shape
    size = pair // 2
    queries = q_ref[...]
    keys_t = k_ref[...].T
    values = v_ref[...]
    grads = grad_ref[...]
    blocks = length // KB
    dq_heads, dk_heads, dv_heads = [], [], []
    for a in range(2):
        own = jnp.where(head_lanes(grads.shape, a, size), grads, jnp.zeros_like(grads))
        dq_parts = []
        dk = dv = None
        near = {}
        for qb in range(0, length, QB):
            probs = probs_ref[a, :, qb : qb + QB]
            probs_wide = probs.astype(F32)
            pulled = nt(values, own[qb : qb + QB])
            dots = jnp.sum(probs_wide * pulled, axis=0, keepdims=True)
            grad_scores = (probs_wide * (pulled - dots)).astype(BF16)
            dq_parts.append(nn(keys_t[a * size : (a + 1) * size], grad_scores))
            dk_part = nn(grad_scores, queries[qb : qb + QB])
            dv_part = nn(probs, grads[qb : qb + QB])
            dk = dk_part if dk is None else dk + dk_part
            dv = dv_part if dv is None else dv + dv_part
            wide = grad_scores.astype(F32)
            for i in range(blocks):
                for j in range(QB // KB):
                    gap = i - (qb // KB + j)
                    gap = max(-2, min(2, gap))
                    piece = wide[i * KB : (i + 1) * KB, j * KB : (j + 1) * KB]
                    near[gap] = piece if gap not in near else near[gap] + piece
        dq_heads.append(jnp.concatenate(dq_parts, axis=1))
        dk_heads.append(dk)
        dv_heads.append(dv)
        fold = jnp.concatenate([near[1], near[0], near[-1], jnp.zeros_like(near[0])], axis=1)
        rows = KB
        while rows > 8:
            rows //= 2
            fold = fold[:rows] + pltpu.roll(fold[rows : 2 * rows], 4 * KB - rows, 1)
        line_ref[0, a, :, 0 : 4 * KB] = fold
        far = jnp.concatenate([near[2], near[-2]], axis=1)
        line_ref[0, a, :, 4 * KB : 6 * KB] = jnp.sum(far.reshape(KB // 8, 8, 2 * KB), axis=0)
    first = head_lanes(queries.shape, 0, size)
    dq_ref[...] = jnp.concatenate(dq_heads, axis=0).T.astype(BF16)
    dk_ref[...] = jnp.where(first, dk_heads[0], dk_heads[1]).astype(BF16)
    dv_ref[...] = jnp.where(first, dv_heads[0], dv_heads[1]).astype(BF16)


def attend_back(qkv, grad_mixed, probs):
    head_count, length, _ = probs.shape
    width = grad_mixed.shape[1]
    pairs = head_count // 2
    size = width // pairs

    def column(base):
        return pl.BlockSpec((length, size), lambda p: (0, base + p))

    grad_shape = shaped((length, width), BF16)
    return call(
        attend_back_kernel,
        (pairs,),
        [
            column(0),
            column(pairs),
            column(2 * pairs),
            column(0),
            pl.BlockSpec((2, length, length), lambda p: (p, 0, 0)),
        ],
        [
            column(0),
            column(0),
            column(0),
            pl.BlockSpec((1, 2, 8, 6 * KB), lambda p: (p, 0, 0, 0)),
        ],
        [grad_shape, grad_shape, grad_shape, shaped((pairs, 2, 8, 6 * KB), F32)],
        flops=12 * head_count * length * length * size,
    )(qkv, qkv, qkv, grad_mixed, probs)


def line_one_hot(bucket_total):
    column = np.arange(4 * KB)
    rows = []
    for s in range(8):
        place = (column - s) % (4 * KB)
        offset = np.where(place <= 3 * KB, KB - place, 5 * KB - place)
        rows.append(np.concatenate([offset, np.full(KB, 3 * KB), np.full(KB, -3 * KB)]))
    return one_hot_rows(np.concatenate(rows), bucket_total)


def output_weight_of(place_ref, own_ref, other_ref, use):
    @pl.when(place_ref[2] == 0)
    def _():
        use(own_ref)

    @pl.when(place_ref[2] == 1)
    def _():
        use(other_ref)


def residual_kernel(
    place_ref, tokens_ref, mixed_ref, own_ref, other_ref, gain_ref, residual_ref, normed_ref
):
    def use(weight_ref):
        residual_ref[...] = tokens_ref[...].astype(F32) + nn(mixed_ref[...], weight_ref[...])

    output_weight_of(place_ref, own_ref, other_ref, use)
    residual = residual_ref[...]
    normed_ref[...] = (residual * norm_scale(residual) * gain_ref[...]).astype(BF16)


def residual_step(place, tokens, mixed, own, other, gain):
    length, width = tokens.shape

    def full(*shape):
        return pl.BlockSpec(shape, lambda j, place_ref: (0,) * len(shape))

    table = full(length, width)
    weight = pl.BlockSpec((width, width), lambda j, place_ref: (0, 1))
    return pl.pallas_call(
        residual_kernel,
        grid_spec=pltpu.PrefetchScalarGridSpec(
            num_scalar_prefetch=1,
            grid=(1,),
            in_specs=[table, table, weight, weight, full(1, width)],
            out_specs=[table, table],
        ),
        out_shape=[shaped((length, width), F32), shaped((length, width), BF16)],
        compiler_params=pltpu.CompilerParams(vmem_limit_bytes=56 * MIB),
        cost_estimate=cost_of(
            flops=0, bytes_accessed=0, transcendentals=0
        ),
    )(place, tokens, mixed, own, other, gain)


DEEP = 4


def blocks_of(place_ref, read_a, read_b, write):
    wide = place_ref[0]
    for dx in range(2):
        for dy in range(2):
            for k in range(DEEP):
                to_wide, to_narrow = wide ^ (2 * k + dx), place_ref[1] ^ dy
                write(0, dx, dy, k, read_a(to_wide, to_narrow))
                write(1, dy, dx, k, read_b(to_wide, to_narrow))


def write_mine(refs):
    def write(which, part, row, k, value):
        refs[2 * which + part][row, k] = value

    return write


def write_other(ref):
    def write(which, part, row, k, value):
        ref[which, part, row, k] = value

    return write


FEED_STEPS = 2


def feed_kernel(last, *refs):
    place_ref, normed_ref, grad_ref, base_ref, expand_ref, contract_ref = refs[:6]
    refs = refs[6:]
    if last:
        pulled_in_ref, residual_hbm, gain_ref, own_hbm, other_hbm = refs[:5]
        out_ref, grad_residual_ref, grad_low_ref, grad_mixed_ref, gain_grad_ref = refs[5:10]
        mine = refs[10:14]
        refs = refs[14:]
        residual_ref, weight_ref = refs[-2:]
        refs = refs[:-2]
    else:
        out_ref, pulled_out_ref, both_ref = refs[:3]
        refs = refs[3:]
    total_ref, pulled_ref, turned_ref, expand_grad_ref, contract_grad_ref, in_sems, out_sems = refs
    step = pl.program_id(0)
    wide, narrow, core = place_ref[0], place_ref[1], place_ref[2]
    width = normed_ref.shape[1]

    def base_copy():
        return pltpu.make_async_copy(base_ref, total_ref, in_sems.at[0])

    def pulled_copy():
        return pltpu.make_async_copy(pulled_in_ref, pulled_ref, in_sems.at[1])

    def residual_copy():
        return pltpu.make_async_copy(residual_hbm, residual_ref, in_sems.at[2])

    def weight_copy(hbm):
        source = hbm.at[:, pl.ds(width, width)]
        return pltpu.make_async_copy(source, weight_ref, in_sems.at[3])

    def grad_copies(j):
        rows = expand_grad_ref.shape[1] // (2 * DEEP)

        def target(which, part, row, k):
            if last:
                return mine[2 * which + part].at[row, k]
            return both_ref.at[which, part, row, k]

        copies = []

        def copy(source, place):
            sem = out_sems.at[j * 4 * DEEP + len(copies)]
            copies.append(pltpu.make_async_copy(source, place, sem))

        for dx in range(2):
            for k in range(DEEP):
                start = pl.multiple_of((wide ^ (2 * k + dx)) * rows, 16)
                copy(expand_grad_ref.at[j, pl.ds(start, rows), :], target(0, dx, narrow ^ j, k))
        for dy in range(2):
            for i in range(DEEP):
                to_wide = DEEP * j + i
                start = pl.multiple_of((to_wide * 2 + (narrow ^ dy)) * rows, 16)
                apart = wide ^ to_wide
                copy(
                    contract_grad_ref.at[pl.ds(start, rows), :],
                    target(1, dy, apart & 1, apart >> 1),
                )
        return copies

    @pl.when(step == 0)
    def _():
        base_copy().start()
        if last:
            pulled_copy().start()
            residual_copy().start()

            @pl.when(core == 0)
            def _():
                weight_copy(own_hbm).start()

            @pl.when(core == 1)
            def _():
                weight_copy(other_hbm).start()

        turned_ref[...] = normed_ref[...].T

    expand = expand_ref[0]
    contract = contract_ref[0]
    grad_block = grad_ref[...]
    pre = nn(normed_ref[...], expand)
    grad_hidden = nt(grad_block, contract)
    scale = np.float32(np.sqrt(2.0 / np.pi))
    square = pre * pre
    bent = jnp.tanh(pre * (scale + (scale * np.float32(0.044715)) * square))
    half = 0.5 + 0.5 * bent
    hidden = (pre * half).astype(BF16)
    slope = half + (0.5 * pre) * (1.0 - bent * bent) * (
        scale + (scale * np.float32(3 * 0.044715)) * square
    )
    grad_pre = (grad_hidden * slope).astype(BF16)
    made = nn(hidden, contract)
    pulled = nt(grad_pre, expand)
    block = expand.shape[1]
    contract_grad_ref[pl.ds(pl.multiple_of(step * block, block), block), :] = tn(
        hidden, grad_block
    ).astype(BF16)
    expand_grad_ref[step] = nn(turned_ref[...], grad_pre).astype(BF16)
    for j in range(FEED_STEPS):

        @pl.when(step == j)
        def _(j=j):
            for copy in grad_copies(j):
                copy.start()

    @pl.when(step == 0)
    def _():
        base_copy().wait()
        total_ref[...] += made
        if last:
            pulled_copy().wait()
            pulled_ref[...] += pulled
        else:
            pulled_ref[...] = pulled

    @pl.when(step > 0)
    def _():
        total_ref[...] += made
        pulled_ref[...] += pulled

    @pl.when(step == pl.num_programs(0) - 1)
    def _():
        if last:
            residual_copy().wait()

            @pl.when(core == 0)
            def _():
                weight_copy(own_hbm).wait()

            @pl.when(core == 1)
            def _():
                weight_copy(other_hbm).wait()

            out_ref[...] = total_ref[...].astype(BF16)
            grad_values, grad_gain = norm_backward(
                residual_ref[...], gain_ref[...], pulled_ref[...]
            )
            grad_residual = grad_block.astype(F32) + grad_values
            grad_residual_ref[...] = grad_residual
            grad_low_ref[...] = grad_residual.astype(BF16)
            gain_grad_ref[...] = grad_gain
            grad_mixed_ref[...] = nt(grad_low_ref[...], weight_ref[...]).astype(BF16)
        else:
            out_ref[...] = total_ref[...]
            pulled_out_ref[...] = pulled_ref[...]
        for j in range(FEED_STEPS):
            for copy in grad_copies(j):
                copy.wait()


def feed_half(last, place, normed, grad_block, base, weights, more=()):
    length, width = normed.shape
    half = weights.shape[1]
    block = half // FEED_STEPS
    rows = width // (2 * DEEP)

    def full(*shape):
        return pl.BlockSpec(shape, lambda j, place_ref: (0,) * len(shape))

    table = full(length, width)
    anywhere = pl.BlockSpec(memory_space=pl.ANY)
    in_specs = [
        table,
        table,
        anywhere,
        pl.BlockSpec((1, width, block), lambda j, place_ref: (0, j, 0)),
        pl.BlockSpec((1, block, width), lambda j, place_ref: (1, j, 0)),
    ]
    grad_dims = (2, DEEP, rows, block)
    if last:
        in_specs += [anywhere, anywhere, full(1, width), anywhere, anywhere]
        out_specs = [table, table, table, table, full(1, width)] + [anywhere] * 4
        out_shape = [
            shaped((length, width), BF16),
            shaped((length, width), F32),
            shaped((length, width), BF16),
            shaped((length, width), BF16),
            shaped((1, width), F32),
        ] + [shaped(grad_dims, BF16)] * 4
    else:
        out_specs = [table, table, anywhere]
        out_shape = [
            shaped((length, width), F32),
            shaped((length, width), F32),
            shaped((2, 2) + grad_dims, BF16),
        ]
    extra = []
    if last:
        extra = [pltpu.VMEM((length, width), F32), pltpu.VMEM((width, width), BF16)]
    return pl.pallas_call(
        functools.partial(feed_kernel, last),
        grid_spec=pltpu.PrefetchScalarGridSpec(
            num_scalar_prefetch=1,
            grid=(FEED_STEPS,),
            in_specs=in_specs,
            out_specs=out_specs,
            scratch_shapes=[
                pltpu.VMEM((length, width), F32),
                pltpu.VMEM((length, width), F32),
                pltpu.VMEM((width, length), BF16),
                pltpu.VMEM((FEED_STEPS, width, block), BF16),
                pltpu.VMEM((half, width), BF16),
                pltpu.SemaphoreType.DMA((4,)),
                pltpu.SemaphoreType.DMA((FEED_STEPS * 4 * DEEP,)),
            ]
            + extra,
        ),
        out_shape=out_shape,
        compiler_params=pltpu.CompilerParams(vmem_limit_bytes=56 * MIB),
        cost_estimate=cost_of(
            flops=6 * length * width * half * 2, bytes_accessed=8 * MIB, transcendentals=0
        ),
    )(place, normed, grad_block, base, weights, weights, *more)


def project_grad_kernel(place_ref, *refs):
    normed_ref, dq_ref, dk_ref, dv_ref, mixed_ref, grad_ref = refs[:6]
    mine = refs[6:10]
    other_ref, turned_ref, grads_ref = refs[10:]
    step = pl.program_id(0)
    width = dq_ref.shape[1]
    rows = width // (4 * DEEP)

    @pl.when(step == 0)
    def _():
        turned_ref[...] = normed_ref[...].T
        grads_ref[0] = nn(turned_ref[...], dq_ref[...]).astype(BF16)

    @pl.when(step == 1)
    def _():
        grads_ref[1] = nn(turned_ref[...], dk_ref[...]).astype(BF16)

    @pl.when(step == 2)
    def _():
        grads_ref[2] = nn(turned_ref[...], dv_ref[...]).astype(BF16)

    @pl.when(step == 3)
    def _():
        grads_ref[3] = tn(mixed_ref[...], grad_ref[...]).astype(BF16)

        def reader(which, core):
            def read(wide, narrow):
                start = pl.multiple_of((wide * 2 + core) * rows, 16)
                return grads_ref[2 * narrow + which, pl.ds(start, rows), :]

            return read

        core = place_ref[2]
        blocks_of(place_ref, reader(0, 1 - core), reader(1, 1 - core), write_other(other_ref))
        blocks_of(place_ref, reader(0, core), reader(1, core), write_mine(mine))


def project_grad(place, normed, dq, dk, dv, mixed, grad):
    length, width = normed.shape
    rows = width // (4 * DEEP)

    def full(*shape):
        return pl.BlockSpec(shape, lambda j, place_ref: (0,) * len(shape))

    dims = (2, DEEP, rows, width)
    return pl.pallas_call(
        project_grad_kernel,
        grid_spec=pltpu.PrefetchScalarGridSpec(
            num_scalar_prefetch=1,
            grid=(4,),
            in_specs=[full(length, width)] * 6,
            out_specs=[full(*dims)] * 4 + [full(2, 2, *dims)],
            scratch_shapes=[
                pltpu.VMEM((width, length), BF16),
                pltpu.VMEM((4, width, width), BF16),
            ],
        ),
        out_shape=[shaped(dims, BF16)] * 4 + [shaped((2, 2) + dims, BF16)],
        compiler_params=pltpu.CompilerParams(vmem_limit_bytes=56 * MIB),
        cost_estimate=cost_of(
            flops=8 * length * width * width, bytes_accessed=8 * MIB, transcendentals=0
        ),
    )(place, normed, dq, dk, dv, mixed, grad)


HALF = DEEP // 2
SOURCES = [
    (range(DEEP), 0, 0),
    (range(DEEP), 1, 0),
    (range(DEEP), 0, 1),
    (range(HALF), 1, 1),
    (range(HALF, DEEP), 1, 1),
]
EARLY, LATE = (0, 2), (1, 3)
STRAIGHT_SOURCES = [
    source for some in (EARLY, LATE) for source in [(some, 0, 0), (some, 1, 0), (some, 0, 1)]
]
FAR_SOURCES = [(EARLY, 1, 1), (LATE[:1], 1, 1), (LATE[1:], 1, 1)]


def assemble_kernel(place_ref, *refs):
    out_ref = refs[-1]
    for ref, (deep, dx, dy) in zip(refs, SOURCES):
        rows = ref.shape[1]
        for i in range(ref.shape[0]):
            start = (place_ref[0] ^ (2 * deep[i] + dx)) * 2 + (place_ref[1] ^ dy)
            out_ref[pl.ds(pl.multiple_of(start * rows, 16), rows), :] = ref[i]


def assemble(place, pieces):
    rows, columns = pieces[0].shape[1:]
    dims = (4 * DEEP * rows, columns)
    return pl.pallas_call(
        assemble_kernel,
        grid_spec=pltpu.PrefetchScalarGridSpec(
            num_scalar_prefetch=1,
            grid=(1,),
            in_specs=[
                pl.BlockSpec(piece.shape, lambda j, place_ref: (0, 0, 0)) for piece in pieces
            ],
            out_specs=pl.BlockSpec(dims, lambda j, place_ref: (0, 0)),
        ),
        out_shape=shaped(dims, BF16),
        compiler_params=pltpu.CompilerParams(vmem_limit_bytes=56 * MIB),
        cost_estimate=cost_of(flops=0, bytes_accessed=8 * MIB, transcendentals=0),
    )(place, *pieces)


def assemble_feed_kernel(sources, place_ref, *refs):
    piece_refs, out_ref, sems = refs[: len(sources)], refs[-2], refs[-1]
    copies = []

    def copy(source, base, rows, which):
        target = out_ref.at[which, pl.ds(pl.multiple_of(base, 16), rows), :]
        copies.append(pltpu.make_async_copy(source, target, sems.at[len(copies)]))

    for ref, (deep, dx, dy) in zip(piece_refs, sources):
        rows, columns = ref.shape[2:]
        half = rows // FEED_STEPS
        for i in range(ref.shape[0]):
            start = (place_ref[0] ^ (2 * deep[i] + dx)) * 2 + (place_ref[1] ^ dy)
            for j in range(FEED_STEPS):
                part = ref.at[i, 0, j * half : (j + 1) * half]
                copy(part, j * columns + start * half, half, 0)
            copy(ref.at[i, 1], start * rows, rows, 1)
    for item in copies:
        item.start()
    for item in copies:
        item.wait()


def assemble_feed(place, sources, pieces, begun=None):
    rows, columns = pieces[0].shape[2:]
    dims = (2, 4 * DEEP * rows, columns)
    count = sum(piece.shape[0] for piece in pieces) * (FEED_STEPS + 1)
    anywhere = pl.BlockSpec(memory_space=pl.ANY)
    specs = [pl.BlockSpec(piece.shape, lambda j, place_ref: (0, 0, 0, 0)) for piece in pieces]
    more, aliases = [], {}
    if begun is not None:
        more, aliases = [begun], {1 + len(pieces): 0}
    return pl.pallas_call(
        functools.partial(assemble_feed_kernel, sources),
        grid_spec=pltpu.PrefetchScalarGridSpec(
            num_scalar_prefetch=1,
            grid=(1,),
            in_specs=specs + [anywhere] * len(more),
            out_specs=anywhere,
            scratch_shapes=[pltpu.SemaphoreType.DMA((count,))],
        ),
        out_shape=shaped(dims, BF16),
        input_output_aliases=aliases,
        compiler_params=pltpu.CompilerParams(vmem_limit_bytes=56 * MIB),
        cost_estimate=cost_of(flops=4e9, bytes_accessed=8 * MIB, transcendentals=0),
    )(place, *pieces, *more)


def finish_feed_kernel(place_ref, *refs):
    parts, (expand_ref, contract_ref) = refs[:-2], refs[-2:]
    rows, columns = parts[0].shape[2:]
    unit = columns // DEEP
    for ref, dy, dc in [(parts[dc], dy, dc) for dc in range(2) for dy in range(2)]:
        y, c = place_ref[1] ^ dy, place_ref[2] ^ dc
        start = pl.multiple_of((c * 2 + y) * rows, 8)
        contract_ref[pl.ds(start, rows), :] = ref[dy, 1].astype(F32)
        for to_y in range(2):
            for to_c in range(2):

                @pl.when((y == to_y) & (c == to_c))
                def _(ref=ref, dy=dy, to_y=to_y, to_c=to_c):
                    value = ref[dy, 0].astype(F32)
                    for i in range(DEEP):
                        base = ((to_y * DEEP + i) * 2 + to_c) * unit
                        expand_ref[:, base : base + unit] = value[:, i * unit : (i + 1) * unit]


def finish_feed(place, parts):
    rows, columns = parts[0].shape[2:]
    dims = [(rows, 4 * columns), (4 * rows, columns)]
    return pl.pallas_call(
        finish_feed_kernel,
        grid_spec=pltpu.PrefetchScalarGridSpec(
            num_scalar_prefetch=1,
            grid=(1,),
            in_specs=[pl.BlockSpec(part.shape, lambda j, place_ref: (0, 0, 0, 0)) for part in parts],
            out_specs=[pl.BlockSpec(d, lambda j, place_ref: (0, 0)) for d in dims],
        ),
        out_shape=[shaped(d, F32) for d in dims],
        compiler_params=pltpu.CompilerParams(vmem_limit_bytes=56 * MIB),
        cost_estimate=cost_of(flops=0, bytes_accessed=4 * MIB, transcendentals=0),
    )(place, *parts)


def finish_square_kernel(place_ref, *refs):
    parts, outs = refs[:-4], refs[-4:]
    rows = parts[0].shape[2]
    for ref, dy, dc in [(parts[dc], dy, dc) for dc in range(2) for dy in range(2)]:
        y, c = place_ref[1] ^ dy, place_ref[2] ^ dc
        for to_y in range(2):

            @pl.when(y == to_y)
            def _(ref=ref, dy=dy, to_y=to_y, c=c):
                for i in range(2):
                    start = pl.multiple_of(c * rows, 8)
                    outs[2 * to_y + i][pl.ds(start, rows), :] = ref[dy, i].astype(F32)


def finish_square(place, parts):
    rows, columns = parts[0].shape[2:]
    dims = (2 * rows, columns)
    return pl.pallas_call(
        finish_square_kernel,
        grid_spec=pltpu.PrefetchScalarGridSpec(
            num_scalar_prefetch=1,
            grid=(1,),
            in_specs=[pl.BlockSpec(part.shape, lambda j, place_ref: (0, 0, 0, 0)) for part in parts],
            out_specs=[pl.BlockSpec(dims, lambda j, place_ref: (0, 0))] * 4,
        ),
        out_shape=[shaped(dims, F32)] * 4,
        compiler_params=pltpu.CompilerParams(vmem_limit_bytes=56 * MIB),
        cost_estimate=cost_of(flops=0, bytes_accessed=4 * MIB, transcendentals=0),
    )(place, *parts)


def tokens_back_kernel(
    place_ref,
    dq_ref,
    dk_ref,
    dv_ref,
    own_ref,
    other_ref,
    tokens_ref,
    gain_ref,
    residual_ref,
    out_ref,
    gain_grad_ref,
    pulled_ref,
):
    width = dq_ref.shape[1]

    def pull(first_ref, second_ref):
        pulled = nt(dq_ref[...], first_ref[:, 0:width])
        pulled += nt(dk_ref[...], first_ref[:, width : 2 * width])
        pulled += nt(dv_ref[...], second_ref[:, 0:width])
        pulled_ref[...] = pulled

    @pl.when(place_ref[2] == 1)
    def _():
        pull(own_ref, other_ref)

    @pl.when(place_ref[2] == 0)
    def _():
        pull(other_ref, own_ref)

    grad_values, grad_gain = norm_backward(
        tokens_ref[...].astype(F32), gain_ref[...], pulled_ref[...]
    )
    out_ref[...] = residual_ref[...] + grad_values
    gain_grad_ref[...] = grad_gain


def tokens_back(place, dq, dk, dv, own, other, tokens, gain, grad_residual):
    length, width = tokens.shape

    def full(*shape):
        return pl.BlockSpec(shape, lambda j, place_ref: (0,) * len(shape))

    table = full(length, width)
    return pl.pallas_call(
        tokens_back_kernel,
        grid_spec=pltpu.PrefetchScalarGridSpec(
            num_scalar_prefetch=1,
            grid=(1,),
            in_specs=[table, table, table]
            + [full(width, 2 * width)] * 2
            + [table, full(1, width), table],
            out_specs=[table, full(1, width)],
            scratch_shapes=[pltpu.VMEM((length, width), F32)],
        ),
        out_shape=[shaped((length, width), F32), shaped((1, width), F32)],
        compiler_params=pltpu.CompilerParams(vmem_limit_bytes=56 * MIB),
        cost_estimate=cost_of(
            flops=6 * length * width * width, bytes_accessed=8 * MIB, transcendentals=0
        ),
    )(place, dq, dk, dv, own, other, tokens, gain, grad_residual)


def exchange(value, dz=0, dx=0, dy=0, dc=0):
    flip = ((2 * dz + dx) * 2 + dy) * 2 + dc
    total = 8 * DEEP
    return lax.ppermute(value, ("wide", "narrow"), [(i, i ^ flip) for i in range(total)])


def after(value, *done):
    return lax.optimization_barrier((value,) + done)[0]


def together(*values):
    return lax.optimization_barrier(values)


def gather_stage_z(piece):
    return jnp.stack([piece] + [exchange(piece, dz=k) for k in range(1, DEEP)])


def gather_stage_xy(near):
    return exchange(near, dx=1), exchange(near, dy=1)


def gather_stage_far(over_x, over_y):
    half = over_x.shape[0] // 2
    return exchange(over_y[:half], dx=1), exchange(over_x[half:], dy=1)


def low(value):
    return value.astype(BF16)


def add(*values):
    return sum(value.astype(F32) for value in values)


def reduce_first_out(mine, other):
    return low(add(mine[1], other[0, 1])), low(add(mine[3], other[1, 1]))


def reduce_first(outs):
    return exchange(outs[0], dx=1), exchange(outs[1], dy=1)


def reduce_second_out(mine, other, first):
    return tuple(low(add(mine[2 * i][1], other[i, 0, 1], first[i][1])) for i in range(2))


def reduce_second(outs):
    return exchange(outs[0], dy=1), exchange(outs[1], dx=1)


def reduce_level(mine, other, first, second, k):
    return jnp.stack(
        [add(mine[2 * i][0, k], other[i, 0, 0, k], first[i][0, k], second[i][k]) for i in range(2)]
    )


def reduce_deep_out(*parts):
    return tuple(low(reduce_level(*parts, k)) for k in range(1, DEEP))


def reduce_deep(outs):
    return tuple(exchange(out, dz=k + 1) for k, out in enumerate(outs))


def reduce_last(parts, deep):
    return low(reduce_level(*parts, 0) + add(*deep))


def spread_y(part):
    return exchange(part, dy=1)


def spread_core(part, other_y):
    both = jnp.stack([part, other_y])
    return both, exchange(both, dc=1)


def on_device(
    tokens,
    query_weight,
    key_weight,
    value_weight,
    output_weight,
    expand_weight,
    contract_weight,
    attention_gain,
    feedforward_gain,
    bias_table,
    query_length,
    passage_length,
    pair_order,
    regrouped_grad,
):
    row_count, length, width = tokens.shape
    bucket_count, head_count = bias_table.shape
    wide_index = lax.axis_index("wide")
    wide_count = lax.axis_size("wide")
    narrow_index = lax.axis_index("narrow")
    narrow_count = lax.axis_size("narrow")
    by_hand = wide_count == 2 * DEEP and narrow_count == 4
    hidden_count = expand_weight.shape[1]
    part_rows = hidden_count // (4 * DEEP)

    square_weights = (query_weight, key_weight, value_weight, output_weight)
    if by_hand:
        narrow_y, core = narrow_index // 2, narrow_index % 2
    else:
        wide_index = narrow_y = core = jnp.int32(0)
    place = jnp.stack([wide_index, narrow_y, core]).astype(jnp.int32)

    gain_one = attention_gain[None]
    gain_two = feedforward_gain[None]
    group_rows = regrouped_grad.shape[0]
    chosen = lax.dynamic_slice_in_dim(pair_order, narrow_index * group_rows, group_rows)
    local_rows = chosen // (row_count * narrow_count) * row_count + chosen % row_count
    arranged = jnp.zeros_like(regrouped_grad).at[local_rows].set(regrouped_grad)

    spot = np.arange(2 * length)
    offsets = np.where(spot <= 2 * length - KB, length - KB - spot, 3 * length - KB - spot)
    band_hot = jnp.asarray(one_hot_rows(np.clip(offsets, 1 - length, length - 1), bucket_count))
    lines = jnp.dot(bias_table.T, band_hot.T, precision=lax.Precision.HIGHEST)
    lines = lines.reshape(head_count // 2, 2, 2 * length)
    positions = jnp.arange(length, dtype=jnp.int32)
    fill = jnp.where(positions < query_length[0] + passage_length[0], 0.0, negative)
    fill = fill.astype(F32)[:, None]

    if by_hand:
        half_rows = query_weight.shape[0] // 2
        own_half = 1 - core
        first = jnp.concatenate(square_weights[:2], axis=1)
        second = jnp.concatenate(square_weights[2:], axis=1)
        square_piece = lax.dynamic_slice_in_dim(
            jnp.where(core == 1, first, second), narrow_y * half_rows, half_rows
        )
        expand_piece = lax.dynamic_slice_in_dim(
            lax.dynamic_index_in_dim(
                expand_weight.reshape(-1, 2 * DEEP, 2, part_rows), own_half, 2, False
            ).reshape(-1, hidden_count // 2),
            narrow_y * half_rows,
            half_rows,
        )
        contract_rows = contract_weight.shape[0] // 4
        contract_piece = lax.dynamic_slice_in_dim(
            contract_weight, (own_half * 2 + narrow_y) * contract_rows, contract_rows
        )
        feed_piece = jnp.stack(
            [
                jnp.concatenate(
                    [expand_piece[:, j * width : (j + 1) * width] for j in range(FEED_STEPS)]
                ),
                contract_piece,
            ]
        )
        square_near = gather_stage_z(square_piece)
        square_near, arranged, lines, fill, feed_piece, gain_one, gain_two, local_rows = together(
            square_near, arranged, lines, fill, feed_piece, gain_one, gain_two, local_rows
        )
        square_xy = gather_stage_xy(square_near)
        feed_two = exchange(feed_piece, dz=2)
        feed_early = jnp.stack([feed_piece, feed_two])
        square_xy, feed_early, feed_piece = together(square_xy, feed_early, feed_piece)
        square_far = gather_stage_far(*square_xy)
        feed_one = exchange(feed_piece, dz=1)
        square_far, feed_one = together(square_far, feed_one)
        square_own = assemble(place, [square_near, *square_xy, *square_far])
        square_own, feed_early, feed_piece = together(square_own, feed_early, feed_piece)
        square_other = exchange(square_own, dc=1)
        feed_early_xy = gather_stage_xy(feed_early)
        feed_three = exchange(feed_piece, dz=3)
    else:

        def gathered(weight):
            return lax.all_gather(weight, "wide", axis=0, tiled=True)

        square_other = gathered(jnp.concatenate(square_weights[:2], axis=1))
        square_own = gathered(jnp.concatenate(square_weights[2:], axis=1))
        full_expand = gathered(expand_weight).reshape(width, 2 * DEEP, 2, part_rows)
        full_contract = gathered(contract_weight).reshape(2 * DEEP, 2, part_rows, width)
        feed_other, feed_own = (
            jnp.stack(
                [
                    full_expand[:, :, i]
                    .reshape(width, FEED_STEPS, -1)
                    .transpose(1, 0, 2)
                    .reshape(-1, width),
                    full_contract[:, i].reshape(-1, width),
                ]
            )
            for i in range(2)
        )

    inputs = tokens.reshape(length, width)
    attention_input, qkv = project(place, inputs, gain_one, square_own, square_other)
    if by_hand:
        arranged = after(arranged, qkv)
    grad_block = lax.all_to_all(arranged, "wide", split_axis=0, concat_axis=0, tiled=True).reshape(
        length, width
    )
    if by_hand:
        qkv, feed_early_xy, feed_three = together(qkv, feed_early_xy, feed_three)
        feed_late = jnp.stack([feed_one, feed_three])
        qkv, feed_late = together(qkv, feed_late)
        feed_late_xy = gather_stage_xy(feed_late)
        feed_early_far = [exchange(feed_early_xy[0], dy=1)]
    mixed, probs = attend(qkv, lines, fill, head_count)
    if by_hand:
        mixed, feed_late_xy = together(mixed, feed_late_xy)
        feed_late_far = gather_stage_far(*feed_late_xy)
        feed_begun = assemble_feed(
            place,
            STRAIGHT_SOURCES,
            [feed_early, *feed_early_xy, feed_late, *feed_late_xy],
        )
        mixed, feed_begun = together(mixed, feed_begun)
    residual, expand_input = residual_step(
        place, inputs, mixed, square_own, square_other, gain_two
    )
    if by_hand:
        feed_own = assemble_feed(
            place, FAR_SOURCES, [*feed_early_far, *feed_late_far], after(feed_begun, residual)
        )
        feed_other = exchange(feed_own, dc=1)
    partial_out, partial_pulled, feed_sent = feed_half(
        False, place, expand_input, grad_block, residual, feed_own
    )
    if by_hand:
        feed_got = exchange(feed_sent, dc=1)
    results = feed_half(
        True,
        place,
        expand_input,
        grad_block,
        partial_out,
        feed_other,
        (partial_pulled, residual, gain_two, square_own, square_other),
    )
    block_output, grad_residual, grad_low, grad_mixed, gain_two_grad = results[:5]
    feed_mine = results[5:9]
    if by_hand:
        feed_got, grad_mixed, block_output = together(feed_got, grad_mixed, block_output)
        outs = reduce_first_out(feed_mine, feed_got)
        grad_mixed, *outs = together(grad_mixed, *outs)
        feed_first = reduce_first(outs)
    dq, dk, dv, line_grads = attend_back(qkv, grad_mixed, probs)
    results = project_grad(place, attention_input, dq, dk, dv, mixed, grad_low)
    square_mine, square_sent = results[:4], results[4]
    if by_hand:
        square_sent, *feed_first = together(square_sent, *feed_first)
        square_got = exchange(square_sent, dc=1)
        outs = reduce_second_out(feed_mine, feed_got, feed_first)
        dq, *outs = together(dq, *outs)
        feed_second = reduce_second(outs)
    tokens_grad, gain_one_grad = tokens_back(
        place, dq, dk, dv, square_own, square_other, inputs, gain_one, grad_residual
    )
    if by_hand:
        block_output, line_grads, gain_one_grad = together(
            block_output, line_grads, gain_one_grad
        )
    received = lax.all_to_all(
        block_output.reshape(-1, regrouped_grad.shape[1], width),
        "wide",
        split_axis=0,
        concat_axis=0,
        tiled=True,
    )
    if not by_hand:
        table_grad = jnp.dot(
            jnp.asarray(line_one_hot(bucket_count).T),
            line_grads.reshape(head_count, -1).T,
            precision=lax.Precision.HIGHEST,
        )
        small = jnp.concatenate([gain_one_grad[0], gain_two_grad[0], table_grad.reshape(-1)])
        small_count = small.shape[0]
        regrouped = jnp.take(received, local_rows, axis=0)
    if by_hand:
        square_got, gain_one_grad = together(square_got, gain_one_grad)
        outs = reduce_first_out(square_mine, square_got)
        square_first = reduce_first(outs)
        feed_second = after(feed_second, *outs)
        feed_parts = (feed_mine, feed_got, feed_first, feed_second)
        outs = reduce_deep_out(*feed_parts)
        feed_deep = reduce_deep(outs)
        square_first, received = together(after(square_first, *outs), received)
        regrouped = jnp.take(received, local_rows, axis=0)
        line_grads = after(line_grads, *outs)
        table_grad = jnp.dot(
            jnp.asarray(line_one_hot(bucket_count).T),
            line_grads.reshape(head_count, -1).T,
            precision=lax.Precision.HIGHEST,
        )
        small = jnp.concatenate([gain_one_grad[0], gain_two_grad[0], table_grad.reshape(-1)])
        small_count = small.shape[0]
        small = jnp.pad(small, (0, -small_count % 1024)).reshape(-1, 128)
        small = jnp.broadcast_to(small[None], (8 * DEEP,) + small.shape)
        small = lax.all_to_all(small, ("wide", "narrow"), 0, 0, tiled=True)
        outs = reduce_second_out(square_mine, square_got, square_first)
        square_second = reduce_second(outs)
        feed_deep = after(feed_deep, *outs)
        square_parts = (square_mine, square_got, square_first, square_second)
        feed_deep, regrouped = together(feed_deep, regrouped)
        feed_part = reduce_last(feed_parts, feed_deep)
        feed_other_y = spread_y(feed_part)
        outs = reduce_deep_out(*square_parts)
        feed_other_y, outs, small = together(feed_other_y, outs, small)
        square_deep = reduce_deep(outs)
        feed_spread = spread_core(feed_part, feed_other_y)
        final_expand, final_contract = finish_feed(place, feed_spread)
        square_deep, small = together(after(square_deep, final_expand), small)
        square_part = reduce_last(square_parts, square_deep)
        finals = finish_square(place, spread_core(square_part, spread_y(square_part)))
        small = jnp.sum(small, axis=0).reshape(-1)
    else:

        def summed(grad):
            part = lax.psum_scatter(grad, "wide", scatter_dimension=0, tiled=True)
            return lax.psum(part, "narrow").astype(F32)

        def stacked(which, mine, other):
            kept = jnp.stack(mine[2 * which : 2 * which + 2])
            return jnp.stack([kept, other[which]])

        expand_all = stacked(0, feed_mine, feed_sent)
        expand_all = expand_all.reshape(expand_all.shape[:5] + (DEEP, part_rows))
        expand_all = expand_all.transpose(3, 1, 4, 2, 5, 0, 6)
        contract_all = stacked(1, feed_mine, feed_sent).transpose(3, 2, 0, 1, 4, 5)
        first = stacked(0, square_mine, square_sent)
        second = stacked(1, square_mine, square_sent).transpose(0, 2, 1, 3, 4, 5)
        square_all = jnp.stack([first, second]).transpose(4, 2, 1, 5, 3, 0, 6)
        final_contract = summed(contract_all.reshape(hidden_count, width))
        final_expand = summed(expand_all.reshape(width, hidden_count))
        final_square = summed(square_all.reshape(width, 4 * width))
        finals = [final_square[:, i * width : (i + 1) * width] for i in range(4)]
        small = lax.psum(small, ("wide", "narrow"))

    return (
        regrouped,
        tokens_grad.reshape(row_count, length, width),
        *finals,
        final_expand,
        final_contract,
        small[:width],
        small[width : 2 * width],
        small[2 * width : small_count].reshape(bucket_count, head_count),
    )


def solution(mesh):
    in_specs = (
        P(("wide", "narrow"), None, None),
        P("wide", None),
        P("wide", None),
        P("wide", None),
        P("wide", None),
        P("wide", None),
        P("wide", None),
        P(),
        P(),
        P(),
        P(("wide", "narrow")),
        P(("wide", "narrow")),
        P(),
        P("narrow", "wide", None),
    )
    out_specs = (
        P("narrow", "wide", None),
        P(("wide", "narrow"), None, None),
        P("wide", None),
        P("wide", None),
        P("wide", None),
        P("wide", None),
        P("wide", None),
        P("wide", None),
        P(),
        P(),
        P(),
    )
    return jax.shard_map(
        on_device, mesh=mesh, in_specs=in_specs, out_specs=out_specs, check_vma=False
    )
```

```python
import functools

import jax
import jax.numpy as jnp
import numpy as np
from jax import lax
from jax.experimental import pallas as pl
from jax.experimental.pallas import tpu as pltpu
from jax.sharding import PartitionSpec as P

MAX_DIST = 128
epsilon = 1e-06
negative = -1000000000.0
F32 = jnp.float32
BF16 = jnp.bfloat16
MIB = 1024 * 1024


def bucket_index(offset_values, bucket_total, max_reach):
    exact_part = bucket_total // 4
    bounds_table = np.ceil(
        exact_part * (max_reach / exact_part) ** (np.arange(1, exact_part) / exact_part) - 1e-06
    ).astype(np.int32)
    distance = np.abs(offset_values)
    passed = np.zeros_like(distance)
    for limit_value in bounds_table:
        passed = passed + (distance >= int(limit_value)).astype(np.int32)
    coarse = np.where(distance < exact_part, distance, exact_part + passed)
    return coarse + (offset_values > 0).astype(np.int32) * (bucket_total // 2)


def one_hot_rows(offset_values, bucket_total):
    ids = bucket_index(np.asarray(offset_values, np.int32), bucket_total, MAX_DIST)
    return (ids[:, None] == np.arange(bucket_total)[None, :]).astype(np.float32)


def nn(left, right):
    return lax.dot_general(left, right, (((1,), (0,)), ((), ())), preferred_element_type=F32)


def nt(left, right):
    return lax.dot_general(left, right, (((1,), (1,)), ((), ())), preferred_element_type=F32)


def tn(left, right):
    return lax.dot_general(left, right, (((0,), (0,)), ((), ())), preferred_element_type=F32)


def norm_scale(values):
    return lax.rsqrt(jnp.mean(values * values, axis=-1, keepdims=True) + epsilon)


def norm_backward(values, gain, grad):
    scale = norm_scale(values)
    scaled = grad * gain
    dots = jnp.mean(scaled * values, axis=-1, keepdims=True)
    grad_values = scale * scaled - values * (scale * scale * scale * dots)
    grad_gain = jnp.sum(grad * (values * scale), axis=0, keepdims=True)
    return grad_values, grad_gain


def whole(shape):
    return pl.BlockSpec(shape, lambda *_: (0,) * len(shape))


def cost_of(flops, bytes_accessed, transcendentals):
    return pl.CostEstimate(flops=10 * int(flops), bytes_accessed=bytes_accessed, transcendentals=0)


def call(kernel, grid, in_specs, out_specs, out_shape, scratch=(), flops=0, vmem=56):
    return pl.pallas_call(
        kernel,
        grid=grid,
        in_specs=in_specs,
        out_specs=out_specs,
        out_shape=out_shape,
        scratch_shapes=list(scratch),
        compiler_params=pltpu.CompilerParams(vmem_limit_bytes=vmem * MIB),
        cost_estimate=cost_of(flops=flops, bytes_accessed=8 * MIB, transcendentals=0),
    )


def shaped(shape, kind):
    return jax.ShapeDtypeStruct(shape, kind)


def project_kernel(place_ref, tokens_ref, gain_ref, own_ref, other_ref, normed_ref, qkv_ref):
    step = pl.program_id(0)
    own_half = 1 - place_ref[2]

    @pl.when(step == 0)
    def _():
        values = tokens_ref[...].astype(F32)
        normed_ref[...] = (values * norm_scale(values) * gain_ref[...]).astype(BF16)

    @pl.when((step < 2) & (own_half * 2 + step < 3))
    def _():
        qkv_ref[...] = nn(normed_ref[...], own_ref[...]).astype(BF16)

    @pl.when((step >= 2) & (step - own_half * 2 < 3))
    def _():
        qkv_ref[...] = nn(normed_ref[...], other_ref[...]).astype(BF16)


def project(place, tokens, gain, own, other):
    length, width = tokens.shape

    def column(j, place_ref):
        own_half = 1 - place_ref[2]
        return (0, jnp.where(j < 2, own_half * 2 + j, j - own_half * 2))

    def full(*shape):
        return pl.BlockSpec(shape, lambda j, place_ref: (0,) * len(shape))

    return pl.pallas_call(
        project_kernel,
        grid_spec=pltpu.PrefetchScalarGridSpec(
            num_scalar_prefetch=1,
            grid=(4,),
            in_specs=[
                full(length, width),
                full(1, width),
                pl.BlockSpec((width, width), lambda j, place_ref: (0, jnp.minimum(j, 1))),
                pl.BlockSpec((width, width), lambda j, place_ref: (0, jnp.maximum(j - 2, 0))),
            ],
            out_specs=[full(length, width), pl.BlockSpec((length, width), column)],
        ),
        out_shape=[shaped((length, width), BF16), shaped((length, 4 * width), BF16)],
        compiler_params=pltpu.CompilerParams(vmem_limit_bytes=62 * MIB),
        cost_estimate=cost_of(
            flops=6 * length * width * width, bytes_accessed=8 * MIB, transcendentals=0
        ),
    )(place, tokens, gain, own, other)


QB = 512
KB = 128


def head_lanes(shape, which, size):
    lanes = lax.broadcasted_iota(jnp.int32, shape, 1)
    return (lanes < size) == (which == 0)


def attend_kernel(q_ref, k_ref, v_ref, line_ref, fill_ref, mixed_ref, probs_ref):
    length, pair = q_ref.shape
    size = pair // 2
    queries = q_ref[...]
    keys = k_ref[...]
    values_t = v_ref[...].T
    fill = fill_ref[...]
    heads = []
    for a in range(2):
        own = jnp.where(head_lanes(queries.shape, a, size), queries, jnp.zeros_like(queries))
        line = jnp.broadcast_to(line_ref[0, a : a + 1, :], (KB, 2 * length))
        band = pltpu.roll(line, 0, 1, stride=1, stride_axis=0)
        parts = []
        for qb in range(0, length, QB):
            raw = nt(keys, own[qb : qb + QB])
            rows = []
            for kb in range(0, length, KB):
                start = length - KB - kb + qb
                rows.append(
                    raw[kb : kb + KB] + (band[:, start : start + QB] + fill[kb : kb + KB])
                )
            scores = jnp.concatenate(rows, axis=0)
            peak = jnp.max(scores, axis=0, keepdims=True)
            weights = jnp.exp(scores - peak)
            total = jnp.sum(weights, axis=0, keepdims=True)
            probs = (weights * (1.0 / total)).astype(BF16)
            probs_ref[a, :, qb : qb + QB] = probs
            parts.append(nn(values_t[a * size : (a + 1) * size], probs))
        heads.append(jnp.concatenate(parts, axis=1))
    mixed_ref[...] = jnp.concatenate(heads, axis=0).T.astype(BF16)


def attend(qkv, lines, fill, head_count):
    length = qkv.shape[0]
    width = qkv.shape[1] // 4
    pairs = head_count // 2
    size = width // pairs

    def column(base):
        return pl.BlockSpec((length, size), lambda p: (0, base + p))

    return call(
        attend_kernel,
        (pairs,),
        [
            column(0),
            column(pairs),
            column(2 * pairs),
            pl.BlockSpec((1, 2, 2 * length), lambda p: (p, 0, 0)),
            whole((length, 1)),
        ],
        [column(0), pl.BlockSpec((2, length, length), lambda p: (p, 0, 0))],
        [shaped((length, width), BF16), shaped((head_count, length, length), BF16)],
        flops=8 * head_count * length * length * size,
    )(qkv, qkv, qkv, lines, fill)


def attend_back_kernel(
    q_ref, k_ref, v_ref, grad_ref, probs_ref, dq_ref, dk_ref, dv_ref, line_ref
):
    length, pair = q_ref.shape
    size = pair // 2
    queries = q_ref[...]
    keys_t = k_ref[...].T
    values = v_ref[...]
    grads = grad_ref[...]
    blocks = length // KB
    dq_heads, dk_heads, dv_heads = [], [], []
    for a in range(2):
        own = jnp.where(head_lanes(grads.shape, a, size), grads, jnp.zeros_like(grads))
        dq_parts = []
        dk = dv = None
        near = {}
        for qb in range(0, length, QB):
            probs = probs_ref[a, :, qb : qb + QB]
            probs_wide = probs.astype(F32)
            pulled = nt(values, own[qb : qb + QB])
            dots = jnp.sum(probs_wide * pulled, axis=0, keepdims=True)
            grad_scores = (probs_wide * (pulled - dots)).astype(BF16)
            dq_parts.append(nn(keys_t[a * size : (a + 1) * size], grad_scores))
            dk_part = nn(grad_scores, queries[qb : qb + QB])
            dv_part = nn(probs, grads[qb : qb + QB])
            dk = dk_part if dk is None else dk + dk_part
            dv = dv_part if dv is None else dv + dv_part
            wide = grad_scores.astype(F32)
            for i in range(blocks):
                for j in range(QB // KB):
                    gap = i - (qb // KB + j)
                    gap = max(-2, min(2, gap))
                    piece = wide[i * KB : (i + 1) * KB, j * KB : (j + 1) * KB]
                    near[gap] = piece if gap not in near else near[gap] + piece
        dq_heads.append(jnp.concatenate(dq_parts, axis=1))
        dk_heads.append(dk)
        dv_heads.append(dv)
        fold = jnp.concatenate([near[1], near[0], near[-1], jnp.zeros_like(near[0])], axis=1)
        rows = KB
        while rows > 8:
            rows //= 2
            fold = fold[:rows] + pltpu.roll(fold[rows : 2 * rows], 4 * KB - rows, 1)
        line_ref[0, a, :, 0 : 4 * KB] = fold
        far = jnp.concatenate([near[2], near[-2]], axis=1)
        line_ref[0, a, :, 4 * KB : 6 * KB] = jnp.sum(far.reshape(KB // 8, 8, 2 * KB), axis=0)
    first = head_lanes(queries.shape, 0, size)
    dq_ref[...] = jnp.concatenate(dq_heads, axis=0).T.astype(BF16)
    dk_ref[...] = jnp.where(first, dk_heads[0], dk_heads[1]).astype(BF16)
    dv_ref[...] = jnp.where(first, dv_heads[0], dv_heads[1]).astype(BF16)


def attend_back(qkv, grad_mixed, probs):
    head_count, length, _ = probs.shape
    width = grad_mixed.shape[1]
    pairs = head_count // 2
    size = width // pairs

    def column(base):
        return pl.BlockSpec((length, size), lambda p: (0, base + p))

    grad_shape = shaped((length, width), BF16)
    return call(
        attend_back_kernel,
        (pairs,),
        [
            column(0),
            column(pairs),
            column(2 * pairs),
            column(0),
            pl.BlockSpec((2, length, length), lambda p: (p, 0, 0)),
        ],
        [
            column(0),
            column(0),
            column(0),
            pl.BlockSpec((1, 2, 8, 6 * KB), lambda p: (p, 0, 0, 0)),
        ],
        [grad_shape, grad_shape, grad_shape, shaped((pairs, 2, 8, 6 * KB), F32)],
        flops=12 * head_count * length * length * size,
    )(qkv, qkv, qkv, grad_mixed, probs)


def line_one_hot(bucket_total):
    column = np.arange(4 * KB)
    rows = []
    for s in range(8):
        place = (column - s) % (4 * KB)
        offset = np.where(place <= 3 * KB, KB - place, 5 * KB - place)
        rows.append(np.concatenate([offset, np.full(KB, 3 * KB), np.full(KB, -3 * KB)]))
    return one_hot_rows(np.concatenate(rows), bucket_total)


def output_weight_of(place_ref, own_ref, other_ref, use):
    @pl.when(place_ref[2] == 0)
    def _():
        use(own_ref)

    @pl.when(place_ref[2] == 1)
    def _():
        use(other_ref)


def residual_kernel(
    place_ref, tokens_ref, mixed_ref, own_ref, other_ref, gain_ref, residual_ref, normed_ref
):
    def use(weight_ref):
        residual_ref[...] = tokens_ref[...].astype(F32) + nn(mixed_ref[...], weight_ref[...])

    output_weight_of(place_ref, own_ref, other_ref, use)
    residual = residual_ref[...]
    normed_ref[...] = (residual * norm_scale(residual) * gain_ref[...]).astype(BF16)


def residual_step(place, tokens, mixed, own, other, gain):
    length, width = tokens.shape

    def full(*shape):
        return pl.BlockSpec(shape, lambda j, place_ref: (0,) * len(shape))

    table = full(length, width)
    weight = pl.BlockSpec((width, width), lambda j, place_ref: (0, 1))
    return pl.pallas_call(
        residual_kernel,
        grid_spec=pltpu.PrefetchScalarGridSpec(
            num_scalar_prefetch=1,
            grid=(1,),
            in_specs=[table, table, weight, weight, full(1, width)],
            out_specs=[table, table],
        ),
        out_shape=[shaped((length, width), F32), shaped((length, width), BF16)],
        compiler_params=pltpu.CompilerParams(vmem_limit_bytes=62 * MIB),
        cost_estimate=cost_of(
            flops=0, bytes_accessed=0, transcendentals=0
        ),
    )(place, tokens, mixed, own, other, gain)


DEEP = 4


def blocks_of(place_ref, read_a, read_b, write):
    wide = place_ref[0]
    for dx in range(2):
        for dy in range(2):
            for k in range(DEEP):
                to_wide, to_narrow = wide ^ (2 * k + dx), place_ref[1] ^ dy
                write(0, dx, dy, k, read_a(to_wide, to_narrow))
                write(1, dy, dx, k, read_b(to_wide, to_narrow))


def write_mine(refs):
    def write(which, part, row, k, value):
        refs[2 * which + part][row, k] = value

    return write


def write_other(ref):
    def write(which, part, row, k, value):
        ref[which, part, row, k] = value

    return write


FEED_STEPS = 2


def feed_kernel(last, *refs):
    place_ref, normed_ref, grad_ref, base_ref, expand_ref, contract_ref = refs[:6]
    refs = refs[6:]
    if last:
        pulled_in_ref, residual_hbm, gain_ref, own_hbm, other_hbm = refs[:5]
        out_ref, grad_residual_ref, grad_low_ref, grad_mixed_ref, gain_grad_ref = refs[5:10]
        mine = refs[10:14]
        refs = refs[14:]
        residual_ref, weight_ref = refs[-2:]
        refs = refs[:-2]
    else:
        out_ref, pulled_out_ref, both_ref = refs[:3]
        refs = refs[3:]
    total_ref, pulled_ref, turned_ref, expand_grad_ref, contract_grad_ref, in_sems, out_sems = refs
    step = pl.program_id(0)
    wide, narrow, core = place_ref[0], place_ref[1], place_ref[2]
    width = normed_ref.shape[1]

    def base_copy():
        return pltpu.make_async_copy(base_ref, total_ref, in_sems.at[0])

    def pulled_copy():
        return pltpu.make_async_copy(pulled_in_ref, pulled_ref, in_sems.at[1])

    def residual_copy():
        return pltpu.make_async_copy(residual_hbm, residual_ref, in_sems.at[2])

    def weight_copy(hbm):
        source = hbm.at[:, pl.ds(width, width)]
        return pltpu.make_async_copy(source, weight_ref, in_sems.at[3])

    def grad_copies(j):
        rows = expand_grad_ref.shape[1] // (2 * DEEP)

        def target(which, part, row, k):
            if last:
                return mine[2 * which + part].at[row, k]
            return both_ref.at[which, part, row, k]

        copies = []

        def copy(source, place):
            sem = out_sems.at[j * 4 * DEEP + len(copies)]
            copies.append(pltpu.make_async_copy(source, place, sem))

        for dx in range(2):
            for k in range(DEEP):
                start = pl.multiple_of((wide ^ (2 * k + dx)) * rows, 16)
                copy(expand_grad_ref.at[j, pl.ds(start, rows), :], target(0, dx, narrow ^ j, k))
        for dy in range(2):
            for i in range(DEEP):
                to_wide = DEEP * j + i
                start = pl.multiple_of((to_wide * 2 + (narrow ^ dy)) * rows, 16)
                apart = wide ^ to_wide
                copy(
                    contract_grad_ref.at[pl.ds(start, rows), :],
                    target(1, dy, apart & 1, apart >> 1),
                )
        return copies

    @pl.when(step == 0)
    def _():
        base_copy().start()
        if last:
            pulled_copy().start()
            residual_copy().start()

            @pl.when(core == 0)
            def _():
                weight_copy(own_hbm).start()

            @pl.when(core == 1)
            def _():
                weight_copy(other_hbm).start()

        turned_ref[...] = normed_ref[...].T

    expand = expand_ref[0]
    contract = contract_ref[0]
    grad_block = grad_ref[...]
    pre = nn(normed_ref[...], expand)
    grad_hidden = nt(grad_block, contract)
    scale = np.float32(np.sqrt(2.0 / np.pi))
    square = pre * pre
    bent = jnp.tanh(pre * (scale + (scale * np.float32(0.044715)) * square))
    half = 0.5 + 0.5 * bent
    hidden = (pre * half).astype(BF16)
    slope = half + (0.5 * pre) * (1.0 - bent * bent) * (
        scale + (scale * np.float32(3 * 0.044715)) * square
    )
    grad_pre = (grad_hidden * slope).astype(BF16)
    made = nn(hidden, contract)
    pulled = nt(grad_pre, expand)
    block = expand.shape[1]
    contract_grad_ref[pl.ds(pl.multiple_of(step * block, block), block), :] = tn(
        hidden, grad_block
    ).astype(BF16)
    expand_grad_ref[step] = nn(turned_ref[...], grad_pre).astype(BF16)
    for j in range(FEED_STEPS):

        @pl.when(step == j)
        def _(j=j):
            for copy in grad_copies(j):
                copy.start()

    @pl.when(step == 0)
    def _():
        base_copy().wait()
        total_ref[...] += made
        if last:
            pulled_copy().wait()
            pulled_ref[...] += pulled
        else:
            pulled_ref[...] = pulled

    @pl.when(step > 0)
    def _():
        total_ref[...] += made
        pulled_ref[...] += pulled

    @pl.when(step == pl.num_programs(0) - 1)
    def _():
        if last:
            residual_copy().wait()

            @pl.when(core == 0)
            def _():
                weight_copy(own_hbm).wait()

            @pl.when(core == 1)
            def _():
                weight_copy(other_hbm).wait()

            out_ref[...] = total_ref[...].astype(BF16)
            grad_values, grad_gain = norm_backward(
                residual_ref[...], gain_ref[...], pulled_ref[...]
            )
            grad_residual = grad_block.astype(F32) + grad_values
            grad_residual_ref[...] = grad_residual
            grad_low_ref[...] = grad_residual.astype(BF16)
            gain_grad_ref[...] = grad_gain
            grad_mixed_ref[...] = nt(grad_low_ref[...], weight_ref[...]).astype(BF16)
        else:
            out_ref[...] = total_ref[...]
            pulled_out_ref[...] = pulled_ref[...]
        for j in range(FEED_STEPS):
            for copy in grad_copies(j):
                copy.wait()


def feed_half(last, place, normed, grad_block, base, weights, more=()):
    length, width = normed.shape
    half = weights.shape[1]
    block = half // FEED_STEPS
    rows = width // (2 * DEEP)

    def full(*shape):
        return pl.BlockSpec(shape, lambda j, place_ref: (0,) * len(shape))

    table = full(length, width)
    anywhere = pl.BlockSpec(memory_space=pl.ANY)
    in_specs = [
        table,
        table,
        anywhere,
        pl.BlockSpec((1, width, block), lambda j, place_ref: (0, j, 0)),
        pl.BlockSpec((1, block, width), lambda j, place_ref: (1, j, 0)),
    ]
    grad_dims = (2, DEEP, rows, block)
    if last:
        in_specs += [anywhere, anywhere, full(1, width), anywhere, anywhere]
        out_specs = [table, table, table, table, full(1, width)] + [anywhere] * 4
        out_shape = [
            shaped((length, width), BF16),
            shaped((length, width), F32),
            shaped((length, width), BF16),
            shaped((length, width), BF16),
            shaped((1, width), F32),
        ] + [shaped(grad_dims, BF16)] * 4
    else:
        out_specs = [table, table, anywhere]
        out_shape = [
            shaped((length, width), F32),
            shaped((length, width), F32),
            shaped((2, 2) + grad_dims, BF16),
        ]
    extra = []
    if last:
        extra = [pltpu.VMEM((length, width), F32), pltpu.VMEM((width, width), BF16)]
    return pl.pallas_call(
        functools.partial(feed_kernel, last),
        grid_spec=pltpu.PrefetchScalarGridSpec(
            num_scalar_prefetch=1,
            grid=(FEED_STEPS,),
            in_specs=in_specs,
            out_specs=out_specs,
            scratch_shapes=[
                pltpu.VMEM((length, width), F32),
                pltpu.VMEM((length, width), F32),
                pltpu.VMEM((width, length), BF16),
                pltpu.VMEM((FEED_STEPS, width, block), BF16),
                pltpu.VMEM((half, width), BF16),
                pltpu.SemaphoreType.DMA((4,)),
                pltpu.SemaphoreType.DMA((FEED_STEPS * 4 * DEEP,)),
            ]
            + extra,
        ),
        out_shape=out_shape,
        compiler_params=pltpu.CompilerParams(vmem_limit_bytes=56 * MIB),
        cost_estimate=cost_of(
            flops=6 * length * width * half * 2, bytes_accessed=8 * MIB, transcendentals=0
        ),
    )(place, normed, grad_block, base, weights, weights, *more)


def project_grad_kernel(place_ref, *refs):
    normed_ref, dq_ref, dk_ref, dv_ref, mixed_ref, grad_ref = refs[:6]
    mine = refs[6:10]
    other_ref, turned_ref, grads_ref = refs[10:]
    step = pl.program_id(0)
    width = dq_ref.shape[1]
    rows = width // (4 * DEEP)

    @pl.when(step == 0)
    def _():
        turned_ref[...] = normed_ref[...].T
        grads_ref[0] = nn(turned_ref[...], dq_ref[...]).astype(BF16)

    @pl.when(step == 1)
    def _():
        grads_ref[1] = nn(turned_ref[...], dk_ref[...]).astype(BF16)

    @pl.when(step == 2)
    def _():
        grads_ref[2] = nn(turned_ref[...], dv_ref[...]).astype(BF16)

    @pl.when(step == 3)
    def _():
        grads_ref[3] = tn(mixed_ref[...], grad_ref[...]).astype(BF16)

        def reader(which, core):
            def read(wide, narrow):
                start = pl.multiple_of((wide * 2 + core) * rows, 16)
                return grads_ref[2 * narrow + which, pl.ds(start, rows), :]

            return read

        core = place_ref[2]
        blocks_of(place_ref, reader(0, 1 - core), reader(1, 1 - core), write_other(other_ref))
        blocks_of(place_ref, reader(0, core), reader(1, core), write_mine(mine))


def project_grad(place, normed, dq, dk, dv, mixed, grad):
    length, width = normed.shape
    rows = width // (4 * DEEP)

    def full(*shape):
        return pl.BlockSpec(shape, lambda j, place_ref: (0,) * len(shape))

    dims = (2, DEEP, rows, width)
    return pl.pallas_call(
        project_grad_kernel,
        grid_spec=pltpu.PrefetchScalarGridSpec(
            num_scalar_prefetch=1,
            grid=(4,),
            in_specs=[full(length, width)] * 6,
            out_specs=[full(*dims)] * 4 + [full(2, 2, *dims)],
            scratch_shapes=[
                pltpu.VMEM((width, length), BF16),
                pltpu.VMEM((4, width, width), BF16),
            ],
        ),
        out_shape=[shaped(dims, BF16)] * 4 + [shaped((2, 2) + dims, BF16)],
        compiler_params=pltpu.CompilerParams(vmem_limit_bytes=56 * MIB),
        cost_estimate=cost_of(
            flops=8 * length * width * width, bytes_accessed=8 * MIB, transcendentals=0
        ),
    )(place, normed, dq, dk, dv, mixed, grad)


HALF = DEEP // 2
SOURCES = [
    (range(DEEP), 0, 0),
    (range(DEEP), 1, 0),
    (range(DEEP), 0, 1),
    (range(HALF), 1, 1),
    (range(HALF, DEEP), 1, 1),
]
EARLY, LATE = (0, 2), (1, 3)
STRAIGHT_SOURCES = [
    source for some in (EARLY, LATE) for source in [(some, 0, 0), (some, 1, 0), (some, 0, 1)]
]
FAR_SOURCES = [(EARLY, 1, 1), (LATE[:1], 1, 1), (LATE[1:], 1, 1)]


def assemble_kernel(place_ref, *refs):
    out_ref = refs[-1]
    for ref, (deep, dx, dy) in zip(refs, SOURCES):
        rows = ref.shape[1]
        for i in range(ref.shape[0]):
            start = (place_ref[0] ^ (2 * deep[i] + dx)) * 2 + (place_ref[1] ^ dy)
            out_ref[pl.ds(pl.multiple_of(start * rows, 16), rows), :] = ref[i]


def assemble(place, pieces):
    rows, columns = pieces[0].shape[1:]
    dims = (4 * DEEP * rows, columns)
    return pl.pallas_call(
        assemble_kernel,
        grid_spec=pltpu.PrefetchScalarGridSpec(
            num_scalar_prefetch=1,
            grid=(1,),
            in_specs=[
                pl.BlockSpec(piece.shape, lambda j, place_ref: (0, 0, 0)) for piece in pieces
            ],
            out_specs=pl.BlockSpec(dims, lambda j, place_ref: (0, 0)),
        ),
        out_shape=shaped(dims, BF16),
        compiler_params=pltpu.CompilerParams(vmem_limit_bytes=56 * MIB),
        cost_estimate=cost_of(flops=0, bytes_accessed=8 * MIB, transcendentals=0),
    )(place, *pieces)


def assemble_feed_kernel(sources, place_ref, *refs):
    piece_refs, out_ref, sems = refs[: len(sources)], refs[-2], refs[-1]
    copies = []

    def copy(source, base, rows, which):
        target = out_ref.at[which, pl.ds(pl.multiple_of(base, 16), rows), :]
        copies.append(pltpu.make_async_copy(source, target, sems.at[len(copies)]))

    for ref, (deep, dx, dy) in zip(piece_refs, sources):
        rows, columns = ref.shape[2:]
        half = rows // FEED_STEPS
        for i in range(ref.shape[0]):
            start = (place_ref[0] ^ (2 * deep[i] + dx)) * 2 + (place_ref[1] ^ dy)
            for j in range(FEED_STEPS):
                part = ref.at[i, 0, j * half : (j + 1) * half]
                copy(part, j * columns + start * half, half, 0)
            copy(ref.at[i, 1], start * rows, rows, 1)
    for item in copies:
        item.start()
    for item in copies:
        item.wait()


def assemble_feed(place, sources, pieces, begun=None):
    rows, columns = pieces[0].shape[2:]
    dims = (2, 4 * DEEP * rows, columns)
    count = sum(piece.shape[0] for piece in pieces) * (FEED_STEPS + 1)
    anywhere = pl.BlockSpec(memory_space=pl.ANY)
    specs = [pl.BlockSpec(piece.shape, lambda j, place_ref: (0, 0, 0, 0)) for piece in pieces]
    more, aliases = [], {}
    if begun is not None:
        more, aliases = [begun], {1 + len(pieces): 0}
    return pl.pallas_call(
        functools.partial(assemble_feed_kernel, sources),
        grid_spec=pltpu.PrefetchScalarGridSpec(
            num_scalar_prefetch=1,
            grid=(1,),
            in_specs=specs + [anywhere] * len(more),
            out_specs=anywhere,
            scratch_shapes=[pltpu.SemaphoreType.DMA((count,))],
        ),
        out_shape=shaped(dims, BF16),
        input_output_aliases=aliases,
        compiler_params=pltpu.CompilerParams(vmem_limit_bytes=56 * MIB),
        cost_estimate=cost_of(flops=4e9, bytes_accessed=8 * MIB, transcendentals=0),
    )(place, *pieces, *more)


def finish_feed_kernel(place_ref, *refs):
    parts, (expand_ref, contract_ref) = refs[:-2], refs[-2:]
    rows, columns = parts[0].shape[2:]
    unit = columns // DEEP
    for ref, dy, dc in [(parts[dc], dy, dc) for dc in range(2) for dy in range(2)]:
        y, c = place_ref[1] ^ dy, place_ref[2] ^ dc
        start = pl.multiple_of((c * 2 + y) * rows, 8)
        contract_ref[pl.ds(start, rows), :] = ref[dy, 1].astype(F32)
        for to_y in range(2):
            for to_c in range(2):

                @pl.when((y == to_y) & (c == to_c))
                def _(ref=ref, dy=dy, to_y=to_y, to_c=to_c):
                    value = ref[dy, 0].astype(F32)
                    for i in range(DEEP):
                        base = ((to_y * DEEP + i) * 2 + to_c) * unit
                        expand_ref[:, base : base + unit] = value[:, i * unit : (i + 1) * unit]


def finish_feed(place, parts):
    rows, columns = parts[0].shape[2:]
    dims = [(rows, 4 * columns), (4 * rows, columns)]
    return pl.pallas_call(
        finish_feed_kernel,
        grid_spec=pltpu.PrefetchScalarGridSpec(
            num_scalar_prefetch=1,
            grid=(1,),
            in_specs=[pl.BlockSpec(part.shape, lambda j, place_ref: (0, 0, 0, 0)) for part in parts],
            out_specs=[pl.BlockSpec(d, lambda j, place_ref: (0, 0)) for d in dims],
        ),
        out_shape=[shaped(d, F32) for d in dims],
        compiler_params=pltpu.CompilerParams(vmem_limit_bytes=56 * MIB),
        cost_estimate=cost_of(flops=0, bytes_accessed=4 * MIB, transcendentals=0),
    )(place, *parts)


def finish_square_kernel(place_ref, *refs):
    parts, outs = refs[:-4], refs[-4:]
    rows = parts[0].shape[2]
    for ref, dy, dc in [(parts[dc], dy, dc) for dc in range(2) for dy in range(2)]:
        y, c = place_ref[1] ^ dy, place_ref[2] ^ dc
        for to_y in range(2):

            @pl.when(y == to_y)
            def _(ref=ref, dy=dy, to_y=to_y, c=c):
                for i in range(2):
                    start = pl.multiple_of(c * rows, 8)
                    outs[2 * to_y + i][pl.ds(start, rows), :] = ref[dy, i].astype(F32)


def finish_square(place, parts):
    rows, columns = parts[0].shape[2:]
    dims = (2 * rows, columns)
    return pl.pallas_call(
        finish_square_kernel,
        grid_spec=pltpu.PrefetchScalarGridSpec(
            num_scalar_prefetch=1,
            grid=(1,),
            in_specs=[pl.BlockSpec(part.shape, lambda j, place_ref: (0, 0, 0, 0)) for part in parts],
            out_specs=[pl.BlockSpec(dims, lambda j, place_ref: (0, 0))] * 4,
        ),
        out_shape=[shaped(dims, F32)] * 4,
        compiler_params=pltpu.CompilerParams(vmem_limit_bytes=56 * MIB),
        cost_estimate=cost_of(flops=0, bytes_accessed=4 * MIB, transcendentals=0),
    )(place, *parts)


def tokens_back_kernel(
    place_ref,
    dq_ref,
    dk_ref,
    dv_ref,
    own_ref,
    other_ref,
    tokens_ref,
    gain_ref,
    residual_ref,
    out_ref,
    gain_grad_ref,
    pulled_ref,
):
    width = dq_ref.shape[1]

    def pull(first_ref, second_ref):
        pulled = nt(dq_ref[...], first_ref[:, 0:width])
        pulled += nt(dk_ref[...], first_ref[:, width : 2 * width])
        pulled += nt(dv_ref[...], second_ref[:, 0:width])
        pulled_ref[...] = pulled

    @pl.when(place_ref[2] == 1)
    def _():
        pull(own_ref, other_ref)

    @pl.when(place_ref[2] == 0)
    def _():
        pull(other_ref, own_ref)

    grad_values, grad_gain = norm_backward(
        tokens_ref[...].astype(F32), gain_ref[...], pulled_ref[...]
    )
    out_ref[...] = residual_ref[...] + grad_values
    gain_grad_ref[...] = grad_gain


def tokens_back(place, dq, dk, dv, own, other, tokens, gain, grad_residual):
    length, width = tokens.shape

    def full(*shape):
        return pl.BlockSpec(shape, lambda j, place_ref: (0,) * len(shape))

    table = full(length, width)
    return pl.pallas_call(
        tokens_back_kernel,
        grid_spec=pltpu.PrefetchScalarGridSpec(
            num_scalar_prefetch=1,
            grid=(1,),
            in_specs=[table, table, table]
            + [full(width, 2 * width)] * 2
            + [table, full(1, width), table],
            out_specs=[table, full(1, width)],
            scratch_shapes=[pltpu.VMEM((length, width), F32)],
        ),
        out_shape=[shaped((length, width), F32), shaped((1, width), F32)],
        compiler_params=pltpu.CompilerParams(vmem_limit_bytes=56 * MIB),
        cost_estimate=cost_of(
            flops=6 * length * width * width, bytes_accessed=8 * MIB, transcendentals=0
        ),
    )(place, dq, dk, dv, own, other, tokens, gain, grad_residual)


def exchange(value, dz=0, dx=0, dy=0, dc=0):
    flip = ((2 * dz + dx) * 2 + dy) * 2 + dc
    total = 8 * DEEP
    return lax.ppermute(value, ("wide", "narrow"), [(i, i ^ flip) for i in range(total)])


def after(value, *done):
    return lax.optimization_barrier((value,) + done)[0]


def together(*values):
    return lax.optimization_barrier(values)


def gather_stage_z(piece):
    return jnp.stack([piece] + [exchange(piece, dz=k) for k in range(1, DEEP)])


def gather_stage_xy(near):
    return exchange(near, dx=1), exchange(near, dy=1)


def gather_stage_far(over_x, over_y):
    half = over_x.shape[0] // 2
    return exchange(over_y[:half], dx=1), exchange(over_x[half:], dy=1)


def low(value):
    return value.astype(BF16)


def add(*values):
    return sum(value.astype(F32) for value in values)


def reduce_first_out(mine, other):
    return low(add(mine[1], other[0, 1])), low(add(mine[3], other[1, 1]))


def reduce_first(outs):
    return exchange(outs[0], dx=1), exchange(outs[1], dy=1)


def reduce_second_out(mine, other, first):
    return tuple(low(add(mine[2 * i][1], other[i, 0, 1], first[i][1])) for i in range(2))


def reduce_second(outs):
    return exchange(outs[0], dy=1), exchange(outs[1], dx=1)


def reduce_level(mine, other, first, second, k):
    return jnp.stack(
        [add(mine[2 * i][0, k], other[i, 0, 0, k], first[i][0, k], second[i][k]) for i in range(2)]
    )


def reduce_deep_out(*parts):
    return tuple(low(reduce_level(*parts, k)) for k in range(1, DEEP))


def reduce_deep(outs):
    return tuple(exchange(out, dz=k + 1) for k, out in enumerate(outs))


def reduce_last(parts, deep):
    return low(reduce_level(*parts, 0) + add(*deep))


def spread_y(part):
    return exchange(part, dy=1)


def spread_core(part, other_y):
    both = jnp.stack([part, other_y])
    return both, exchange(both, dc=1)


def on_device(
    tokens,
    query_weight,
    key_weight,
    value_weight,
    output_weight,
    expand_weight,
    contract_weight,
    attention_gain,
    feedforward_gain,
    bias_table,
    query_length,
    passage_length,
    pair_order,
    regrouped_grad,
):
    row_count, length, width = tokens.shape
    bucket_count, head_count = bias_table.shape
    wide_index = lax.axis_index("wide")
    wide_count = lax.axis_size("wide")
    narrow_index = lax.axis_index("narrow")
    narrow_count = lax.axis_size("narrow")
    by_hand = wide_count == 2 * DEEP and narrow_count == 4
    hidden_count = expand_weight.shape[1]
    part_rows = hidden_count // (4 * DEEP)

    square_weights = (query_weight, key_weight, value_weight, output_weight)
    if by_hand:
        narrow_y, core = narrow_index // 2, narrow_index % 2
    else:
        wide_index = narrow_y = core = jnp.int32(0)
    place = jnp.stack([wide_index, narrow_y, core]).astype(jnp.int32)

    gain_one = attention_gain[None]
    gain_two = feedforward_gain[None]
    group_rows = regrouped_grad.shape[0]
    chosen = lax.dynamic_slice_in_dim(pair_order, narrow_index * group_rows, group_rows)
    local_rows = chosen // (row_count * narrow_count) * row_count + chosen % row_count
    arranged = jnp.zeros_like(regrouped_grad).at[local_rows].set(regrouped_grad)

    spot = np.arange(2 * length)
    offsets = np.where(spot <= 2 * length - KB, length - KB - spot, 3 * length - KB - spot)
    band_hot = jnp.asarray(one_hot_rows(np.clip(offsets, 1 - length, length - 1), bucket_count))
    lines = jnp.dot(bias_table.T, band_hot.T, precision=lax.Precision.HIGHEST)
    lines = lines.reshape(head_count // 2, 2, 2 * length)
    positions = jnp.arange(length, dtype=jnp.int32)
    fill = jnp.where(positions < query_length[0] + passage_length[0], 0.0, negative)
    fill = fill.astype(F32)[:, None]

    if by_hand:
        half_rows = query_weight.shape[0] // 2
        own_half = 1 - core
        first = jnp.concatenate(square_weights[:2], axis=1)
        second = jnp.concatenate(square_weights[2:], axis=1)
        square_piece = lax.dynamic_slice_in_dim(
            jnp.where(core == 1, first, second), narrow_y * half_rows, half_rows
        )
        expand_piece = lax.dynamic_slice_in_dim(
            lax.dynamic_index_in_dim(
                expand_weight.reshape(-1, 2 * DEEP, 2, part_rows), own_half, 2, False
            ).reshape(-1, hidden_count // 2),
            narrow_y * half_rows,
            half_rows,
        )
        contract_rows = contract_weight.shape[0] // 4
        contract_piece = lax.dynamic_slice_in_dim(
            contract_weight, (own_half * 2 + narrow_y) * contract_rows, contract_rows
        )
        feed_piece = jnp.stack(
            [
                jnp.concatenate(
                    [expand_piece[:, j * width : (j + 1) * width] for j in range(FEED_STEPS)]
                ),
                contract_piece,
            ]
        )
        square_near = gather_stage_z(square_piece)
        square_near, arranged, lines, fill, feed_piece, gain_one, gain_two, local_rows = together(
            square_near, arranged, lines, fill, feed_piece, gain_one, gain_two, local_rows
        )
        square_xy = gather_stage_xy(square_near)
        feed_two = exchange(feed_piece, dz=2)
        feed_early = jnp.stack([feed_piece, feed_two])
        square_xy, feed_early, feed_piece = together(square_xy, feed_early, feed_piece)
        square_far = gather_stage_far(*square_xy)
        feed_one = exchange(feed_piece, dz=1)
        square_far, feed_one = together(square_far, feed_one)
        square_own = assemble(place, [square_near, *square_xy, *square_far])
        square_own, feed_early, feed_piece = together(square_own, feed_early, feed_piece)
        square_other = exchange(square_own, dc=1)
        feed_early_xy = gather_stage_xy(feed_early)
        feed_three = exchange(feed_piece, dz=3)
    else:

        def gathered(weight):
            return lax.all_gather(weight, "wide", axis=0, tiled=True)

        square_other = gathered(jnp.concatenate(square_weights[:2], axis=1))
        square_own = gathered(jnp.concatenate(square_weights[2:], axis=1))
        full_expand = gathered(expand_weight).reshape(width, 2 * DEEP, 2, part_rows)
        full_contract = gathered(contract_weight).reshape(2 * DEEP, 2, part_rows, width)
        feed_other, feed_own = (
            jnp.stack(
                [
                    full_expand[:, :, i]
                    .reshape(width, FEED_STEPS, -1)
                    .transpose(1, 0, 2)
                    .reshape(-1, width),
                    full_contract[:, i].reshape(-1, width),
                ]
            )
            for i in range(2)
        )

    inputs = tokens.reshape(length, width)
    attention_input, qkv = project(place, inputs, gain_one, square_own, square_other)
    if by_hand:
        arranged = after(arranged, qkv)
    grad_block = lax.all_to_all(arranged, "wide", split_axis=0, concat_axis=0, tiled=True).reshape(
        length, width
    )
    if by_hand:
        qkv, feed_early_xy, feed_three = together(qkv, feed_early_xy, feed_three)
        feed_late = jnp.stack([feed_one, feed_three])
        qkv, feed_late = together(qkv, feed_late)
        feed_late_xy = gather_stage_xy(feed_late)
        feed_early_far = [exchange(feed_early_xy[0], dy=1)]
    mixed, probs = attend(qkv, lines, fill, head_count)
    if by_hand:
        mixed, feed_late_xy = together(mixed, feed_late_xy)
        feed_late_far = gather_stage_far(*feed_late_xy)
        feed_begun = assemble_feed(
            place,
            STRAIGHT_SOURCES,
            [feed_early, *feed_early_xy, feed_late, *feed_late_xy],
        )
        mixed, feed_begun = together(mixed, feed_begun)
    residual, expand_input = residual_step(
        place, inputs, mixed, square_own, square_other, gain_two
    )
    if by_hand:
        feed_own = assemble_feed(
            place, FAR_SOURCES, [*feed_early_far, *feed_late_far], after(feed_begun, residual)
        )
        feed_other = exchange(feed_own, dc=1)
    partial_out, partial_pulled, feed_sent = feed_half(
        False, place, expand_input, grad_block, residual, feed_own
    )
    if by_hand:
        feed_got = exchange(feed_sent, dc=1)
    results = feed_half(
        True,
        place,
        expand_input,
        grad_block,
        partial_out,
        feed_other,
        (partial_pulled, residual, gain_two, square_own, square_other),
    )
    block_output, grad_residual, grad_low, grad_mixed, gain_two_grad = results[:5]
    feed_mine = results[5:9]
    if by_hand:
        feed_got, grad_mixed, block_output = together(feed_got, grad_mixed, block_output)
        outs = reduce_first_out(feed_mine, feed_got)
        grad_mixed, *outs = together(grad_mixed, *outs)
        feed_first = reduce_first(outs)
    dq, dk, dv, line_grads = attend_back(qkv, grad_mixed, probs)
    results = project_grad(place, attention_input, dq, dk, dv, mixed, grad_low)
    square_mine, square_sent = results[:4], results[4]
    if by_hand:
        square_sent, *feed_first = together(square_sent, *feed_first)
        square_got = exchange(square_sent, dc=1)
        outs = reduce_second_out(feed_mine, feed_got, feed_first)
        dq, *outs = together(dq, *outs)
        feed_second = reduce_second(outs)
    tokens_grad, gain_one_grad = tokens_back(
        place, dq, dk, dv, square_own, square_other, inputs, gain_one, grad_residual
    )
    if by_hand:
        block_output, line_grads, gain_one_grad = together(
            block_output, line_grads, gain_one_grad
        )
    received = lax.all_to_all(
        block_output.reshape(-1, regrouped_grad.shape[1], width),
        "wide",
        split_axis=0,
        concat_axis=0,
        tiled=True,
    )
    if not by_hand:
        table_grad = jnp.dot(
            jnp.asarray(line_one_hot(bucket_count).T),
            line_grads.reshape(head_count, -1).T,
            precision=lax.Precision.HIGHEST,
        )
        small = jnp.concatenate([gain_one_grad[0], gain_two_grad[0], table_grad.reshape(-1)])
        small_count = small.shape[0]
        regrouped = jnp.take(received, local_rows, axis=0)
    if by_hand:
        square_got, gain_one_grad = together(square_got, gain_one_grad)
        outs = reduce_first_out(square_mine, square_got)
        square_first = reduce_first(outs)
        feed_second = after(feed_second, *outs)
        feed_parts = (feed_mine, feed_got, feed_first, feed_second)
        outs = reduce_deep_out(*feed_parts)
        feed_deep = reduce_deep(outs)
        square_first, received = together(after(square_first, *outs), received)
        regrouped = jnp.take(received, local_rows, axis=0)
        line_grads = after(line_grads, *outs)
        table_grad = jnp.dot(
            jnp.asarray(line_one_hot(bucket_count).T),
            line_grads.reshape(head_count, -1).T,
            precision=lax.Precision.HIGHEST,
        )
        small = jnp.concatenate([gain_one_grad[0], gain_two_grad[0], table_grad.reshape(-1)])
        small_count = small.shape[0]
        small = jnp.pad(small, (0, -small_count % 1024)).reshape(-1, 128)
        small = jnp.broadcast_to(small[None], (8 * DEEP,) + small.shape)
        small = lax.all_to_all(small, ("wide", "narrow"), 0, 0, tiled=True)
        outs = reduce_second_out(square_mine, square_got, square_first)
        square_second = reduce_second(outs)
        feed_deep = after(feed_deep, *outs)
        square_parts = (square_mine, square_got, square_first, square_second)
        feed_deep, regrouped = together(feed_deep, regrouped)
        feed_part = reduce_last(feed_parts, feed_deep)
        feed_other_y = spread_y(feed_part)
        outs = reduce_deep_out(*square_parts)
        feed_other_y, outs, small = together(feed_other_y, outs, small)
        square_deep = reduce_deep(outs)
        feed_spread = spread_core(feed_part, feed_other_y)
        final_expand, final_contract = finish_feed(place, feed_spread)
        square_deep, small = together(after(square_deep, final_expand), small)
        square_part = reduce_last(square_parts, square_deep)
        finals = finish_square(place, spread_core(square_part, spread_y(square_part)))
        small = jnp.sum(small, axis=0).reshape(-1)
    else:

        def summed(grad):
            part = lax.psum_scatter(grad, "wide", scatter_dimension=0, tiled=True)
            return lax.psum(part, "narrow").astype(F32)

        def stacked(which, mine, other):
            kept = jnp.stack(mine[2 * which : 2 * which + 2])
            return jnp.stack([kept, other[which]])

        expand_all = stacked(0, feed_mine, feed_sent)
        expand_all = expand_all.reshape(expand_all.shape[:5] + (DEEP, part_rows))
        expand_all = expand_all.transpose(3, 1, 4, 2, 5, 0, 6)
        contract_all = stacked(1, feed_mine, feed_sent).transpose(3, 2, 0, 1, 4, 5)
        first = stacked(0, square_mine, square_sent)
        second = stacked(1, square_mine, square_sent).transpose(0, 2, 1, 3, 4, 5)
        square_all = jnp.stack([first, second]).transpose(4, 2, 1, 5, 3, 0, 6)
        final_contract = summed(contract_all.reshape(hidden_count, width))
        final_expand = summed(expand_all.reshape(width, hidden_count))
        final_square = summed(square_all.reshape(width, 4 * width))
        finals = [final_square[:, i * width : (i + 1) * width] for i in range(4)]
        small = lax.psum(small, ("wide", "narrow"))

    return (
        regrouped,
        tokens_grad.reshape(row_count, length, width),
        *finals,
        final_expand,
        final_contract,
        small[:width],
        small[width : 2 * width],
        small[2 * width : small_count].reshape(bucket_count, head_count),
    )


def solution(mesh):
    in_specs = (
        P(("wide", "narrow"), None, None),
        P("wide", None),
        P("wide", None),
        P("wide", None),
        P("wide", None),
        P("wide", None),
        P("wide", None),
        P(),
        P(),
        P(),
        P(("wide", "narrow")),
        P(("wide", "narrow")),
        P(),
        P("narrow", "wide", None),
    )
    out_specs = (
        P("narrow", "wide", None),
        P(("wide", "narrow"), None, None),
        P("wide", None),
        P("wide", None),
        P("wide", None),
        P("wide", None),
        P("wide", None),
        P("wide", None),
        P(),
        P(),
        P(),
    )
    return jax.shard_map(
        on_device, mesh=mesh, in_specs=in_specs, out_specs=out_specs, check_vma=False
    )
```
